256 devices in a mesh: gx: 8 (over x, core), gy: 32 (over y, z).
Axes of the slice: x: 4, y: 4, z: 8, core: 2. Of those that a mesh axis runs over, the one named last changes fastest.
Arguments:
- rock_rhs: float32 [256, 512, 128], P('gx', 'gy'), may hold values from -6 to 6
- frac_rhs: float32 [8192, 4096], P(('gx', 'gy')), may hold values from -6 to 6
- perm: float32 [256, 512, 128], P('gx', 'gy'), may hold values from 0.1 to 10
- storage: float32 [256, 512, 128], P('gx', 'gy'), may hold values from 0.002 to 0.05
- pressure: float32 [256, 512, 128], P('gx', 'gy'), may hold values from -4 to 4
- frac_perm: float32 [8192, 4096], P(('gx', 'gy')), may hold values from 0.5 to 20
- frac_storage: float32 [8192, 4096], P(('gx', 'gy')), may hold values from 0.002 to 0.05
- frac_pressure: float32 [8192, 4096], P(('gx', 'gy')), may hold values from -4 to 4
- couple_geom: float32 [8192, 128], P(('gx', 'gy')), may hold values from 0.1 to 2
- couple_count: int32 [8192], P(('gx', 'gy')), may hold values from 1 to 128, as said below
- couple_frac_cell: int32 [8192, 128], P(('gx', 'gy')), may hold values from 0 to 4095
- couple_rock_cell: int32 [8192, 128], P(('gx', 'gy')), may hold values from 0 to 65535
- host_offset: int32 [8192], P(('gx', 'gy')), may hold values from -1 to 1, as said below
- cross_pairs: int32 [2, 65536], P(None, ('gx', 'gy')), may hold values from 0 to 131071, as said below
- cross_geom: float32 [65536], P(('gx', 'gy')), may hold values from 0.1 to 2
- aggregates: int32 [256, 512, 128], P('gx', 'gy'), may hold values from 0 to 63, as said below
Outputs:
- rock_update: float32 [256, 512, 128], P('gx', 'gy')
- frac_update: float32 [8192, 4096], P(('gx', 'gy'))
- residual_norm: float32 [], replicated
The draws below stay inside these ranges and needn't reach their ends.
Inputs may be any that keep to these rules, and one draw needn't show every extreme that they name: `couple_count`: every fracture has at least one live slot, and in every draw some fracture fills all 128. `host_offset`: the host block always exists: owners at the first gy index never have -1, owners at the last never +1. `cross_pairs`: cells are numbered within the owner device's 32 fractures, 4096 each; the two ends of a pair lie in different fractures. `aggregates`: each aggregate is a face-connected set of cells inside one device's block; every one of the 64 numbers is used in every block, with counts that differ from block to block.
All inputs are finite; a program needn't handle non-finite values.
Results may differ from the reference program's by a relative error of at most 0.0003.
Values sent between devices are 32-bit elements; how exact they have to be, the bound alone decides.
A program may use at most 128 MiB of HBM per device.

```python
import math
import jax
import jax.numpy as jnp
from jax import lax

CX = 32
CY = 16
NZ = 128
FR_DEV = 32
IX_DEV = 256
FSIDE = 64
KC = 128
NAGG = 64
ITERS = 2
NX = 256
NY = 512
FRACS = 8192
IXS = 65536
N_GX = 8
N_GY = 32


def draw_couple_count(key, part):
    counts = jax.random.randint(jax.random.fold_in(key, 11), (FRACS,), 1, KC + 1)
    full_at = jax.random.randint(jax.random.fold_in(key, 12), (), 0, FRACS)
    hop_at = jax.random.randint(jax.random.fold_in(key, 13), (), 1, FRACS)
    counts = counts.at[full_at].set(KC)
    counts = counts.at[(full_at + hop_at) % FRACS].set(1)
    return counts.astype(jnp.int32)


def draw_host_offset(key, part):
    offsets = jax.random.randint(jax.random.fold_in(key, 21), (FRACS,), -1, 2)
    lanes = NY // CY
    owner_y = jnp.arange(FRACS, dtype=jnp.int32) // FR_DEV % lanes
    offsets = jnp.where(owner_y == 0, jnp.maximum(offsets, 0), offsets)
    offsets = jnp.where(owner_y == lanes - 1, jnp.minimum(offsets, 0), offsets)
    return offsets.astype(jnp.int32)


def draw_cross_pairs(key, part):
    span = FR_DEV * FSIDE * FSIDE
    former = jax.random.randint(jax.random.fold_in(key, 31), (IXS,), 0, span)
    jumps = jax.random.randint(jax.random.fold_in(key, 32), (IXS,), 1, FR_DEV)
    latter = (former + jumps * FSIDE * FSIDE) % span
    return jnp.stack([former, latter]).astype(jnp.int32)


def draw_aggregates(key, part):
    blocks_x = NX // CX
    blocks_y = NY // CY
    total = CX * CY * NZ
    stride = total // NAGG
    jitter = stride // 4
    cell_x = lax.broadcasted_iota(jnp.int32, (CX, CY, NZ), 0)
    cell_y = lax.broadcasted_iota(jnp.int32, (CX, CY, NZ), 1)
    cell_z = lax.broadcasted_iota(jnp.int32, (CX, CY, NZ), 2)
    turned_y = jnp.where(cell_x % 2 == 0, cell_y, CY - 1 - cell_y)
    lane = cell_x * CY + turned_y
    turned_z = jnp.where(lane % 2 == 0, cell_z, NZ - 1 - cell_z)
    position = (lane * NZ + turned_z).reshape(-1)
    shifts = jax.random.randint(jax.random.fold_in(key, 41), (blocks_x * blocks_y, NAGG - 1), -jitter, jitter + 1)
    cuts = (jnp.arange(1, NAGG, dtype=jnp.int32) * stride)[None, :] + shifts
    labels = jax.vmap(lambda row: jnp.searchsorted(row, position, side='right'))(cuts)
    labels = labels.reshape(blocks_x, blocks_y, CX, CY, NZ).transpose(0, 2, 1, 3, 4)
    return labels.reshape(NX, NY, NZ).astype(jnp.int32)


def place_ends(values, own_key, least, top_value):
    longest = values.shape.index(max(values.shape))
    spots = []
    for shift in (0, 1):
        where = [jax.random.randint(jax.random.fold_in(own_key, axis), (), 0, length) for axis, length in enumerate(values.shape)]
        where[longest] = (where[longest] + shift) % values.shape[longest]
        spots.append(tuple(where))
    return values.at[spots[0]].set(least).at[spots[1]].set(top_value)


def level_of(stream_key, dims, split, smallest, largest):
    def one(dim, shards_of):
        draws = jax.random.uniform(jax.random.fold_in(jax.random.fold_in(stream_key, 6), dim), (shards_of,), jnp.float32, smallest / len(split), largest / len(split))
        return jnp.repeat(jnp.exp(draws), dims[dim] // shards_of).reshape((-1,) + (1,) * (len(dims) - dim - 1))

    level = one(*split[0])
    for cut in split[1:]:
        level = level * one(*cut)
    return level


def scatter_about(rng, extent, deviation, limit, shards=(), kind=jnp.bfloat16):
    drawn = deviation * jax.random.normal(rng, extent, jnp.float32)
    if shards:
        drawn = drawn * level_of(rng, extent, shards, -0.22, 0.18)
    return jnp.clip(drawn, -limit, limit).astype(kind)


def setup_inputs(seed: int = 0) -> dict:
    streams_of = jax.random.split(jax.random.key(seed), 17)
    rock_rhs = scatter_about(streams_of[0], (NX, NY, NZ), 1.0, 6.0, ((0, 8), (1, 32)), jnp.float32)
    frac_rhs = scatter_about(streams_of[1], (FRACS, FSIDE * FSIDE), 1.0, 6.0, ((0, 256),), jnp.float32)
    perm = jnp.clip(jnp.exp(math.log(10.0) - 4.6051702 * jax.random.uniform(streams_of[2], (NX, NY, NZ), jnp.float32) ** level_of(streams_of[2], (NX, NY, NZ), ((0, 8), (1, 32)), -0.2, 0.2)), 0.1, 10.0)
    storage = jnp.clip(jnp.exp(math.log(0.05) - 3.218876 * jax.random.uniform(streams_of[3], (NX, NY, NZ), jnp.float32) ** level_of(streams_of[3], (NX, NY, NZ), ((0, 8), (1, 32)), -0.2, 0.2)), 0.002, 0.05)
    pressure = scatter_about(streams_of[4], (NX, NY, NZ), 1.0, 4.0, ((0, 8), (1, 32)), jnp.float32)
    frac_perm = jnp.clip(jnp.exp(math.log(20.0) - 3.6888795 * jax.random.uniform(streams_of[5], (FRACS, FSIDE * FSIDE), jnp.float32) ** level_of(streams_of[5], (FRACS, FSIDE * FSIDE), ((0, 256),), -0.2, 0.2)), 0.5, 20.0)
    frac_storage = jnp.clip(jnp.exp(math.log(0.05) - 3.218876 * jax.random.uniform(streams_of[6], (FRACS, FSIDE * FSIDE), jnp.float32) ** level_of(streams_of[6], (FRACS, FSIDE * FSIDE), ((0, 256),), -0.2, 0.2)), 0.002, 0.05)
    frac_pressure = scatter_about(streams_of[7], (FRACS, FSIDE * FSIDE), 1.0, 4.0, ((0, 256),), jnp.float32)
    couple_geom = jnp.clip(jnp.exp(math.log(2.0) - 2.9957323 * jax.random.uniform(streams_of[8], (FRACS, KC), jnp.float32) ** level_of(streams_of[8], (FRACS, KC), ((0, 256),), -0.2, 0.2)), 0.1, 2.0)
    couple_count = draw_couple_count(jax.random.fold_in(streams_of[16], 71), 0)
    couple_frac_cell = place_ends(jax.random.randint(streams_of[10], (FRACS, KC), 0, FSIDE * FSIDE), jax.random.fold_in(streams_of[10], 1), 0, (FSIDE * FSIDE) - 1).astype(jnp.int32)
    couple_rock_cell = place_ends(jax.random.randint(streams_of[11], (FRACS, KC), 0, CX * CY * NZ), jax.random.fold_in(streams_of[11], 1), 0, (CX * CY * NZ) - 1).astype(jnp.int32)
    host_offset = draw_host_offset(jax.random.fold_in(streams_of[16], 71), 0)
    cross_pairs = draw_cross_pairs(jax.random.fold_in(streams_of[16], 71), 0)
    cross_geom = jnp.clip(jnp.exp(math.log(2.0) - 2.9957323 * jax.random.uniform(streams_of[14], (IXS,), jnp.float32) ** level_of(streams_of[14], (IXS,), ((0, 256),), -0.2, 0.2)), 0.1, 2.0)
    aggregates = draw_aggregates(jax.random.fold_in(streams_of[16], 71), 0)
    return dict(rock_rhs=rock_rhs, frac_rhs=frac_rhs, perm=perm, storage=storage, pressure=pressure, frac_perm=frac_perm, frac_storage=frac_storage, frac_pressure=frac_pressure, couple_geom=couple_geom, couple_count=couple_count, couple_frac_cell=couple_frac_cell, couple_rock_cell=couple_rock_cell, host_offset=host_offset, cross_pairs=cross_pairs, cross_geom=cross_geom, aggregates=aggregates)


mobility_rate = 0.5
relaxation = 0.8
epsilon = 1e-06

def harmonic(former, latter):
    return 2.0 * former * latter / (former + latter)

def mobility(former, latter):
    return jnp.exp(-mobility_rate * 0.5 * (former + latter))

def neighbours(padded):
    return [padded[2:, 1:-1, 1:-1], padded[:-2, 1:-1, 1:-1], padded[1:-1, 2:, 1:-1], padded[1:-1, :-2, 1:-1], padded[1:-1, 1:-1, 2:], padded[1:-1, 1:-1, :-2]]

def fracture_faces(conduct, frac_press):
    column = lax.broadcasted_iota(jnp.int32, conduct.shape, 1)
    along = column % FSIDE
    across = column // FSIDE
    t_along = jnp.where(along < FSIDE - 1, harmonic(conduct, jnp.roll(conduct, -1, 1)) * mobility(frac_press, jnp.roll(frac_press, -1, 1)), 0.0)
    t_across = jnp.where(across < FSIDE - 1, harmonic(conduct, jnp.roll(conduct, -FSIDE, 1)) * mobility(frac_press, jnp.roll(frac_press, -FSIDE, 1)), 0.0)
    return [t_along, jnp.roll(t_along, 1, 1), t_across, jnp.roll(t_across, FSIDE, 1)]

def fracture_stencil(face_list, frac_diag, vector):
    result = frac_diag * vector
    for weight, stride in zip(face_list, (-1, 1, -FSIDE, FSIDE)):
        result = result - weight * jnp.roll(vector, stride, 1)
    return result

def givens_solve(columns, start_norm):
    small_rhs = [start_norm] + [jnp.zeros((), jnp.float32) for column in range(len(columns))]
    rotations = []
    upper = []
    for column, entries in enumerate(columns):
        entries = list(entries)
        for earlier, (cosine, sine) in enumerate(rotations):
            former, latter = (entries[earlier], entries[earlier + 1])
            entries[earlier] = cosine * former + sine * latter
            entries[earlier + 1] = -sine * former + cosine * latter
        radius = jnp.sqrt(entries[column] * entries[column] + entries[column + 1] * entries[column + 1])
        cosine = entries[column] / radius
        sine = entries[column + 1] / radius
        entries[column] = radius
        rotations.append((cosine, sine))
        small_rhs[column + 1] = -sine * small_rhs[column]
        small_rhs[column] = cosine * small_rhs[column]
        upper.append(entries[:column + 1])
    count = len(columns)
    coeffs = [None] * count
    for column in range(count - 1, -1, -1):
        total = small_rhs[column]
        for later in range(column + 1, count):
            total = total - upper[later][column] * coeffs[later]
        coeffs[column] = total / upper[column][column]
    return (coeffs, jnp.abs(small_rhs[count]))

def reference(rock_rhs, frac_rhs, perm, storage, pressure, frac_perm, frac_storage, frac_pressure, couple_geom, couple_count, couple_frac_cell, couple_rock_cell, host_offset, cross_pairs, cross_geom, aggregates):
    fcells = FSIDE * FSIDE
    cell_count = NX * NY * NZ
    devices = N_GX * N_GY
    weights = [harmonic(perm, near_perm) * mobility(pressure, near_press) for near_perm, near_press in zip(neighbours(jnp.pad(perm, 1)), neighbours(jnp.pad(pressure, 1)))]
    face_list = fracture_faces(frac_perm, frac_pressure)
    slot_ids = lax.broadcasted_iota(jnp.int32, (FRACS, KC), 1)
    row_ids = lax.broadcasted_iota(jnp.int32, (FRACS, KC), 0)
    live_mask = slot_ids < couple_count[:, None]
    frac_value = jnp.take_along_axis(frac_pressure, couple_frac_cell, axis=1)
    coupling = jnp.where(live_mask, couple_geom * jnp.exp(-mobility_rate * frac_value), 0.0)
    owner = jnp.arange(FRACS, dtype=jnp.int32) // FR_DEV
    owner_x = owner // N_GY
    host_y = owner % N_GY + host_offset
    local_x = couple_rock_cell // (CY * NZ)
    local_y = couple_rock_cell // NZ % CY
    local_z = couple_rock_cell % NZ
    global_cell = ((owner_x[:, None] * CX + local_x) * NY + host_y[:, None] * CY + local_y) * NZ + local_z
    base = jnp.arange(IXS, dtype=jnp.int32) // IX_DEV * (FR_DEV * fcells)
    former_cell = cross_pairs[0] + base
    latter_cell = cross_pairs[1] + base
    press_flat = frac_pressure.reshape(-1)
    cross_coef = cross_geom * mobility(press_flat[former_cell], press_flat[latter_cell])
    cross_sum = jnp.zeros((FRACS * fcells,), jnp.float32).at[former_cell].add(cross_coef).at[latter_cell].add(cross_coef)
    couple_frac_sum = jnp.zeros((FRACS, fcells), jnp.float32).at[row_ids, couple_frac_cell].add(coupling)
    frac_diag = frac_storage + sum(face_list) + couple_frac_sum + cross_sum.reshape(FRACS, fcells)
    couple_rock_sum = jnp.zeros((cell_count,), jnp.float32).at[global_cell].add(coupling).reshape(NX, NY, NZ)
    rock_diag = storage + sum(weights) + couple_rock_sum

    def rock_part(rock_vec, frac_vec):
        result = rock_diag * rock_vec
        for weight, near in zip(weights, neighbours(jnp.pad(rock_vec, 1))):
            result = result - weight * near
        flux = coupling * jnp.take_along_axis(frac_vec, couple_frac_cell, axis=1)
        return result - jnp.zeros((cell_count,), jnp.float32).at[global_cell].add(flux).reshape(NX, NY, NZ)

    def frac_part(rock_vec, frac_vec):
        result = fracture_stencil(face_list, frac_diag, frac_vec)
        host_value = rock_vec.reshape(-1)[global_cell]
        result = result - jnp.zeros((FRACS, fcells), jnp.float32).at[row_ids, couple_frac_cell].add(coupling * host_value)
        flat = frac_vec.reshape(-1)
        crossing = jnp.zeros((FRACS * fcells,), jnp.float32).at[former_cell].add(cross_coef * flat[latter_cell]).at[latter_cell].add(cross_coef * flat[former_cell])
        return result - crossing.reshape(FRACS, fcells)
    grid_x = lax.broadcasted_iota(jnp.int32, (NX, NY, NZ), 0)
    grid_y = lax.broadcasted_iota(jnp.int32, (NX, NY, NZ), 1)
    global_agg = (grid_x // CX * N_GY + grid_y // CY) * NAGG + aggregates
    coarse_cell = rock_diag
    for weight, near in zip(weights, neighbours(jnp.pad(global_agg, 1, constant_values=-1))):
        coarse_cell = coarse_cell - jnp.where(near == global_agg, weight, 0.0)
    segments = NAGG * devices
    agg_flat = global_agg.reshape(-1)
    coarse_diag = jax.ops.segment_sum(coarse_cell.reshape(-1), agg_flat, num_segments=segments)

    def precond(rock_vec, frac_vec):
        smooth_rock = relaxation * rock_vec / rock_diag
        smooth_frac = relaxation * frac_vec / frac_diag
        leftover = rock_vec - rock_part(smooth_rock, smooth_frac)
        coarse_rhs = jax.ops.segment_sum(leftover.reshape(-1), agg_flat, num_segments=segments)
        coarse_sol = coarse_rhs / coarse_diag
        return (smooth_rock + coarse_sol[global_agg], smooth_frac)

    def inner(former, latter):
        return jnp.sum(former[0] * latter[0]) + jnp.sum(former[1] * latter[1])
    rhs_pair = (rock_rhs, frac_rhs)
    start_norm = jnp.sqrt(inner(rhs_pair, rhs_pair) + epsilon)
    krylov = [(rock_rhs / start_norm, frac_rhs / start_norm)]
    directions = []
    columns = []
    for column in range(ITERS):
        direction = precond(*krylov[-1])
        directions.append(direction)
        image = (rock_part(*direction), frac_part(*direction))
        projections = [inner(image, vector) for vector in krylov]
        for coeff, vector in zip(projections, krylov):
            image = (image[0] - coeff * vector[0], image[1] - coeff * vector[1])
        next_norm = jnp.sqrt(inner(image, image) + epsilon)
        krylov.append((image[0] / next_norm, image[1] / next_norm))
        columns.append(projections + [next_norm])
    coeffs, residual_norm = givens_solve(columns, start_norm)
    rock_update = sum((coeff * direction[0] for coeff, direction in zip(coeffs, directions)))
    frac_update = sum((coeff * direction[1] for coeff, direction in zip(coeffs, directions)))
    return (rock_update, frac_update, residual_norm)
```

```python
import functools

import jax
import jax.numpy as jnp
from jax import lax
from jax.experimental import pallas as pl
from jax.experimental.pallas import tpu as pltpu
from jax.sharding import PartitionSpec as P

CX, CY, NZ = 32, 16, 128
FR, FCELLS, FSIDE, KC = 32, 4096, 64, 128
SLABS = FCELLS // 128
NAGG = 64
ROWS = CX * CY
CROSS = 256
relaxation = 0.8
epsilon = 1e-06
MESH = pl.DeviceIdType.MESH
f32 = jnp.float32
bf16 = jnp.bfloat16


def iota(shape, dim):
    return lax.broadcasted_iota(jnp.int32, shape, dim)


def loop(count, body, unroll=1):
    lax.fori_loop(0, count, lambda i, c: (body(i), c)[1], 0, unroll=unroll)


def halves(x):
    high = x.astype(bf16)
    return high, (x - high.astype(f32)).astype(bf16)


def nt_dot(a, b):
    return lax.dot_general(a, b, (((1,), (1,)), ((), ())), preferred_element_type=f32)


def lanes_of(table, index):
    return jnp.take_along_axis(table, index, axis=1)


def kernel(
    sizes,
    rock_rhs, frac_rhs, perm, storage, pressure, frac_perm, frac_storage, frac_pressure,
    geom, count, frac_cell, rock_cell, offset, pairs, cross_geom, agg,
    rock_out, frac_out, res_out,
    Z0, E, PA, PE, WX, WYM, WYP, WZM, WZP, RD, INVR, W1R, Q, S, DEL, SEG,
    FD, INVF, TAP, TAM, TCP, TCM, W1F, ZF, F2, S2,
    U, LV, BF, XU, LVX, XV, IDX, OFF, CPL, PICK, HV, AGS, VALS,
    sx, rx, sy, ry, sic, ric, sag, rag, szy, rzy, sfl, rfl, sans, rans, scs, rcs,
    AR0, AR1, AR2, send_sem, recv_sem,
):
    n_gx, n_y, n_z = sizes
    n_gy = n_y * n_z
    gx = lax.axis_index("gx")
    gy = lax.axis_index("gy")
    my_y, my_z = gy // n_z, gy % n_z
    x_dev = [((gx + 1) % n_gx, gy), ((gx + n_gx - 1) % n_gx, gy)]
    y_dev = [(gx, (gy + 1) % n_gy), (gx, (gy + n_gy - 1) % n_gy)]
    gx_peers = [((gx + p) % n_gx, gy) for p in range(1, n_gx)]
    y_peers = [(gx, (my_y + p) % n_y * n_z + my_z) for p in range(1, n_y)]
    z_peers = [(gx, my_y * n_z + (my_z + p) % n_z) for p in range(1, n_z)]

    barrier = pltpu.get_barrier_semaphore()
    everyone = gx_peers + y_peers + z_peers + y_dev
    for device in everyone:
        pl.semaphore_signal(barrier, inc=1, device_id=device, device_id_type=MESH)

    started = []

    def send(src, dst, device):
        number = len(started)
        copy = pltpu.make_async_remote_copy(
            src_ref=src, dst_ref=dst, send_sem=send_sem.at[number],
            recv_sem=recv_sem.at[number], device_id=device, device_id_type=MESH,
        )
        copy.start()
        started.append(copy)
        return copy

    sub8 = iota((8, 128), 0)
    sub16 = iota((16, 128), 0)
    sub32 = iota((32, 128), 0)
    sub128 = iota((128, 128), 0)
    lane16 = iota((16, 128), 1)
    lane32 = iota((32, 128), 1)
    row_lane = iota((1, 128), 1)

    def to_table(get):
        def body(r):
            F2[pl.ds(r, FR, stride=SLABS), :] = get(r)
        loop(SLABS, body, 2)

    def slab(r):
        return pl.ds(pl.multiple_of(r * 128, 128), 128)

    def pick_slots(out):
        def body(f):
            cell = frac_cell[pl.ds(f, 1), :]
            table = F2[pl.ds(pl.multiple_of(f * SLABS, SLABS), SLABS), :]
            got = lanes_of(table, jnp.broadcast_to(cell & 127, (SLABS, 128)))
            out[pl.ds(f, 1), :] = jnp.sum(
                jnp.where(sub32 == cell >> 7, got, 0.0), axis=0, keepdims=True)
        loop(FR, body, 4)

    ends = [(e, h) for e in (0, 1) for h in (0, 1)]

    def end_cells(e, h):
        return pairs[e : e + 1, h * 128 : (h + 1) * 128]

    def pick_ends():
        low = [jnp.broadcast_to(end_cells(e, h) & 127, (8, 128)) for e, h in ends]
        high = [(end_cells(e, h) >> 7) - sub8 for e, h in ends]

        def body(i, accs):
            for j in range(4):
                row = pl.multiple_of(i * 32 + j * 8, 8)
                table = F2[pl.ds(row, 8), :]
                accs = tuple(
                    jnp.where(high[n] == row, lanes_of(table, low[n]), accs[n])
                    for n in range(4)
                )
            return accs
        accs = lax.fori_loop(0, FR * SLABS // 32, body, (jnp.zeros((8, 128), f32),) * 4)
        return [jnp.sum(a, axis=0, keepdims=True) for a in accs]

    def spread_frac(slot_vals, end_vals):
        for n, (e, h) in enumerate(ends):
            hot = sub128 == (end_cells(e, h) & 127)
            high, low = halves(end_vals[n])
            LVX[0:128, n * 128 : (n + 1) * 128] = jnp.where(hot, high.astype(f32), 0.0).astype(bf16)
            LVX[128:256, n * 128 : (n + 1) * 128] = jnp.where(hot, low.astype(f32), 0.0).astype(bf16)
        for m in range(4):
            part = nt_dot(XU[m * 256 : (m + 1) * 256, :], LVX[...])
            S2[m * 256 : (m + 1) * 256, :] = part[:, :128] + part[:, 128:]

        def body(f):
            cell = frac_cell[pl.ds(f, 1), :]
            high, low = halves(jnp.where(sub32 == cell >> 7, slot_vals[pl.ds(f, 1), :], 0.0))
            part = nt_dot(jnp.concatenate([high, low], axis=0), BF[f])
            rows = pl.ds(pl.multiple_of(f * SLABS, SLABS), SLABS)
            S2[rows, :] = S2[rows, :] + part[:32] + part[32:]
        loop(FR, body, 2)

    def build_hot(src):
        def body(f):
            high = IDX[src, pl.ds(f, 1), :] >> 7
            for m in range(4):
                hot = (sub128 + m * 128 == high).astype(f32).astype(bf16)
                U[src, m * 128 : (m + 1) * 128, slab(f)] = hot
        loop(FR, body)

    def spread_rock(src, vals, first):
        def body(f):
            hot = sub128 == (IDX[src, pl.ds(f, 1), :] & 127)
            high, low = halves(vals[pl.ds(f, 1), :])
            LV[0:128, slab(f)] = jnp.where(hot, high.astype(f32), 0.0).astype(bf16)
            LV[128:256, slab(f)] = jnp.where(hot, low.astype(f32), 0.0).astype(bf16)
        loop(FR, body, 2)
        for m in range(2):
            part = nt_dot(U[src, m * 256 : (m + 1) * 256, :], LV[...])
            total = part[:, :128] + part[:, 128:]
            rows = pl.ds(m * 256, 256)
            DEL[rows, :] = total if first else DEL[rows, :] + total

    def pick_rock(get, outs):
        def body(f):
            cells = [IDX[src, pl.ds(f, 1), :] for src in range(3)]
            low = [jnp.broadcast_to(c & 127, (8, 128)) for c in cells]
            high = [(c >> 7) - sub8 for c in cells]
            accs = [jnp.zeros((8, 128), f32)] * 3
            for i in range(CX):
                for j in range(2):
                    table = get(i, j)
                    row = i * 16 + j * 8
                    accs = [
                        jnp.where(high[n] == row, lanes_of(table, low[n]), accs[n])
                        for n in range(3)
                    ]
            for n in range(3):
                outs[n][pl.ds(f, 1), :] = jnp.sum(accs[n], axis=0, keepdims=True)
        loop(FR, body)

    def aggregate_sums(src):
        for chunk in range(4):
            def body(i, accs):
                for j in (0, 8):
                    value, number = src[i, j : j + 8, :], agg[i, j : j + 8, :]
                    accs = tuple(
                        acc + jnp.where(number == chunk * 16 + a, value, 0.0)
                        for a, acc in enumerate(accs)
                    )
                return accs
            accs = lax.fori_loop(0, CX, body, (jnp.zeros((8, 128), f32),) * 16)
            for a, acc in enumerate(accs):
                SEG[chunk * 16 + a : chunk * 16 + a + 1, :] = jnp.sum(acc, axis=0, keepdims=True)
        ones = jnp.ones((16, 128), bf16)
        rest = SEG[...]
        total = jnp.zeros((16, 128), f32)
        for _ in range(3):
            high = rest.astype(bf16)
            rest = rest - high.astype(f32)
            total = total + nt_dot(ones, high)
        return total

    SEG[NAGG:128, :] = jnp.zeros((128 - NAGG, 128), f32)

    to_table(lambda r: frac_pressure[:, slab(r)])
    pick_slots(PICK)

    def split_slots(f):
        where = offset[f]
        row = pl.ds(f, 1)
        OFF[row, :] = jnp.full((1, 128), where, jnp.int32)
        cell = rock_cell[row, :]
        live = row_lane < count[f]
        IDX[0, row, :] = jnp.where(live & (where == 0), cell, -1)
        sic[0, 0, row, :] = jnp.where(live & (where == 1), cell, -1).astype(f32)
        sic[1, 0, row, :] = jnp.where(live & (where == -1), cell, -1).astype(f32)
        value = jnp.where(live, geom[row, :] * jnp.exp(-0.5 * PICK[row, :]), 0.0)
        CPL[row, :] = value
    loop(FR, split_slots, 2)
    sic[0, 1] = CPL[...]
    sic[1, 1] = CPL[...]

    for d, plane in enumerate((CX - 1, 0)):
        sx[d, 0] = perm[plane]
        sx[d, 1] = pressure[plane]
        sx[d, 2] = agg[plane].astype(f32)
    for d, row in enumerate((CY - 1, 0)):
        sy[d, 0] = perm[:, row, :]
        sy[d, 1] = pressure[:, row, :]
        sy[d, 2] = agg[:, row, :].astype(f32)

    pl.semaphore_wait(barrier, len(everyone))
    slots_sent = [send(sic.at[d], ric.at[d], y_dev[d]) for d in (0, 1)]
    faces_sent = [send(sx.at[d], rx.at[d], x_dev[d]) for d in (0, 1)]
    faces_sent += [send(sy.at[d], ry.at[d], y_dev[d]) for d in (0, 1)]

    def face_along(r):
        conduct, press = frac_perm[:, slab(r)], frac_pressure[:, slab(r)]
        scaled = conduct * jnp.exp(-0.25 * press)
        F2[pl.ds(r, FR, stride=SLABS), :] = press
        near, near_scaled = pltpu.roll(conduct, 127, 1), pltpu.roll(scaled, 127, 1)
        weight = 2.0 * scaled * near_scaled / (conduct + near)
        weight = jnp.where(lane32 % FSIDE < FSIDE - 1, weight, 0.0)
        TAP[:, slab(r)] = weight
        TAM[:, slab(r)] = pltpu.roll(weight, 1, 1)
        after = slab(jnp.minimum(r + 1, SLABS - 1))
        next_conduct = frac_perm[:, after]
        next_scaled = next_conduct * jnp.exp(-0.25 * frac_pressure[:, after])
        first = lane32 < FSIDE
        near = pltpu.roll(jnp.where(first, next_conduct, conduct), FSIDE, 1)
        near_scaled = pltpu.roll(jnp.where(first, next_scaled, scaled), FSIDE, 1)
        weight = 2.0 * scaled * near_scaled / (conduct + near)
        TCP[:, slab(r)] = jnp.where(first | (r < SLABS - 1), weight, 0.0)
    loop(SLABS, face_along)

    pressures = pick_ends()
    for n, (e, h) in enumerate(ends):
        for m in range(8):
            hot = (sub128 + m * 128 == end_cells(e, h) >> 7).astype(f32).astype(bf16)
            XU[m * 128 : (m + 1) * 128, n * 128 : (n + 1) * 128] = hot
    for h in (0, 1):
        XV[h : h + 1, :] = cross_geom[0:1, h * 128 : (h + 1) * 128] * jnp.exp(
            -0.25 * (pressures[h] + pressures[h + 2]))

    def build_lanes(f):
        BF[f] = (sub128 == (frac_cell[pl.ds(f, 1), :] & 127)).astype(f32).astype(bf16)
    loop(FR, build_lanes)
    coefs = [XV[h : h + 1, :] for h in (0, 1)]
    spread_frac(CPL, coefs + coefs)

    def face_back(r):
        before = slab(jnp.maximum(r - 1, 0))
        first = lane32 < FSIDE
        own = TCP[:, slab(r)]
        back = pltpu.roll(jnp.where(first, own, TCP[:, before]), FSIDE, 1)
        back = jnp.where(jnp.logical_not(first) | (r > 0), back, 0.0)
        TCM[:, slab(r)] = back
        diag = frac_storage[:, slab(r)] + TAP[:, slab(r)] + TAM[:, slab(r)] + own + back
        diag = diag + S2[pl.ds(r, FR, stride=SLABS), :]
        FD[:, slab(r)] = diag
        INVF[:, slab(r)] = relaxation / diag
    loop(SLABS, face_back)

    def smooth_frac(k, source):
        def body(r):
            z = source[:, slab(r)] * INVF[:, slab(r)]
            ZF[k, :, slab(r)] = z
            F2[pl.ds(r, FR, stride=SLABS), :] = z
        loop(SLABS, body, 2)
        pick_slots(PICK)
        sfl[k] = CPL[...] * PICK[...]
        return [send(sfl.at[k], rfl.at[k, d], y_dev[d]) for d in (0, 1)]

    flux_sent = smooth_frac(0, frac_rhs)

    build_hot(0)
    spread_rock(0, CPL, True)
    for copy in slots_sent:
        copy.wait_recv()
    for d in (0, 1):
        IDX[1 + d] = ric[d, 0].astype(jnp.int32)
        build_hot(1 + d)
        spread_rock(1 + d, ric.at[d, 1], False)
    pick_rock(lambda i, j: agg[i, j * 8 : j * 8 + 8, :].astype(f32), [AGS, sag.at[0], sag.at[1]])
    aggs_sent = [send(sag.at[1 - d], rag.at[d], y_dev[d]) for d in (0, 1)]

    for copy in faces_sent:
        copy.wait_recv()
    open_x = [gx > 0, gx < n_gx - 1]
    open_y = [gy > 0, gy < n_gy - 1]

    def scale_rock(i):
        conduct = perm[i]
        PA[i + 1] = conduct
        PE[i + 1] = conduct * jnp.exp(-0.25 * pressure[i])
    loop(CX, scale_rock)
    for d, plane in enumerate((0, CX + 1)):
        conduct = jnp.where(open_x[d], rx[d, 0], 0.0)
        PA[plane] = conduct
        PE[plane] = conduct * jnp.exp(-0.25 * rx[d, 1])
    for d in (0, 1):
        conduct = jnp.where(open_y[d], ry[d, 0], 0.0)
        ry[d, 0] = conduct
        ry[d, 1] = conduct * jnp.exp(-0.25 * ry[d, 1])

    def below(x, edge):
        return jnp.where(sub16 == 0, edge, pltpu.roll(x, 1, 0))

    def above(x, edge):
        return jnp.where(sub16 == CY - 1, edge, pltpu.roll(x, CY - 1, 0))

    def rock_faces(i):
        conduct, scaled = PA[i + 1], PE[i + 1]
        row = pl.ds(i, 1)

        def weight(near, near_scaled):
            return 2.0 * scaled * near_scaled / (conduct + near)
        WX[i] = weight(PA[i], PE[i])
        WYM[i] = weight(below(conduct, ry[0, 0, row, :]), below(scaled, ry[0, 1, row, :]))
        WYP[i] = weight(above(conduct, ry[1, 0, row, :]), above(scaled, ry[1, 1, row, :]))
        up = weight(pltpu.roll(conduct, 127, 1), pltpu.roll(scaled, 127, 1))
        up = jnp.where(lane16 < NZ - 1, up, 0.0)
        WZP[i] = up
        WZM[i] = pltpu.roll(up, 1, 1)
    loop(CX, rock_faces)
    WX[CX] = 2.0 * PE[CX] * PE[CX + 1] / (PA[CX] + PA[CX + 1])

    def rock_diagonal(i):
        faces = [WX[i], WX[i + 1], WYM[i], WYP[i], WZM[i], WZP[i]]
        rows = pl.ds(pl.multiple_of(i * CY, CY), CY)
        diag = storage[i] + sum(faces) + DEL[rows, :]
        RD[i] = diag
        INVR[i] = relaxation / diag
        mine = agg[i]
        inside = lambda n: jnp.clip(n, 0, CX - 1)
        nears = [
            jnp.where(i > 0, agg[inside(i - 1)], -1),
            jnp.where(i < CX - 1, agg[inside(i + 1)], -1),
            below(mine, -1), above(mine, -1),
            pltpu.roll(mine, 1, 1), pltpu.roll(mine, 127, 1),
        ]
        for face, near in zip(faces, nears):
            diag = diag - jnp.where(near == mine, face, 0.0)
        S[i] = diag
    loop(CX, rock_diagonal)
    coarse_diag = aggregate_sums(S)
    coarse_diag = jnp.where(lane16 < NAGG, coarse_diag, 1.0)

    def stencil(i, center, low_x, high_x, low_y, high_y):
        out = RD[i] * center
        out = out - WX[i] * low_x - WX[i + 1] * high_x
        out = out - WYM[i] * below(center, low_y) - WYP[i] * above(center, high_y)
        return out - WZM[i] * pltpu.roll(center, 1, 1) - WZP[i] * pltpu.roll(center, 127, 1)

    def iterate(k, rock_vec, frac_vec, flux_sent):
        def smooth_rock(i):
            Z0[k, i + 1] = rock_vec[i] * INVR[i]
        loop(CX, smooth_rock, 2)
        for d, row in enumerate((CY - 1, 0)):
            szy[k, d] = Z0[k, 1 : CX + 1, row, :]
        halo_sent = [
            send(Z0.at[k, CX], Z0.at[k, 0], x_dev[0]),
            send(Z0.at[k, 1], Z0.at[k, CX + 1], x_dev[1]),
        ] + [send(szy.at[k, d], rzy.at[k, d], y_dev[d]) for d in (0, 1)]
        pick_rock(lambda i, j: Z0[k, i + 1, j * 8 : j * 8 + 8, :],
                  [HV, sans.at[k, 0], sans.at[k, 1]])
        answers_sent = [send(sans.at[k, 1 - d], rans.at[k, d], y_dev[d]) for d in (0, 1)]
        values = pick_ends()
        spread_rock(0, sfl.at[k], True)
        for d, copy in enumerate(flux_sent):
            copy.wait_recv()
            spread_rock(1 + d, rfl.at[k, d], False)
        for copy in halo_sent:
            copy.wait_recv()

        def residual(i):
            row = pl.ds(i, 1)
            rows = pl.ds(pl.multiple_of(i * CY, CY), CY)
            image = stencil(i, Z0[k, i + 1], Z0[k, i], Z0[k, i + 2],
                            rzy[k, 0, row, :], rzy[k, 1, row, :]) - DEL[rows, :]
            Q[i] = image
            S[i] = rock_vec[i] - image
        loop(CX, residual)
        coarse = aggregate_sums(S) / coarse_diag
        scs[k] = coarse[0:8]
        coarse_sent = [send(scs.at[k], rcs.at[k, d], x_dev[d]) for d in (0, 1)]
        coarse_sent += [send(scs.at[k], rcs.at[k, 2 + d], y_dev[d]) for d in (0, 1)]

        def correct(i):
            E[k, i + 1] = lanes_of(coarse, agg[i])
        loop(CX, correct, 2)
        if k == 0:
            for copy in aggs_sent:
                copy.wait_recv()
            AGS[...] = AGS[...] + rag[0] + rag[1]
        for copy in answers_sent + coarse_sent:
            copy.wait_recv()
        tables = [jnp.concatenate([rcs[k, d], rcs[k, d]], axis=0) for d in range(4)]
        for d, plane in enumerate((0, CX + 1)):
            E[k, plane] = lanes_of(tables[d], rx[d, 2].astype(jnp.int32))
        for d in (0, 1):
            table = jnp.concatenate([tables[2 + d]] * 2, axis=0)
            VALS[d] = lanes_of(table, ry[d, 2].astype(jnp.int32))
        slot_agg = AGS[...].astype(jnp.int32)
        four = [jnp.concatenate([t] * 2, axis=0) for t in (coarse, tables[2], tables[3])]
        own, low, high = [lanes_of(t, slot_agg) for t in four]
        where = OFF[...]
        host = HV[...] + rans[k, 0] + rans[k, 1]
        host = host + jnp.where(where == 0, own, jnp.where(where < 0, low, high))
        VALS[2] = CPL[...] * host
        coefs = [XV[h : h + 1, :] for h in (0, 1)]
        spread_frac(VALS.at[2], [coefs[h] * values[2 * (1 - e) + h] for e, h in ends])

        zero = jnp.zeros((8, 128), f32)

        def fold(x):
            return sum(x[j : j + 8] for j in range(0, x.shape[0], 8))

        def products(x, v, b):
            if k == 0:
                return fold(v * v), fold(x * v), fold(x * x)
            return fold(x * b), fold(x * v), fold(x * x)

        def rock_image(i, accs):
            row = pl.ds(i, 1)
            vec = rock_vec[i]
            image = Q[i] + stencil(i, E[k, i + 1], E[k, i], E[k, i + 2],
                                   VALS[0, row, :], VALS[1, row, :])
            image = image - relaxation * vec
            if k == 0:
                W1R[i] = image
            return tuple(a + p for a, p in zip(accs, products(image, vec, rock_rhs[i])))
        accs = lax.fori_loop(0, CX, rock_image, (zero,) * 3)

        def frac_image(r, accs):
            here = slab(r)
            vec = frac_vec[:, here]
            z = ZF[k, :, here]
            before = ZF[k, :, slab(jnp.maximum(r - 1, 0))]
            after = ZF[k, :, slab(jnp.minimum(r + 1, SLABS - 1))]
            first = lane32 < FSIDE
            down = pltpu.roll(jnp.where(first, after, z), FSIDE, 1)
            up = pltpu.roll(jnp.where(first, z, before), FSIDE, 1)
            image = FD[:, here] * z - S2[pl.ds(r, FR, stride=SLABS), :]
            image = image - TAP[:, here] * pltpu.roll(z, 127, 1) - TAM[:, here] * pltpu.roll(z, 1, 1)
            image = image - TCP[:, here] * down - TCM[:, here] * up
            image = image - relaxation * vec
            if k == 0:
                W1F[:, here] = image
            return tuple(a + p for a, p in zip(accs, products(image, vec, frac_rhs[:, here])))
        return lax.fori_loop(0, SLABS, frac_image, accs)

    dots = list(iterate(0, rock_rhs, frac_rhs, flux_sent))
    flux_sent = smooth_frac(1, W1F)
    dots += list(iterate(1, W1R, W1F, flux_sent))

    tile = jnp.zeros((8, 128), f32)
    for n, part in enumerate(dots):
        tile = jnp.where(sub8 == n, jnp.sum(part, axis=0, keepdims=True), tile)
    groups = [(AR0, gx, gx_peers, n_gx), (AR1, my_y, y_peers, n_y), (AR2, my_z, z_peers, n_z)]
    for slots, me, peers, size in groups:
        slots[pl.ds(me, 1)] = tile[None]
        copies = [send(slots.at[me], slots.at[me], device) for device in peers]
        for copy in copies:
            copy.wait_recv()
        tile = sum(slots[n] for n in range(size))
    tile = jnp.sum(tile, axis=1, keepdims=True)
    bb, pb, pp, qb, qp, qq = [tile[n : n + 1, :] for n in range(6)]
    gram = [[bb, pb, qb], [pb, pp, qp], [qb, qp, qq]]
    shift = relaxation

    def inner(a, c):
        return sum(a[m] * c[n] * gram[m][n] for m in range(3) for n in range(3))

    one, none = jnp.ones((1, 1), f32), jnp.zeros((1, 1), f32)
    start_norm = jnp.sqrt(bb + epsilon)
    v0 = [one / start_norm, none, none]
    image = [shift * v0[0], v0[0], none]
    rest0 = inner(image, image)
    h00 = inner(image, v0)
    image = [a - h00 * c for a, c in zip(image, v0)]
    h10 = jnp.sqrt(jnp.maximum(inner(image, image), 0.0) + epsilon)
    v1 = [a / h10 for a in image]
    image = [shift * v1[0], v1[0] + shift * v1[1], v1[1]]
    h01, h11 = inner(image, v0), inner(image, v1)
    image = [a - h01 * c - h11 * d for a, c, d in zip(image, v0, v1)]
    h21 = jnp.sqrt(jnp.maximum(inner(image, image), 0.0) + epsilon)

    radius = jnp.sqrt(h00 * h00 + h10 * h10)
    cosine, sine = h00 / radius, h10 / radius
    upper01 = cosine * h01 + sine * h11
    lower = cosine * h11 - sine * h01
    right0, right1 = cosine * start_norm, -sine * start_norm
    radius1 = jnp.sqrt(lower * lower + h21 * h21)
    cosine1, sine1 = lower / radius1, h21 / radius1
    res_out[...] = jnp.abs(-sine1 * right1)
    y1 = cosine1 * right1 / radius1
    y0 = (right0 - upper01 * y1) / radius
    on_b = y0 * v0[0] + y1 * v1[0]
    on_p = y1 * v1[1]

    def rock_update(i):
        rock_out[i] = on_b * (Z0[0, i + 1] + E[0, i + 1]) + on_p * (Z0[1, i + 1] + E[1, i + 1])
    loop(CX, rock_update, 2)

    def frac_update(r):
        frac_out[:, slab(r)] = on_b * ZF[0, :, slab(r)] + on_p * ZF[1, :, slab(r)]
    loop(SLABS, frac_update, 2)
    for copy in started:
        copy.wait_send()


def local(sizes, rock_rhs, frac_rhs, perm, storage, pressure, frac_perm, frac_storage,
          frac_pressure, couple_geom, couple_count, couple_frac_cell, couple_rock_cell,
          host_offset, cross_pairs, cross_geom, aggregates):
    n_gx, n_y, n_z = sizes
    vmem = pl.BlockSpec(memory_space=pltpu.VMEM)
    smem = pl.BlockSpec(memory_space=pltpu.SMEM)
    in_specs = [vmem] * 16
    in_specs[9] = in_specs[12] = smem
    block = (CX, CY, NZ)
    tall = (CX + 2, CY, NZ)
    frac = (FR, FCELLS)
    slot = (FR, KC)

    def mem(*shape, kind=f32):
        return pltpu.VMEM(shape, kind)

    scratch = [
        mem(2, *tall), mem(2, *tall), mem(*tall), mem(*tall), mem(CX + 1, CY, NZ),
        *[mem(*block) for _ in range(9)], mem(ROWS, 128), mem(128, 128),
        *[mem(*frac) for _ in range(7)], mem(2, *frac), mem(FR * SLABS, 128), mem(FR * SLABS, 128),
        mem(3, ROWS, FR * KC, kind=bf16), mem(256, FR * KC, kind=bf16),
        mem(FR, 128, 128, kind=bf16), mem(FR * SLABS, 2 * CROSS, kind=bf16),
        mem(256, 2 * CROSS, kind=bf16), mem(8, 128),
        mem(3, *slot, kind=jnp.int32), mem(*slot, kind=jnp.int32),
        mem(*slot), mem(*slot), mem(*slot), mem(*slot), mem(3, *slot),
        mem(2, 3, CY, NZ), mem(2, 3, CY, NZ), mem(2, 3, CX, NZ), mem(2, 3, CX, NZ),
        mem(2, 2, *slot), mem(2, 2, *slot), mem(2, *slot), mem(2, *slot),
        mem(2, 2, CX, NZ), mem(2, 2, CX, NZ), mem(2, *slot), mem(2, 2, *slot),
        mem(2, 2, *slot), mem(2, 2, *slot), mem(2, 8, 128), mem(2, 4, 8, 128),
        mem(n_gx, 8, 128), mem(n_y, 8, 128), mem(n_z, 8, 128),
        pltpu.SemaphoreType.DMA((64,)), pltpu.SemaphoreType.DMA((64,)),
    ]
    rock, fracs, norm = pl.pallas_call(
        functools.partial(kernel, sizes),
        out_shape=(
            jax.ShapeDtypeStruct(block, f32),
            jax.ShapeDtypeStruct(frac, f32),
            jax.ShapeDtypeStruct((1, 1), f32),
        ),
        in_specs=in_specs,
        out_specs=(vmem, vmem, vmem),
        scratch_shapes=scratch,
        compiler_params=pltpu.CompilerParams(
            collective_id=0, has_side_effects=True, vmem_limit_bytes=60 * 1024 * 1024),
    )(rock_rhs, frac_rhs, perm, storage, pressure, frac_perm, frac_storage, frac_pressure,
      couple_geom, couple_count, couple_frac_cell, couple_rock_cell, host_offset, cross_pairs,
      cross_geom.reshape(1, CROSS), aggregates)
    return rock, fracs, norm[0, 0]


def solution(mesh):
    n_gx, n_gy = mesh.shape["gx"], mesh.shape["gy"]
    n_z = 8 if n_gy % 8 == 0 else 2
    grid = P("gx", "gy", None)
    owned = P(("gx", "gy"), None)
    flat = P(("gx", "gy"))
    in_specs = (grid, owned, grid, grid, grid, owned, owned, owned, owned, flat, owned, owned,
                flat, P(None, ("gx", "gy")), flat, grid)
    return jax.shard_map(
        functools.partial(local, (n_gx, n_gy // n_z, n_z)), mesh=mesh, in_specs=in_specs,
        out_specs=(grid, owned, P()), check_vma=False)
```

```python
import functools

import jax
import jax.numpy as jnp
from jax import lax
from jax.experimental import pallas as pl
from jax.experimental.pallas import tpu as pltpu
from jax.sharding import PartitionSpec as P

CX, CY, NZ = 32, 16, 128
FR, FCELLS, FSIDE, KC = 32, 4096, 64, 128
SLABS = FCELLS // 128
NAGG = 64
ROWS = CX * CY
CROSS = 256
relaxation = 0.8
epsilon = 1e-06
MESH = pl.DeviceIdType.MESH
f32 = jnp.float32
bf16 = jnp.bfloat16


def iota(shape, dim):
    return lax.broadcasted_iota(jnp.int32, shape, dim)


def loop(count, body, unroll=1):
    lax.fori_loop(0, count, lambda i, c: (body(i), c)[1], 0, unroll=unroll)


def halves(x):
    high = x.astype(bf16)
    return high, (x - high.astype(f32)).astype(bf16)


def nt_dot(a, b):
    return lax.dot_general(a, b, (((1,), (1,)), ((), ())), preferred_element_type=f32)


def inverse(x):
    guess = pl.reciprocal(x, approx=True)
    guess = guess * (2.0 - x * guess)
    return guess * (2.0 - x * guess)


def lanes_of(table, index):
    return jnp.take_along_axis(table, index, axis=1)


def kernel(
    sizes,
    rock_rhs, frac_rhs, perm, storage, pressure, frac_perm, frac_storage, frac_pressure,
    geom, count, frac_cell, rock_cell, offset, pairs, cross_geom, agg,
    rock_out, frac_out, res_out,
    Z0, E, PA, PE, WX, WYM, WYP, WZM, WZP, RD, INVR, W1R, Q, S, DEL,
    FD, INVF, TAP, TAM, TCP, TCM, W1F, ZF, F2, S2,
    U, LH, LV, TT, TF, BF, XU, LVX, AX, AY, AG, FI, XV, IDX, OFF, CPL, PICK, HV, AGS, VALS,
    sx, rx, sy, ry, sic, ric, szy, rzy, sfl, rfl, sans, rans, scs, rcs,
    AR0, AR1, AR2, send_sem, recv_sem,
):
    n_gx, n_y, n_z = sizes
    n_gy = n_y * n_z
    gx = lax.axis_index("gx")
    gy = lax.axis_index("gy")
    my_y, my_z = gy // n_z, gy % n_z
    x_dev = [((gx + 1) % n_gx, gy), ((gx + n_gx - 1) % n_gx, gy)]
    y_dev = [(gx, (gy + 1) % n_gy), (gx, (gy + n_gy - 1) % n_gy)]
    gx_peers = [((gx + p) % n_gx, gy) for p in range(1, n_gx)]
    y_peers = [(gx, (my_y + p) % n_y * n_z + my_z) for p in range(1, n_y)]
    z_peers = [(gx, my_y * n_z + (my_z + p) % n_z) for p in range(1, n_z)]

    barrier = pltpu.get_barrier_semaphore()
    everyone = gx_peers + y_peers + z_peers + y_dev
    for device in everyone:
        pl.semaphore_signal(barrier, inc=1, device_id=device, device_id_type=MESH)

    started = []

    def send(src, dst, device):
        number = len(started)
        copy = pltpu.make_async_remote_copy(
            src_ref=src, dst_ref=dst, send_sem=send_sem.at[number],
            recv_sem=recv_sem.at[number], device_id=device, device_id_type=MESH,
        )
        copy.start()
        started.append(copy)
        return copy

    sub8 = iota((8, 128), 0)
    sub16 = iota((16, 128), 0)
    sub32 = iota((32, 128), 0)
    sub128 = iota((128, 128), 0)
    lane16 = iota((16, 128), 1)
    lane32 = iota((32, 128), 1)
    row_lane = iota((1, 128), 1)
    short_rows = iota((ROWS, 128), 0).astype(jnp.int16)

    def to_table(get):
        def body(r):
            F2[pl.ds(r, FR, stride=SLABS), :] = get(r)
        loop(SLABS, body, 2)

    def slab(r):
        return pl.ds(pl.multiple_of(r * 128, 128), 128)

    def pick_slots(out):
        def body(f):
            cell = frac_cell[pl.ds(f, 1), :]
            table = F2[pl.ds(pl.multiple_of(f * SLABS, SLABS), SLABS), :]
            got = lanes_of(table, jnp.broadcast_to(cell & 127, (SLABS, 128)))
            out[pl.ds(f, 1), :] = jnp.sum(
                jnp.where(sub32 == cell >> 7, got, 0.0), axis=0, keepdims=True)
        loop(FR, body, 4)

    ends = [(e, h) for e in (0, 1) for h in (0, 1)]

    def end_cells(e, h):
        return pairs[e : e + 1, h * 128 : (h + 1) * 128]

    def turn(get, blocks, out, exact=False):
        for m in range(blocks):
            block = get(m).T
            if exact:
                out[0:128, m * 128 : (m + 1) * 128] = block.astype(bf16)
            else:
                high, low = halves(block)
                out[0:128, m * 128 : (m + 1) * 128] = high
                out[128:256, m * 128 : (m + 1) * 128] = low

    def pick_ends():
        turn(lambda m: F2[m * 128 : (m + 1) * 128, :], 8, TF)
        got = jnp.dot(TF[...], XU[...], preferred_element_type=f32)
        got = got[0:128] + got[128:256]
        return [
            jnp.sum(jnp.where(sub128 == (end_cells(e, h) & 127),
                              got[:, n * 128 : (n + 1) * 128], 0.0), axis=0, keepdims=True)
            for n, (e, h) in enumerate(ends)
        ]

    def spread_ends(end_vals):
        for n, (e, h) in enumerate(ends):
            hot = sub128 == (end_cells(e, h) & 127)
            high = end_vals[n].astype(bf16).astype(f32)
            low = end_vals[n] - high
            LVX[0:128, n * 128 : (n + 1) * 128] = jnp.where(hot, high, 0.0).astype(bf16)
            LVX[128:256, n * 128 : (n + 1) * 128] = jnp.where(hot, low, 0.0).astype(bf16)
        part = nt_dot(XU[...], LVX[...])
        S2[...] = part[:, :128] + part[:, 128:]

    def spread_slots(slot_vals):
        def body(f):
            cell = frac_cell[pl.ds(f, 1), :]
            high, low = halves(jnp.where(sub32 == cell >> 7, slot_vals[pl.ds(f, 1), :], 0.0))
            part = nt_dot(jnp.concatenate([high, low], axis=0), BF[f])
            rows = pl.ds(pl.multiple_of(f * SLABS, SLABS), SLABS)
            S2[rows, :] = S2[rows, :] + part[:32] + part[32:]
        loop(FR, body, FR)

    def build_hot(src):
        def body(f):
            cell = jnp.broadcast_to(IDX[src, pl.ds(f, 1), :], (16, 128))
            high = jnp.concatenate([(cell >> 7).astype(jnp.int16)] * 32, axis=0)
            low = jnp.concatenate([(cell & 127).astype(jnp.int16)] * 8, axis=0)
            U[src, :, slab(f)] = jnp.where(short_rows == high, bf16(1), bf16(0))
            LH[src, :, slab(f)] = jnp.where(short_rows[:128] == low, bf16(1), bf16(0))
        loop(FR, body, 2)

    def spread_rock(src, vals, first):
        def body(f):
            value = vals[pl.ds(f, 1), :]
            high = value.astype(bf16).astype(f32)
            hot = LH[src, :, slab(f)]
            for m, part in enumerate((high, value - high)):
                part = jnp.broadcast_to(part, (16, 128)).astype(bf16)
                LV[m * 128 : m * 128 + 128, slab(f)] = hot * jnp.concatenate([part] * 8, axis=0)
        loop(FR, body, FR)
        part = nt_dot(U[src], LV[...])
        total = part[:, :128] + part[:, 128:]
        DEL[...] = total if first else DEL[...] + total

    def pick_rock(get, outs, agg_outs=None):
        turn(get, 4, TT)
        if agg_outs:
            for m in range(4):
                block = agg[m * 8 : m * 8 + 8].astype(f32).reshape(128, 128).T
                TT[256:384, m * 128 : (m + 1) * 128] = block.astype(bf16)
        table = TT[...] if agg_outs else TT[0:256]
        for src in range(3):
            got = jnp.dot(table, U[src], preferred_element_type=f32)
            for f in range(FR):
                row, here = slice(f, f + 1), slice(f * 128, f * 128 + 128)
                hot = sub128 == IDX[src, row, :] & 127
                value = got[0:128, here] + got[128:256, here]
                outs[src][row, :] = jnp.sum(jnp.where(hot, value, 0.0), axis=0, keepdims=True)
                if agg_outs:
                    agg_outs[src][row, :] = jnp.sum(
                        jnp.where(hot, got[256:384, here], 0.0), axis=0, keepdims=True)

    def agg_cells(b, h):
        cells = agg[2 * b + h]
        return cells, pl.ds(pl.multiple_of(b * 256 + h * 128, 128), 128)

    def build_aggregates():
        def body(b):
            for h in (0, 1):
                cells, here = agg_cells(b, h)
                cells = (cells & 15).astype(jnp.int16)
                for a in range(16):
                    AY[a * 16 : a * 16 + 16, here] = jnp.where(
                        cells == jnp.int16(a), bf16(1), bf16(0))
        loop(16, body, 2)
        place = iota((256, 128), 0) >> 4 == iota((256, 128), 1) & 15
        AG[...] = place.astype(f32).astype(bf16)

    def aggregate_sums(src):
        def body(b):
            for h in (0, 1):
                cells, here = agg_cells(b, h)
                cells = cells >> 4
                value = src[2 * b + h]
                high = value.astype(bf16).astype(f32)
                low = value - high
                for a in range(4):
                    AX[a * 32 : a * 32 + 16, here] = jnp.where(cells == a, high, 0.0).astype(bf16)
                    AX[a * 32 + 16 : a * 32 + 32, here] = jnp.where(cells == a, low, 0.0).astype(bf16)
        loop(16, body, 8)
        part = nt_dot(AX[...], AY[...])
        part = jnp.where(iota((128, 256), 0) & 15 == iota((128, 256), 1) & 15, part, 0.0)
        rest = jnp.concatenate([fold(part[a * 32 : a * 32 + 32]) for a in range(4)], axis=0)
        pieces = []
        for _ in range(3):
            pieces.append(rest.astype(bf16))
            rest = rest - pieces[-1].astype(f32)
        total = jnp.dot(jnp.concatenate(pieces, axis=0), AG[...], preferred_element_type=f32)
        total = total[0:32] + total[32:64] + total[64:96]
        total = jnp.where(sub32 >> 3 == lane32 >> 4, total, 0.0)
        return jnp.broadcast_to(jnp.sum(total, axis=0, keepdims=True), (16, 128))

    def fold(x):
        return sum(x[j : j + 8] for j in range(0, x.shape[0], 8))

    to_table(lambda r: frac_pressure[:, slab(r)])
    pick_slots(PICK)

    def split_slots(f):
        where = offset[f]
        row = pl.ds(f, 1)
        OFF[row, :] = jnp.full((1, 128), where, jnp.int32)
        cell = rock_cell[row, :]
        live = row_lane < count[f]
        IDX[0, row, :] = jnp.where(live & (where == 0), cell, -1)
        sic[0, 0, row, :] = jnp.where(live & (where == 1), cell, -1).astype(f32)
        sic[1, 0, row, :] = jnp.where(live & (where == -1), cell, -1).astype(f32)
        value = jnp.where(live, geom[row, :] * jnp.exp(-0.5 * PICK[row, :]), 0.0)
        CPL[row, :] = value
    loop(FR, split_slots, 4)
    sic[0, 1] = CPL[...]
    sic[1, 1] = CPL[...]

    for d, plane in enumerate((CX - 1, 0)):
        sx[d, 0] = perm[plane]
        sx[d, 1] = pressure[plane]
        sx[d, 2] = agg[plane].astype(f32)
    for d, row in enumerate((CY - 1, 0)):
        sy[d, 0] = perm[:, row, :]
        sy[d, 1] = pressure[:, row, :]
        sy[d, 2] = agg[:, row, :].astype(f32)

    pl.semaphore_wait(barrier, len(everyone))
    slots_sent = [send(sic.at[d], ric.at[d], y_dev[d]) for d in (0, 1)]
    faces_sent = [send(sx.at[d], rx.at[d], x_dev[d]) for d in (0, 1)]
    faces_sent += [send(sy.at[d], ry.at[d], y_dev[d]) for d in (0, 1)]

    def scale_frac(r):
        press = frac_pressure[:, slab(r)]
        TCM[:, slab(r)] = frac_perm[:, slab(r)] * jnp.exp(-0.25 * press)
    loop(SLABS, scale_frac, 4)

    def face_along(r):
        conduct, scaled = frac_perm[:, slab(r)], TCM[:, slab(r)]
        near, near_scaled = pltpu.roll(conduct, 127, 1), pltpu.roll(scaled, 127, 1)
        weight = 2.0 * scaled * near_scaled * inverse(conduct + near)
        weight = jnp.where(lane32 & (FSIDE - 1) < FSIDE - 1, weight, 0.0)
        TAP[:, slab(r)] = weight
        TAM[:, slab(r)] = pltpu.roll(weight, 1, 1)
        after = slab(jnp.minimum(r + 1, SLABS - 1))
        first = lane32 < FSIDE
        near = pltpu.roll(jnp.where(first, frac_perm[:, after], conduct), FSIDE, 1)
        near_scaled = pltpu.roll(jnp.where(first, TCM[:, after], scaled), FSIDE, 1)
        weight = 2.0 * scaled * near_scaled * inverse(conduct + near)
        TCP[:, slab(r)] = jnp.where(first | (r < SLABS - 1), weight, 0.0)
    loop(SLABS, face_along, 4)

    for n, (e, h) in enumerate(ends):
        for m in range(8):
            hot = (sub128 + m * 128 == end_cells(e, h) >> 7).astype(f32).astype(bf16)
            XU[m * 128 : (m + 1) * 128, n * 128 : (n + 1) * 128] = hot
    pressures = pick_ends()
    for h in (0, 1):
        XV[h : h + 1, :] = cross_geom[0:1, h * 128 : (h + 1) * 128] * jnp.exp(
            -0.25 * (pressures[h] + pressures[h + 2]))

    def build_lanes(f):
        BF[f] = (sub128 == (frac_cell[pl.ds(f, 1), :] & 127)).astype(f32).astype(bf16)
    loop(FR, build_lanes, 2)
    coefs = [XV[h : h + 1, :] for h in (0, 1)]
    spread_ends(coefs + coefs)
    spread_slots(CPL)

    def face_back(r):
        before = slab(jnp.maximum(r - 1, 0))
        first = lane32 < FSIDE
        own = TCP[:, slab(r)]
        back = pltpu.roll(jnp.where(first, own, TCP[:, before]), FSIDE, 1)
        back = jnp.where(jnp.logical_not(first) | (r > 0), back, 0.0)
        TCM[:, slab(r)] = back
        diag = frac_storage[:, slab(r)] + TAP[:, slab(r)] + TAM[:, slab(r)] + own + back
        diag = diag + S2[pl.ds(r, FR, stride=SLABS), :]
        FD[:, slab(r)] = diag
        INVF[:, slab(r)] = relaxation * inverse(diag)
    loop(SLABS, face_back, 4)

    def smooth_frac(k, source):
        def body(r):
            z = source[:, slab(r)] * INVF[:, slab(r)]
            ZF[k, :, slab(r)] = z
            F2[pl.ds(r, FR, stride=SLABS), :] = z
        loop(SLABS, body, 4)
        pick_slots(PICK)
        sfl[k] = CPL[...] * PICK[...]
        return [send(sfl.at[k], rfl.at[k, d], y_dev[d]) for d in (0, 1)]

    flux_sent = smooth_frac(0, frac_rhs)

    build_hot(0)
    spread_rock(0, CPL, True)
    for copy in slots_sent:
        copy.wait_recv()
    for d in (0, 1):
        IDX[1 + d] = ric[d, 0].astype(jnp.int32)
        build_hot(1 + d)
        spread_rock(1 + d, ric.at[d, 1], False)
    build_aggregates()
    for copy in faces_sent:
        copy.wait_recv()
    open_x = [gx > 0, gx < n_gx - 1]
    open_y = [gy > 0, gy < n_gy - 1]

    def scale_rock(i):
        conduct = perm[i]
        PA[i + 1] = conduct
        PE[i + 1] = conduct * jnp.exp(-0.25 * pressure[i])
    loop(CX, scale_rock, 4)
    for d, plane in enumerate((0, CX + 1)):
        conduct = jnp.where(open_x[d], rx[d, 0], 0.0)
        PA[plane] = conduct
        PE[plane] = conduct * jnp.exp(-0.25 * rx[d, 1])
    for d in (0, 1):
        conduct = jnp.where(open_y[d], ry[d, 0], 0.0)
        ry[d, 0] = conduct
        ry[d, 1] = conduct * jnp.exp(-0.25 * ry[d, 1])

    def below(x, edge):
        return jnp.where(sub16 == 0, edge, pltpu.roll(x, 1, 0))

    def above(x, edge):
        return jnp.where(sub16 == CY - 1, edge, pltpu.roll(x, CY - 1, 0))

    def face(conduct, scaled, near, near_scaled):
        return 2.0 * scaled * near_scaled * inverse(conduct + near)

    VALS[0] = face(perm[:, 0, :], PE[1 : CX + 1, 0, :], ry[0, 0], ry[0, 1])

    def rock_faces(i):
        conduct, scaled = PA[i + 1], PE[i + 1]
        row = pl.ds(i, 1)
        WX[i] = face(conduct, scaled, PA[i], PE[i])
        side = face(conduct, scaled, above(conduct, ry[1, 0, row, :]),
                    above(scaled, ry[1, 1, row, :]))
        WYP[i] = side
        WYM[i] = below(side, VALS[0, row, :])
        up = face(conduct, scaled, pltpu.roll(conduct, 127, 1), pltpu.roll(scaled, 127, 1))
        up = jnp.where(lane16 < NZ - 1, up, 0.0)
        WZP[i] = up
        WZM[i] = pltpu.roll(up, 1, 1)
    loop(CX, rock_faces, 4)
    WX[CX] = face(PA[CX], PE[CX], PA[CX + 1], PE[CX + 1])

    def rock_diagonal(i):
        faces = [WX[i], WX[i + 1], WYM[i], WYP[i], WZM[i], WZP[i]]
        rows = pl.ds(pl.multiple_of(i * CY, CY), CY)
        diag = storage[i] + sum(faces) + DEL[rows, :]
        RD[i] = diag
        INVR[i] = relaxation * inverse(diag)
        mine = agg[i]
        inside = lambda n: jnp.clip(n, 0, CX - 1)
        nears = [
            jnp.where(i > 0, agg[inside(i - 1)], -1),
            jnp.where(i < CX - 1, agg[inside(i + 1)], -1),
            below(mine, -1), above(mine, -1),
            pltpu.roll(mine, 1, 1), pltpu.roll(mine, 127, 1),
        ]
        for face, near in zip(faces, nears):
            diag = diag - jnp.where(near == mine, face, 0.0)
        S[i] = diag
    loop(CX, rock_diagonal, 4)
    coarse_diag = aggregate_sums(S)
    inverse_coarse = 1.0 / jnp.where(lane16 < NAGG, coarse_diag, 1.0)

    def stencil(i, center, low_x, high_x, low_y, high_y):
        out = RD[i] * center
        out = out - WX[i] * low_x - WX[i + 1] * high_x
        out = out - WYM[i] * below(center, low_y) - WYP[i] * above(center, high_y)
        return out - WZM[i] * pltpu.roll(center, 1, 1) - WZP[i] * pltpu.roll(center, 127, 1)

    def send_faces(k):
        for d, row in enumerate((CY - 1, 0)):
            szy[k, d] = Z0[k, 1 : CX + 1, row, :]
        return [
            send(Z0.at[k, CX], Z0.at[k, 0], x_dev[0]),
            send(Z0.at[k, 1], Z0.at[k, CX + 1], x_dev[1]),
        ] + [send(szy.at[k, d], rzy.at[k, d], y_dev[d]) for d in (0, 1)]

    def iterate(k, rock_vec, frac_vec, halo_sent, flux_sent):
        pick_rock(lambda m: Z0[k, m * 8 + 1 : m * 8 + 9].reshape(128, 128),
                  [HV, sans.at[k, 0, 0], sans.at[k, 1, 0]],
                  None if k else [AGS, sans.at[k, 0, 1], sans.at[k, 1, 1]])
        parts = 1 if k else 2
        answers_sent = [
            send(sans.at[k, 1 - d, 0:parts], rans.at[k, d, 0:parts], y_dev[d]) for d in (0, 1)]
        spread_rock(0, sfl.at[k], True)
        for d, copy in enumerate(flux_sent):
            copy.wait_recv()
            spread_rock(1 + d, rfl.at[k, d], False)
        for copy in halo_sent:
            copy.wait_recv()

        def residual(i):
            row = pl.ds(i, 1)
            rows = pl.ds(pl.multiple_of(i * CY, CY), CY)
            image = stencil(i, Z0[k, i + 1], Z0[k, i], Z0[k, i + 2],
                            rzy[k, 0, row, :], rzy[k, 1, row, :]) - DEL[rows, :]
            Q[i] = image
            S[i] = rock_vec[i] - image
        loop(CX, residual, 8)
        coarse = aggregate_sums(S) * inverse_coarse
        scs[k] = coarse[0:8]
        coarse_sent = [send(scs.at[k], rcs.at[k, d], x_dev[d]) for d in (0, 1)]
        coarse_sent += [send(scs.at[k], rcs.at[k, 2 + d], y_dev[d]) for d in (0, 1)]

        values = pick_ends()
        coefs = [XV[h : h + 1, :] for h in (0, 1)]
        spread_ends([coefs[h] * values[2 * (1 - e) + h] for e, h in ends])

        def correct(i):
            E[k, i + 1] = lanes_of(coarse, agg[i])
        loop(CX, correct, 8)

        def frac_faces(r):
            here = slab(r)
            z = ZF[k, :, here]
            before = ZF[k, :, slab(jnp.maximum(r - 1, 0))]
            after = ZF[k, :, slab(jnp.minimum(r + 1, SLABS - 1))]
            first = lane32 < FSIDE
            down = pltpu.roll(jnp.where(first, after, z), FSIDE, 1)
            up = pltpu.roll(jnp.where(first, z, before), FSIDE, 1)
            image = FD[:, here] * z
            image = image - TAP[:, here] * pltpu.roll(z, 127, 1) - TAM[:, here] * pltpu.roll(z, 1, 1)
            image = image - TCP[:, here] * down - TCM[:, here] * up
            FI[:, here] = image - relaxation * frac_vec[:, here]
        loop(SLABS, frac_faces, 4)
        for copy in answers_sent + coarse_sent:
            copy.wait_recv()
        if k == 0:
            AGS[...] = AGS[...] + rans[0, 0, 1] + rans[0, 1, 1]
        tables = [jnp.concatenate([rcs[k, d], rcs[k, d]], axis=0) for d in range(4)]
        for d, plane in enumerate((0, CX + 1)):
            E[k, plane] = lanes_of(tables[d], rx[d, 2].astype(jnp.int32))
        for d in (0, 1):
            table = jnp.concatenate([tables[2 + d]] * 2, axis=0)
            VALS[d] = lanes_of(table, ry[d, 2].astype(jnp.int32))
        slot_agg = AGS[...].astype(jnp.int32)
        four = [jnp.concatenate([t] * 2, axis=0) for t in (coarse, tables[2], tables[3])]
        own, low, high = [lanes_of(t, slot_agg) for t in four]
        where = OFF[...]
        host = HV[...] + rans[k, 0, 0] + rans[k, 1, 0]
        host = host + jnp.where(where == 0, own, jnp.where(where < 0, low, high))
        VALS[2] = CPL[...] * host

        zero = jnp.zeros((8, 128), f32)

        def products(x, v, b):
            if k == 0:
                return fold(v * v), fold(x * v), fold(x * x)
            return fold(x * b), fold(x * v), fold(x * x)

        def rock_image(i, accs):
            row = pl.ds(i, 1)
            vec = rock_vec[i]
            image = Q[i] + stencil(i, E[k, i + 1], E[k, i], E[k, i + 2],
                                   VALS[0, row, :], VALS[1, row, :])
            image = image - relaxation * vec
            if k == 0:
                W1R[i] = image
                Z0[1, i + 1] = image * INVR[i]
            return tuple(a + p for a, p in zip(accs, products(image, vec, rock_rhs[i])))
        accs = lax.fori_loop(0, CX, rock_image, (zero,) * 3, unroll=8)
        halo_sent = send_faces(1) if k == 0 else None
        spread_slots(VALS.at[2])

        def frac_image(r, accs):
            here = slab(r)
            vec = frac_vec[:, here]
            image = FI[:, here] - S2[pl.ds(r, FR, stride=SLABS), :]
            if k == 0:
                W1F[:, here] = image
            return tuple(a + p for a, p in zip(accs, products(image, vec, frac_rhs[:, here])))
        accs = lax.fori_loop(0, SLABS, frac_image, accs, unroll=4)
        return list(accs), halo_sent

    def smooth_rock(i):
        Z0[0, i + 1] = rock_rhs[i] * INVR[i]
    loop(CX, smooth_rock, 8)
    dots, halo_sent = iterate(0, rock_rhs, frac_rhs, send_faces(0), flux_sent)
    flux_sent = smooth_frac(1, W1F)
    dots += iterate(1, W1R, W1F, halo_sent, flux_sent)[0]

    tile = jnp.zeros((8, 128), f32)
    for n, part in enumerate(dots):
        tile = jnp.where(sub8 == n, jnp.sum(part, axis=0, keepdims=True), tile)
    groups = [(AR0, gx, gx_peers, n_gx), (AR1, my_y, y_peers, n_y), (AR2, my_z, z_peers, n_z)]
    for slots, me, peers, size in groups:
        slots[pl.ds(me, 1)] = tile[None]
        copies = [send(slots.at[me], slots.at[me], device) for device in peers]
        for copy in copies:
            copy.wait_recv()
        tile = sum(slots[n] for n in range(size))
    tile = jnp.sum(tile, axis=1, keepdims=True)
    bb, pb, pp, qb, qp, qq = [tile[n : n + 1, :] for n in range(6)]
    gram = [[bb, pb, qb], [pb, pp, qp], [qb, qp, qq]]
    shift = relaxation

    def inner(a, c):
        return sum(a[m] * c[n] * gram[m][n] for m in range(3) for n in range(3))

    one, none = jnp.ones((1, 1), f32), jnp.zeros((1, 1), f32)
    start_norm = jnp.sqrt(bb + epsilon)
    v0 = [one / start_norm, none, none]
    image = [shift * v0[0], v0[0], none]
    rest0 = inner(image, image)
    h00 = inner(image, v0)
    image = [a - h00 * c for a, c in zip(image, v0)]
    h10 = jnp.sqrt(jnp.maximum(inner(image, image), 0.0) + epsilon)
    v1 = [a / h10 for a in image]
    image = [shift * v1[0], v1[0] + shift * v1[1], v1[1]]
    h01, h11 = inner(image, v0), inner(image, v1)
    image = [a - h01 * c - h11 * d for a, c, d in zip(image, v0, v1)]
    h21 = jnp.sqrt(jnp.maximum(inner(image, image), 0.0) + epsilon)

    radius = jnp.sqrt(h00 * h00 + h10 * h10)
    cosine, sine = h00 / radius, h10 / radius
    upper01 = cosine * h01 + sine * h11
    lower = cosine * h11 - sine * h01
    right0, right1 = cosine * start_norm, -sine * start_norm
    radius1 = jnp.sqrt(lower * lower + h21 * h21)
    cosine1, sine1 = lower / radius1, h21 / radius1
    res_out[...] = jnp.abs(-sine1 * right1)
    y1 = cosine1 * right1 / radius1
    y0 = (right0 - upper01 * y1) / radius
    on_b = y0 * v0[0] + y1 * v1[0]
    on_p = y1 * v1[1]

    def rock_update(i):
        rock_out[i] = on_b * (Z0[0, i + 1] + E[0, i + 1]) + on_p * (Z0[1, i + 1] + E[1, i + 1])
    loop(CX, rock_update, 8)

    def frac_update(r):
        frac_out[:, slab(r)] = on_b * ZF[0, :, slab(r)] + on_p * ZF[1, :, slab(r)]
    loop(SLABS, frac_update, 8)
    for copy in started:
        copy.wait_send()


def local(sizes, rock_rhs, frac_rhs, perm, storage, pressure, frac_perm, frac_storage,
          frac_pressure, couple_geom, couple_count, couple_frac_cell, couple_rock_cell,
          host_offset, cross_pairs, cross_geom, aggregates):
    n_gx, n_y, n_z = sizes
    vmem = pl.BlockSpec(memory_space=pltpu.VMEM)
    smem = pl.BlockSpec(memory_space=pltpu.SMEM)
    in_specs = [vmem] * 16
    in_specs[9] = in_specs[12] = smem
    block = (CX, CY, NZ)
    tall = (CX + 2, CY, NZ)
    frac = (FR, FCELLS)
    slot = (FR, KC)

    def mem(*shape, kind=f32):
        return pltpu.VMEM(shape, kind)

    scratch = [
        mem(2, *tall), mem(2, *tall), mem(*tall), mem(*tall), mem(CX + 1, CY, NZ),
        *[mem(*block) for _ in range(9)], mem(ROWS, 128),
        *[mem(*frac) for _ in range(7)], mem(2, *frac), mem(FR * SLABS, 128), mem(FR * SLABS, 128),
        mem(3, ROWS, FR * KC, kind=bf16), mem(3, 128, FR * KC, kind=bf16),
        mem(256, FR * KC, kind=bf16), mem(384, ROWS, kind=bf16), mem(256, FR * SLABS, kind=bf16),
        mem(FR, 128, 128, kind=bf16), mem(FR * SLABS, 2 * CROSS, kind=bf16),
        mem(256, 2 * CROSS, kind=bf16), mem(128, 4096, kind=bf16), mem(256, 4096, kind=bf16),
        mem(256, 128, kind=bf16), mem(*frac), mem(8, 128),
        mem(3, *slot, kind=jnp.int32), mem(*slot, kind=jnp.int32),
        mem(*slot), mem(*slot), mem(*slot), mem(*slot), mem(3, *slot),
        mem(2, 3, CY, NZ), mem(2, 3, CY, NZ), mem(2, 3, CX, NZ), mem(2, 3, CX, NZ),
        mem(2, 2, *slot), mem(2, 2, *slot),
        mem(2, 2, CX, NZ), mem(2, 2, CX, NZ), mem(2, *slot), mem(2, 2, *slot),
        mem(2, 2, 2, *slot), mem(2, 2, 2, *slot), mem(2, 8, 128), mem(2, 4, 8, 128),
        mem(n_gx, 8, 128), mem(n_y, 8, 128), mem(n_z, 8, 128),
        pltpu.SemaphoreType.DMA((64,)), pltpu.SemaphoreType.DMA((64,)),
    ]
    rock, fracs, norm = pl.pallas_call(
        functools.partial(kernel, sizes),
        out_shape=(
            jax.ShapeDtypeStruct(block, f32),
            jax.ShapeDtypeStruct(frac, f32),
            jax.ShapeDtypeStruct((1, 1), f32),
        ),
        in_specs=in_specs,
        out_specs=(vmem, vmem, vmem),
        scratch_shapes=scratch,
        compiler_params=pltpu.CompilerParams(
            collective_id=0, has_side_effects=True, vmem_limit_bytes=60 * 1024 * 1024),
    )(rock_rhs, frac_rhs, perm, storage, pressure, frac_perm, frac_storage, frac_pressure,
      couple_geom, couple_count, couple_frac_cell, couple_rock_cell, host_offset, cross_pairs,
      cross_geom.reshape(1, CROSS), aggregates)
    return rock, fracs, norm[0, 0]


def solution(mesh):
    n_gx, n_gy = mesh.shape["gx"], mesh.shape["gy"]
    n_z = 8 if n_gy % 8 == 0 else 2
    grid = P("gx", "gy", None)
    owned = P(("gx", "gy"), None)
    flat = P(("gx", "gy"))
    in_specs = (grid, owned, grid, grid, grid, owned, owned, owned, owned, flat, owned, owned,
                flat, P(None, ("gx", "gy")), flat, grid)
    return jax.shard_map(
        functools.partial(local, (n_gx, n_gy // n_z, n_z)), mesh=mesh, in_specs=in_specs,
        out_specs=(grid, owned, P()), check_vma=False)
```

```python
import functools

import jax
import jax.numpy as jnp
from jax import lax
from jax.experimental import pallas as pl
from jax.experimental.pallas import tpu as pltpu
from jax.sharding import PartitionSpec as P

CX, CY, NZ = 32, 16, 128
FR, FCELLS, FSIDE, KC = 32, 4096, 64, 128
SLABS = FCELLS // 128
NAGG = 64
ROWS = CX * CY
CROSS = 256
relaxation = 0.8
epsilon = 1e-06
MESH = pl.DeviceIdType.MESH
UB, UF, UR = 32, 32, 32
f32 = jnp.float32
bf16 = jnp.bfloat16

def iota(shape, dim):
    return lax.broadcasted_iota(jnp.int32, shape, dim)

def loop(count, body, unroll=1):
    lax.fori_loop(0, count, lambda i, c: (body(i), c)[1], 0, unroll=unroll)

def halves(x):
    high = x.astype(bf16)
    return high, (x - high.astype(f32)).astype(bf16)

def nt_dot(a, b):
    return lax.dot_general(a, b, (((1,), (1,)), ((), ())), preferred_element_type=f32)

def inverse(x):
    guess = pl.reciprocal(x, approx=True)
    guess = guess * (2.0 - x * guess)
    return guess * (2.0 - x * guess)

def lanes_of(table, index):
    return jnp.take_along_axis(table, index, axis=1)

def kernel(
    sizes,
    rock_rhs, frac_rhs, perm, storage, pressure, frac_perm, frac_storage, frac_pressure,
    geom, count, frac_cell, rock_cell, offset, pairs, cross_geom, agg,
    rock_out, frac_out, res_out,
    Z0, E, PA, PE, WX, WYM, WYP, WZM, WZP, RD, INVR, W1R, Q, S, DEL,
    FD, INVF, TAP, TAM, TCP, TCM, W1F, ZF, F2, S2,
    U, LV, TT, TF, BF, XU, LVX, AX, AY, AG, FI, XV, IDX, OFF, CPL, PICK, HV, AGS, VALS,
    sx, rx, sy, ry, sic, ric, szy, rzy, sfl, rfl, sans, rans, scs, rcs,
    AR0, AR1, AR2, send_sem, recv_sem,
):
    n_gx, n_y, n_z = sizes
    n_gy = n_y * n_z
    gx = lax.axis_index("gx")
    gy = lax.axis_index("gy")
    my_y, my_z = gy // n_z, gy % n_z
    x_dev = [((gx + 1) % n_gx, gy), ((gx + n_gx - 1) % n_gx, gy)]
    y_dev = [(gx, (gy + 1) % n_gy), (gx, (gy + n_gy - 1) % n_gy)]
    gx_peers = [((gx + p) % n_gx, gy) for p in range(1, n_gx)]
    y_peers = [(gx, (my_y + p) % n_y * n_z + my_z) for p in range(1, n_y)]
    z_peers = [(gx, my_y * n_z + (my_z + p) % n_z) for p in range(1, n_z)]

    barrier = pltpu.get_barrier_semaphore()
    everyone = gx_peers + y_peers + z_peers + y_dev
    for device in everyone:
        pl.semaphore_signal(barrier, inc=1, device_id=device, device_id_type=MESH)

    started = []

    def send(src, dst, device):
        number = len(started)
        copy = pltpu.make_async_remote_copy(
            src_ref=src, dst_ref=dst, send_sem=send_sem.at[number],
            recv_sem=recv_sem.at[number], device_id=device, device_id_type=MESH,
        )
        copy.start()
        started.append(copy)
        return copy

    sub8 = iota((8, 128), 0)
    sub16 = iota((16, 128), 0)
    sub32 = iota((32, 128), 0)
    sub128 = iota((128, 128), 0)
    lane16 = iota((16, 128), 1)
    lane32 = iota((32, 128), 1)
    row_lane = iota((1, 128), 1)
    short_rows = iota((ROWS, 128), 0).astype(jnp.int16)

    def to_table(get):
        def body(r):
            F2[pl.ds(r, FR, stride=SLABS), :] = get(r)
        loop(SLABS, body, 2)

    def slab(r):
        return pl.ds(pl.multiple_of(r * 128, 128), 128)

    def pick_slots(out):
        def body(f):
            cell = frac_cell[pl.ds(f, 1), :]
            table = F2[pl.ds(pl.multiple_of(f * SLABS, SLABS), SLABS), :]
            got = lanes_of(table, jnp.broadcast_to(cell & 127, (SLABS, 128)))
            out[pl.ds(f, 1), :] = jnp.sum(
                jnp.where(sub32 == cell >> 7, got, 0.0), axis=0, keepdims=True)
        loop(FR, body, 32)

    ends = [(e, h) for e in (0, 1) for h in (0, 1)]

    def end_cells(e, h):
        return pairs[e : e + 1, h * 128 : (h + 1) * 128]

    def turn(get, blocks, out, exact=False):
        for m in range(blocks):
            block = get(m).T
            if exact:
                out[0:128, m * 128 : (m + 1) * 128] = block.astype(bf16)
            else:
                high, low = halves(block)
                out[0:128, m * 128 : (m + 1) * 128] = high
                out[128:256, m * 128 : (m + 1) * 128] = low

    def pick_ends():
        turn(lambda m: F2[m * 128 : (m + 1) * 128, :], 8, TF)
        got = jnp.dot(TF[...], XU[...], preferred_element_type=f32)
        got = got[0:128] + got[128:256]
        return [
            jnp.sum(jnp.where(sub128 == (end_cells(e, h) & 127),
                              got[:, n * 128 : (n + 1) * 128], 0.0), axis=0, keepdims=True)
            for n, (e, h) in enumerate(ends)
        ]

    def spread_ends(end_vals):
        for n, (e, h) in enumerate(ends):
            hot = sub128 == (end_cells(e, h) & 127)
            high = end_vals[n].astype(bf16).astype(f32)
            low = end_vals[n] - high
            LVX[0:128, n * 128 : (n + 1) * 128] = jnp.where(hot, high, 0.0).astype(bf16)
            LVX[128:256, n * 128 : (n + 1) * 128] = jnp.where(hot, low, 0.0).astype(bf16)
        part = nt_dot(XU[...], LVX[...])
        S2[...] = part[:, :128] + part[:, 128:]

    def spread_slots(slot_vals):
        def body(f):
            cell = frac_cell[pl.ds(f, 1), :]
            high, low = halves(jnp.where(sub32 == cell >> 7, slot_vals[pl.ds(f, 1), :], 0.0))
            part = nt_dot(jnp.concatenate([high, low], axis=0), BF[f])
            rows = pl.ds(pl.multiple_of(f * SLABS, SLABS), SLABS)
            S2[rows, :] = S2[rows, :] + part[:32] + part[32:]
        loop(FR, body, FR)

    def build_hot(src):
        def body(f):
            cell = jnp.broadcast_to(IDX[src, pl.ds(f, 1), :], (16, 128))
            high = jnp.concatenate([(cell >> 7).astype(jnp.int16)] * 32, axis=0)
            U[src, :, slab(f)] = jnp.where(short_rows == high, bf16(1), bf16(0))
        loop(FR, body, UB)

    def spread_rock(src, vals, first):
        def body(f):
            value = vals[pl.ds(f, 1), :]
            high = value.astype(bf16).astype(f32)
            cell = jnp.broadcast_to(IDX[src, pl.ds(f, 1), :] & 127, (16, 128))
            hot = short_rows[:128] == jnp.concatenate([cell.astype(jnp.int16)] * 8, axis=0)
            for m, part in enumerate((high, value - high)):
                part = jnp.broadcast_to(part, (16, 128)).astype(bf16)
                part = jnp.concatenate([part] * 8, axis=0)
                LV[m * 128 : m * 128 + 128, slab(f)] = jnp.where(hot, part, bf16(0))
        loop(FR, body, FR)
        part = nt_dot(U[src], LV[...])
        total = part[:, :128] + part[:, 128:]
        DEL[...] = total if first else DEL[...] + total

    def pick_rock(get, outs, agg_outs=None):
        turn(get, 4, TT)
        if agg_outs:
            for m in range(4):
                block = agg[m * 8 : m * 8 + 8].astype(f32).reshape(128, 128).T
                TT[256:384, m * 128 : (m + 1) * 128] = block.astype(bf16)
        table = TT[...] if agg_outs else TT[0:256]
        for src in range(3):
            got = jnp.dot(table, U[src], preferred_element_type=f32)
            for f in range(FR):
                row, here = slice(f, f + 1), slice(f * 128, f * 128 + 128)
                hot = sub128 == IDX[src, row, :] & 127
                value = got[0:128, here] + got[128:256, here]
                outs[src][row, :] = jnp.sum(jnp.where(hot, value, 0.0), axis=0, keepdims=True)
                if agg_outs:
                    agg_outs[src][row, :] = jnp.sum(
                        jnp.where(hot, got[256:384, here], 0.0), axis=0, keepdims=True)

    def agg_cells(b, h):
        cells = agg[2 * b + h]
        return cells, pl.ds(pl.multiple_of(b * 256 + h * 128, 128), 128)

    def build_aggregates():
        def body(b):
            for h in (0, 1):
                cells, here = agg_cells(b, h)
                cells = (cells & 15).astype(jnp.int16)
                for a in range(16):
                    AY[a * 16 : a * 16 + 16, here] = jnp.where(
                        cells == jnp.int16(a), bf16(1), bf16(0))
        loop(16, body, 2)
        place = iota((256, 128), 0) >> 4 == iota((256, 128), 1) & 15
        AG[...] = place.astype(f32).astype(bf16)

    def aggregate_sums(src):
        def body(b):
            for h in (0, 1):
                cells, here = agg_cells(b, h)
                cells = cells >> 4
                value = src[2 * b + h]
                high = value.astype(bf16).astype(f32)
                low = value - high
                for a in range(4):
                    AX[a * 32 : a * 32 + 16, here] = jnp.where(cells == a, high, 0.0).astype(bf16)
                    AX[a * 32 + 16 : a * 32 + 32, here] = jnp.where(cells == a, low, 0.0).astype(bf16)
        loop(16, body, 16)
        part = nt_dot(AX[...], AY[...])
        part = jnp.where(iota((128, 256), 0) & 15 == iota((128, 256), 1) & 15, part, 0.0)
        rest = jnp.concatenate([fold(part[a * 32 : a * 32 + 32]) for a in range(4)], axis=0)
        pieces = []
        for _ in range(3):
            pieces.append(rest.astype(bf16))
            rest = rest - pieces[-1].astype(f32)
        total = jnp.dot(jnp.concatenate(pieces, axis=0), AG[...], preferred_element_type=f32)
        total = total[0:32] + total[32:64] + total[64:96]
        total = jnp.where(sub32 >> 3 == lane32 >> 4, total, 0.0)
        return jnp.broadcast_to(jnp.sum(total, axis=0, keepdims=True), (16, 128))

    def fold(x):
        return sum(x[j : j + 8] for j in range(0, x.shape[0], 8))

    to_table(lambda r: frac_pressure[:, slab(r)])
    pick_slots(PICK)

    def split_slots(f):
        where = offset[f]
        row = pl.ds(f, 1)
        OFF[row, :] = jnp.full((1, 128), where, jnp.int32)
        cell = rock_cell[row, :]
        live = row_lane < count[f]
        IDX[0, row, :] = jnp.where(live & (where == 0), cell, -1)
        sic[0, 0, row, :] = jnp.where(live & (where == 1), cell, -1).astype(f32)
        sic[1, 0, row, :] = jnp.where(live & (where == -1), cell, -1).astype(f32)
        value = jnp.where(live, geom[row, :] * jnp.exp(-0.5 * PICK[row, :]), 0.0)
        CPL[row, :] = value
    loop(FR, split_slots, 4)
    sic[0, 1] = CPL[...]
    sic[1, 1] = CPL[...]

    for d, plane in enumerate((CX - 1, 0)):
        sx[d, 0] = perm[plane]
        sx[d, 1] = pressure[plane]
        sx[d, 2] = agg[plane].astype(f32)
    for d, row in enumerate((CY - 1, 0)):
        sy[d, 0] = perm[:, row, :]
        sy[d, 1] = pressure[:, row, :]
        sy[d, 2] = agg[:, row, :].astype(f32)

    pl.semaphore_wait(barrier, len(everyone))
    slots_sent = [send(sic.at[d], ric.at[d], y_dev[d]) for d in (0, 1)]
    faces_sent = [send(sx.at[d], rx.at[d], x_dev[d]) for d in (0, 1)]
    faces_sent += [send(sy.at[d], ry.at[d], y_dev[d]) for d in (0, 1)]

    def scale_frac(r):
        press = frac_pressure[:, slab(r)]
        TCM[:, slab(r)] = frac_perm[:, slab(r)] * jnp.exp(-0.25 * press)
    loop(SLABS, scale_frac, UF)

    def face_along(r):
        conduct, scaled = frac_perm[:, slab(r)], TCM[:, slab(r)]
        near, near_scaled = pltpu.roll(conduct, 127, 1), pltpu.roll(scaled, 127, 1)
        weight = 2.0 * scaled * near_scaled * inverse(conduct + near)
        weight = jnp.where(lane32 & (FSIDE - 1) < FSIDE - 1, weight, 0.0)
        TAP[:, slab(r)] = weight
        TAM[:, slab(r)] = pltpu.roll(weight, 1, 1)
        after = slab(jnp.minimum(r + 1, SLABS - 1))
        first = lane32 < FSIDE
        near = pltpu.roll(jnp.where(first, frac_perm[:, after], conduct), FSIDE, 1)
        near_scaled = pltpu.roll(jnp.where(first, TCM[:, after], scaled), FSIDE, 1)
        weight = 2.0 * scaled * near_scaled * inverse(conduct + near)
        TCP[:, slab(r)] = jnp.where(first | (r < SLABS - 1), weight, 0.0)
    loop(SLABS, face_along, UF)

    for n, (e, h) in enumerate(ends):
        for m in range(8):
            hot = (sub128 + m * 128 == end_cells(e, h) >> 7).astype(f32).astype(bf16)
            XU[m * 128 : (m + 1) * 128, n * 128 : (n + 1) * 128] = hot
    pressures = pick_ends()
    for h in (0, 1):
        XV[h : h + 1, :] = cross_geom[0:1, h * 128 : (h + 1) * 128] * jnp.exp(
            -0.25 * (pressures[h] + pressures[h + 2]))

    def build_lanes(f):
        BF[f] = (sub128 == (frac_cell[pl.ds(f, 1), :] & 127)).astype(f32).astype(bf16)
    loop(FR, build_lanes, 2)

    coefs = [XV[h : h + 1, :] for h in (0, 1)]
    spread_ends(coefs + coefs)
    spread_slots(CPL)

    def face_back(r):
        before = slab(jnp.maximum(r - 1, 0))
        first = lane32 < FSIDE
        own = TCP[:, slab(r)]
        back = pltpu.roll(jnp.where(first, own, TCP[:, before]), FSIDE, 1)
        back = jnp.where(jnp.logical_not(first) | (r > 0), back, 0.0)
        TCM[:, slab(r)] = back
        diag = frac_storage[:, slab(r)] + TAP[:, slab(r)] + TAM[:, slab(r)] + own + back
        diag = diag + S2[pl.ds(r, FR, stride=SLABS), :]
        FD[:, slab(r)] = diag
        INVF[:, slab(r)] = relaxation * inverse(diag)
    loop(SLABS, face_back, UF)

    def smooth_frac(k, source):
        def body(r):
            z = source[:, slab(r)] * INVF[:, slab(r)]
            ZF[k, :, slab(r)] = z
            F2[pl.ds(r, FR, stride=SLABS), :] = z
        loop(SLABS, body, UF)
        pick_slots(PICK)
        sfl[k] = CPL[...] * PICK[...]
        return [send(sfl.at[k], rfl.at[k, d], y_dev[d]) for d in (0, 1)]

    flux_sent = smooth_frac(0, frac_rhs)

    build_hot(0)

    spread_rock(0, CPL, True)

    for copy in slots_sent:
        copy.wait_recv()
    for d in (0, 1):
        IDX[1 + d] = ric[d, 0].astype(jnp.int32)
        build_hot(1 + d)
        spread_rock(1 + d, ric.at[d, 1], False)

    build_aggregates()

    for copy in faces_sent:
        copy.wait_recv()
    open_x = [gx > 0, gx < n_gx - 1]
    open_y = [gy > 0, gy < n_gy - 1]

    def scale_rock(i):
        conduct = perm[i]
        PA[i + 1] = conduct
        PE[i + 1] = conduct * jnp.exp(-0.25 * pressure[i])
    loop(CX, scale_rock, UR)
    for d, plane in enumerate((0, CX + 1)):
        conduct = jnp.where(open_x[d], rx[d, 0], 0.0)
        PA[plane] = conduct
        PE[plane] = conduct * jnp.exp(-0.25 * rx[d, 1])
    for d in (0, 1):
        conduct = jnp.where(open_y[d], ry[d, 0], 0.0)
        ry[d, 0] = conduct
        ry[d, 1] = conduct * jnp.exp(-0.25 * ry[d, 1])

    def below(x, edge):
        return jnp.where(sub16 == 0, edge, pltpu.roll(x, 1, 0))

    def above(x, edge):
        return jnp.where(sub16 == CY - 1, edge, pltpu.roll(x, CY - 1, 0))

    def face(conduct, scaled, near, near_scaled):
        return 2.0 * scaled * near_scaled * inverse(conduct + near)

    VALS[0] = face(perm[:, 0, :], PE[1 : CX + 1, 0, :], ry[0, 0], ry[0, 1])

    def rock_faces(i):
        conduct, scaled = PA[i + 1], PE[i + 1]
        row = pl.ds(i, 1)
        WX[i] = face(conduct, scaled, PA[i], PE[i])
        side = face(conduct, scaled, above(conduct, ry[1, 0, row, :]),
                    above(scaled, ry[1, 1, row, :]))
        WYP[i] = side
        WYM[i] = below(side, VALS[0, row, :])
        up = face(conduct, scaled, pltpu.roll(conduct, 127, 1), pltpu.roll(scaled, 127, 1))
        up = jnp.where(lane16 < NZ - 1, up, 0.0)
        WZP[i] = up
        WZM[i] = pltpu.roll(up, 1, 1)
    loop(CX, rock_faces, UR)
    WX[CX] = face(PA[CX], PE[CX], PA[CX + 1], PE[CX + 1])

    def rock_diagonal(i):
        faces = [WX[i], WX[i + 1], WYM[i], WYP[i], WZM[i], WZP[i]]
        rows = pl.ds(pl.multiple_of(i * CY, CY), CY)
        diag = storage[i] + sum(faces) + DEL[rows, :]
        RD[i] = diag
        INVR[i] = relaxation * inverse(diag)
        mine = agg[i]
        inside = lambda n: jnp.clip(n, 0, CX - 1)
        nears = [
            jnp.where(i > 0, agg[inside(i - 1)], -1),
            jnp.where(i < CX - 1, agg[inside(i + 1)], -1),
            below(mine, -1), above(mine, -1),
            pltpu.roll(mine, 1, 1), pltpu.roll(mine, 127, 1),
        ]
        for face, near in zip(faces, nears):
            diag = diag - jnp.where(near == mine, face, 0.0)
        S[i] = diag
    loop(CX, rock_diagonal, UR)

    coarse_diag = aggregate_sums(S)
    inverse_coarse = 1.0 / jnp.where(lane16 < NAGG, coarse_diag, 1.0)

    def stencil(i, center, low_x, high_x, low_y, high_y):
        out = RD[i] * center
        out = out - WX[i] * low_x - WX[i + 1] * high_x
        out = out - WYM[i] * below(center, low_y) - WYP[i] * above(center, high_y)
        return out - WZM[i] * pltpu.roll(center, 1, 1) - WZP[i] * pltpu.roll(center, 127, 1)

    def send_faces(k):
        for d, row in enumerate((CY - 1, 0)):
            szy[k, d] = Z0[k, 1 : CX + 1, row, :]
        return [
            send(Z0.at[k, CX], Z0.at[k, 0], x_dev[0]),
            send(Z0.at[k, 1], Z0.at[k, CX + 1], x_dev[1]),
        ] + [send(szy.at[k, d], rzy.at[k, d], y_dev[d]) for d in (0, 1)]

    def iterate(k, rock_vec, frac_vec, halo_sent, flux_sent):

        pick_rock(lambda m: Z0[k, m * 8 + 1 : m * 8 + 9].reshape(128, 128),
                  [HV, sans.at[k, 0, 0], sans.at[k, 1, 0]],
                  None if k else [AGS, sans.at[k, 0, 1], sans.at[k, 1, 1]])
        parts = 1 if k else 2
        answers_sent = [
            send(sans.at[k, 1 - d, 0:parts], rans.at[k, d, 0:parts], y_dev[d]) for d in (0, 1)]

        spread_rock(0, sfl.at[k], True)
        for d, copy in enumerate(flux_sent):
            copy.wait_recv()
            spread_rock(1 + d, rfl.at[k, d], False)
        for copy in halo_sent:
            copy.wait_recv()

        def residual(i):
            row = pl.ds(i, 1)
            rows = pl.ds(pl.multiple_of(i * CY, CY), CY)
            image = stencil(i, Z0[k, i + 1], Z0[k, i], Z0[k, i + 2],
                            rzy[k, 0, row, :], rzy[k, 1, row, :]) - DEL[rows, :]
            Q[i] = image
            S[i] = rock_vec[i] - image
        loop(CX, residual, UR)

        coarse = aggregate_sums(S) * inverse_coarse
        scs[k] = coarse[0:8]
        coarse_sent = [send(scs.at[k], rcs.at[k, d], x_dev[d]) for d in (0, 1)]
        coarse_sent += [send(scs.at[k], rcs.at[k, 2 + d], y_dev[d]) for d in (0, 1)]

        values = pick_ends()
        coefs = [XV[h : h + 1, :] for h in (0, 1)]
        spread_ends([coefs[h] * values[2 * (1 - e) + h] for e, h in ends])

        def correct(i):
            E[k, i + 1] = lanes_of(coarse, agg[i])
        loop(CX, correct, UR)

        def frac_faces(r):
            here = slab(r)
            z = ZF[k, :, here]
            before = ZF[k, :, slab(jnp.maximum(r - 1, 0))]
            after = ZF[k, :, slab(jnp.minimum(r + 1, SLABS - 1))]
            first = lane32 < FSIDE
            down = pltpu.roll(jnp.where(first, after, z), FSIDE, 1)
            up = pltpu.roll(jnp.where(first, z, before), FSIDE, 1)
            image = FD[:, here] * z
            image = image - TAP[:, here] * pltpu.roll(z, 127, 1) - TAM[:, here] * pltpu.roll(z, 1, 1)
            image = image - TCP[:, here] * down - TCM[:, here] * up
            FI[:, here] = image - relaxation * frac_vec[:, here]
        loop(SLABS, frac_faces, UF)

        for copy in answers_sent + coarse_sent:
            copy.wait_recv()
        if k == 0:
            AGS[...] = AGS[...] + rans[0, 0, 1] + rans[0, 1, 1]
        tables = [jnp.concatenate([rcs[k, d], rcs[k, d]], axis=0) for d in range(4)]
        for d, plane in enumerate((0, CX + 1)):
            E[k, plane] = lanes_of(tables[d], rx[d, 2].astype(jnp.int32))
        for d in (0, 1):
            table = jnp.concatenate([tables[2 + d]] * 2, axis=0)
            VALS[d] = lanes_of(table, ry[d, 2].astype(jnp.int32))
        slot_agg = AGS[...].astype(jnp.int32)
        four = [jnp.concatenate([t] * 2, axis=0) for t in (coarse, tables[2], tables[3])]
        own, low, high = [lanes_of(t, slot_agg) for t in four]
        where = OFF[...]
        host = HV[...] + rans[k, 0, 0] + rans[k, 1, 0]
        host = host + jnp.where(where == 0, own, jnp.where(where < 0, low, high))
        VALS[2] = CPL[...] * host

        zero = jnp.zeros((8, 128), f32)

        def products(x, v, b):
            if k == 0:
                return fold(v * v), fold(x * v), fold(x * x)
            return fold(x * b), fold(x * v), fold(x * x)

        def rock_image(i, accs):
            row = pl.ds(i, 1)
            vec = rock_vec[i]
            image = Q[i] + stencil(i, E[k, i + 1], E[k, i], E[k, i + 2],
                                   VALS[0, row, :], VALS[1, row, :])
            image = image - relaxation * vec
            if k == 0:
                W1R[i] = image
                Z0[1, i + 1] = image * INVR[i]
            return tuple(a + p for a, p in zip(accs, products(image, vec, rock_rhs[i])))
        accs = lax.fori_loop(0, CX, rock_image, (zero,) * 3, unroll=UR)
        halo_sent = send_faces(1) if k == 0 else None

        spread_slots(VALS.at[2])

        def frac_image(r, accs):
            here = slab(r)
            vec = frac_vec[:, here]
            image = FI[:, here] - S2[pl.ds(r, FR, stride=SLABS), :]
            if k == 0:
                W1F[:, here] = image
            return tuple(a + p for a, p in zip(accs, products(image, vec, frac_rhs[:, here])))
        accs = lax.fori_loop(0, SLABS, frac_image, accs, unroll=UF)
        return list(accs), halo_sent

    def smooth_rock(i):
        Z0[0, i + 1] = rock_rhs[i] * INVR[i]
    loop(CX, smooth_rock, UR)
    dots, halo_sent = iterate(0, rock_rhs, frac_rhs, send_faces(0), flux_sent)

    flux_sent = smooth_frac(1, W1F)
    dots += iterate(1, W1R, W1F, halo_sent, flux_sent)[0]

    tile = jnp.zeros((8, 128), f32)
    for n, part in enumerate(dots):
        tile = jnp.where(sub8 == n, jnp.sum(part, axis=0, keepdims=True), tile)
    groups = [(AR0, gx, gx_peers, n_gx), (AR1, my_y, y_peers, n_y), (AR2, my_z, z_peers, n_z)]
    for slots, me, peers, size in groups:
        slots[pl.ds(me, 1)] = tile[None]
        copies = [send(slots.at[me], slots.at[me], device) for device in peers]
        for copy in copies:
            copy.wait_recv()
        tile = sum(slots[n] for n in range(size))
    tile = jnp.sum(tile, axis=1, keepdims=True)
    bb, pb, pp, qb, qp, qq = [tile[n : n + 1, :] for n in range(6)]
    gram = [[bb, pb, qb], [pb, pp, qp], [qb, qp, qq]]
    shift = relaxation

    def inner(a, c):
        return sum(a[m] * c[n] * gram[m][n] for m in range(3) for n in range(3))

    one, none = jnp.ones((1, 1), f32), jnp.zeros((1, 1), f32)
    start_norm = jnp.sqrt(bb + epsilon)
    v0 = [one / start_norm, none, none]
    image = [shift * v0[0], v0[0], none]
    rest0 = inner(image, image)
    h00 = inner(image, v0)
    image = [a - h00 * c for a, c in zip(image, v0)]
    h10 = jnp.sqrt(jnp.maximum(inner(image, image), 0.0) + epsilon)
    v1 = [a / h10 for a in image]
    image = [shift * v1[0], v1[0] + shift * v1[1], v1[1]]
    h01, h11 = inner(image, v0), inner(image, v1)
    image = [a - h01 * c - h11 * d for a, c, d in zip(image, v0, v1)]
    h21 = jnp.sqrt(jnp.maximum(inner(image, image), 0.0) + epsilon)

    radius = jnp.sqrt(h00 * h00 + h10 * h10)
    cosine, sine = h00 / radius, h10 / radius
    upper01 = cosine * h01 + sine * h11
    lower = cosine * h11 - sine * h01
    right0, right1 = cosine * start_norm, -sine * start_norm
    radius1 = jnp.sqrt(lower * lower + h21 * h21)
    cosine1, sine1 = lower / radius1, h21 / radius1
    res_out[...] = jnp.abs(-sine1 * right1)
    y1 = cosine1 * right1 / radius1
    y0 = (right0 - upper01 * y1) / radius
    on_b = y0 * v0[0] + y1 * v1[0]
    on_p = y1 * v1[1]

    def rock_update(i):
        rock_out[i] = on_b * (Z0[0, i + 1] + E[0, i + 1]) + on_p * (Z0[1, i + 1] + E[1, i + 1])
    loop(CX, rock_update, UR)

    def frac_update(r):
        frac_out[:, slab(r)] = on_b * ZF[0, :, slab(r)] + on_p * ZF[1, :, slab(r)]
    loop(SLABS, frac_update, UF)
    for copy in started:
        copy.wait_send()

def local(sizes, rock_rhs, frac_rhs, perm, storage, pressure, frac_perm, frac_storage,
          frac_pressure, couple_geom, couple_count, couple_frac_cell, couple_rock_cell,
          host_offset, cross_pairs, cross_geom, aggregates):
    n_gx, n_y, n_z = sizes
    vmem = pl.BlockSpec(memory_space=pltpu.VMEM)
    smem = pl.BlockSpec(memory_space=pltpu.SMEM)
    in_specs = [vmem] * 16
    in_specs[9] = in_specs[12] = smem
    block = (CX, CY, NZ)
    tall = (CX + 2, CY, NZ)
    frac = (FR, FCELLS)
    slot = (FR, KC)

    def mem(*shape, kind=f32):
        return pltpu.VMEM(shape, kind)

    scratch = [
        mem(2, *tall), mem(2, *tall), mem(*tall), mem(*tall), mem(CX + 1, CY, NZ),
        *[mem(*block) for _ in range(9)], mem(ROWS, 128),
        *[mem(*frac) for _ in range(7)], mem(2, *frac), mem(FR * SLABS, 128), mem(FR * SLABS, 128),
        mem(3, ROWS, FR * KC, kind=bf16),
        mem(256, FR * KC, kind=bf16), mem(384, ROWS, kind=bf16), mem(256, FR * SLABS, kind=bf16),
        mem(FR, 128, 128, kind=bf16), mem(FR * SLABS, 2 * CROSS, kind=bf16),
        mem(256, 2 * CROSS, kind=bf16), mem(128, 4096, kind=bf16), mem(256, 4096, kind=bf16),
        mem(256, 128, kind=bf16), mem(*frac), mem(8, 128),
        mem(3, *slot, kind=jnp.int32), mem(*slot, kind=jnp.int32),
        mem(*slot), mem(*slot), mem(*slot), mem(*slot), mem(3, *slot),
        mem(2, 3, CY, NZ), mem(2, 3, CY, NZ), mem(2, 3, CX, NZ), mem(2, 3, CX, NZ),
        mem(2, 2, *slot), mem(2, 2, *slot),
        mem(2, 2, CX, NZ), mem(2, 2, CX, NZ), mem(2, *slot), mem(2, 2, *slot),
        mem(2, 2, 2, *slot), mem(2, 2, 2, *slot), mem(2, 8, 128), mem(2, 4, 8, 128),
        mem(n_gx, 8, 128), mem(n_y, 8, 128), mem(n_z, 8, 128),
        pltpu.SemaphoreType.DMA((64,)), pltpu.SemaphoreType.DMA((64,)),
    ]
    rock, fracs, norm = pl.pallas_call(
        functools.partial(kernel, sizes),
        out_shape=(
            jax.ShapeDtypeStruct(block, f32),
            jax.ShapeDtypeStruct(frac, f32),
            jax.ShapeDtypeStruct((1, 1), f32),
        ),
        in_specs=in_specs,
        out_specs=(vmem, vmem, vmem),
        scratch_shapes=scratch,
        compiler_params=pltpu.CompilerParams(
            collective_id=0, has_side_effects=True, vmem_limit_bytes=60 * 1024 * 1024),
    )(rock_rhs, frac_rhs, perm, storage, pressure, frac_perm, frac_storage, frac_pressure,
      couple_geom, couple_count, couple_frac_cell, couple_rock_cell, host_offset, cross_pairs,
      cross_geom.reshape(1, CROSS), aggregates)
    return rock, fracs, norm[0, 0]

def solution(mesh):
    n_gx, n_gy = mesh.shape["gx"], mesh.shape["gy"]
    n_z = 8 if n_gy % 8 == 0 else 2
    grid = P("gx", "gy", None)
    owned = P(("gx", "gy"), None)
    flat = P(("gx", "gy"))
    in_specs = (grid, owned, grid, grid, grid, owned, owned, owned, owned, flat, owned, owned,
                flat, P(None, ("gx", "gy")), flat, grid)
    return jax.shard_map(
        functools.partial(local, (n_gx, n_gy // n_z, n_z)), mesh=mesh, in_specs=in_specs,
        out_specs=(grid, owned, P()), check_vma=False)
```

```python
import functools

import jax
import jax.numpy as jnp
from jax import lax
from jax.experimental import pallas as pl
from jax.experimental.pallas import tpu as pltpu
from jax.sharding import PartitionSpec as P

CX, CY, NZ = 32, 16, 128
FR, FCELLS, FSIDE, KC = 32, 4096, 64, 128
SLABS = FCELLS // 128
NAGG = 64
ROWS = CX * CY
CROSS = 256
relaxation = 0.8
epsilon = 1e-06
MESH = pl.DeviceIdType.MESH
UB, UF, UR = 32, 32, 32
f32 = jnp.float32
bf16 = jnp.bfloat16


def iota(shape, dim):
    return lax.broadcasted_iota(jnp.int32, shape, dim)


def loop(count, body, unroll=1):
    lax.fori_loop(0, count, lambda i, c: (body(i), c)[1], 0, unroll=unroll)


def halves(x):
    high = x.astype(bf16)
    return high, (x - high.astype(f32)).astype(bf16)


def nt_dot(a, b):
    return lax.dot_general(a, b, (((1,), (1,)), ((), ())), preferred_element_type=f32)


def inverse(x):
    guess = pl.reciprocal(x, approx=True)
    guess = guess * (2.0 - x * guess)
    return guess * (2.0 - x * guess)


def lanes_of(table, index):
    return jnp.take_along_axis(table, index, axis=1)


def kernel(
    sizes,
    rock_rhs_in, frac_rhs_in, perm_in, storage_in, pressure_in, frac_perm_in, frac_storage_in,
    frac_pressure_in, geom, count, frac_cell, rock_cell, offset, pairs, cross_geom, agg_in,
    rock_out, frac_out, res_out,
    Z0, E, PA, PE, WX, WYM, WYP, WZM, WZP, RD, INVR, W1R, Q, S, DEL,
    FD, INVF, TAP, TAM, TCP, TCM, W1F, ZF, F2, S2,
    U, LV, TT, TF, BF, XU, LVX, AX, AY, AG, FI, XV, IDX, OFF, CPL, PICK, HV, AGS, VALS,
    sx, rx, sy, ry, sic, ric, szy, rzy, sfl, rfl, sans, rans, scs, rcs,
    AR0, AR1, AR2, rock_rhs, frac_rhs, perm, storage, pressure, frac_perm, frac_storage,
    frac_pressure, agg, send_sem, recv_sem, load_sem,
):
    n_gx, n_y, n_z = sizes
    n_gy = n_y * n_z
    gx = lax.axis_index("gx")
    gy = lax.axis_index("gy")
    my_y, my_z = gy // n_z, gy % n_z
    x_dev = [((gx + 1) % n_gx, gy), ((gx + n_gx - 1) % n_gx, gy)]
    y_dev = [(gx, (gy + 1) % n_gy), (gx, (gy + n_gy - 1) % n_gy)]
    gx_peers = [((gx + p) % n_gx, gy) for p in range(1, n_gx)]
    y_peers = [(gx, (my_y + p) % n_y * n_z + my_z) for p in range(1, n_y)]
    z_peers = [(gx, my_y * n_z + (my_z + p) % n_z) for p in range(1, n_z)]

    loads = [
        pltpu.make_async_copy(src, dst, load_sem.at[n])
        for n, (src, dst) in enumerate((
            (frac_pressure_in, frac_pressure), (perm_in, perm), (pressure_in, pressure),
            (agg_in, agg), (frac_perm_in, frac_perm), (frac_storage_in, frac_storage),
            (frac_rhs_in, frac_rhs), (storage_in, storage), (rock_rhs_in, rock_rhs)))
    ]
    for copy in loads:
        copy.start()

    barrier = pltpu.get_barrier_semaphore()
    everyone = gx_peers + y_peers + z_peers + y_dev
    for device in everyone:
        pl.semaphore_signal(barrier, inc=1, device_id=device, device_id_type=MESH)

    started = []

    def send(src, dst, device):
        number = len(started)
        copy = pltpu.make_async_remote_copy(
            src_ref=src, dst_ref=dst, send_sem=send_sem.at[number],
            recv_sem=recv_sem.at[number], device_id=device, device_id_type=MESH,
        )
        copy.start()
        started.append(copy)
        return copy

    sub8 = iota((8, 128), 0)
    sub16 = iota((16, 128), 0)
    sub32 = iota((32, 128), 0)
    sub128 = iota((128, 128), 0)
    lane16 = iota((16, 128), 1)
    lane32 = iota((32, 128), 1)
    row_lane = iota((1, 128), 1)
    short_rows = iota((ROWS, 128), 0).astype(jnp.int16)

    def to_table(get):
        def body(r):
            F2[pl.ds(r, FR, stride=SLABS), :] = get(r)
        loop(SLABS, body, 2)

    def slab(r):
        return pl.ds(pl.multiple_of(r * 128, 128), 128)

    def pick_slots(out):
        def body(f):
            cell = frac_cell[pl.ds(f, 1), :]
            table = F2[pl.ds(pl.multiple_of(f * SLABS, SLABS), SLABS), :]
            got = lanes_of(table, jnp.broadcast_to(cell & 127, (SLABS, 128)))
            out[pl.ds(f, 1), :] = jnp.sum(
                jnp.where(sub32 == cell >> 7, got, 0.0), axis=0, keepdims=True)
        loop(FR, body, 32)

    ends = [(e, h) for e in (0, 1) for h in (0, 1)]

    def end_cells(e, h):
        return pairs[e : e + 1, h * 128 : (h + 1) * 128]

    def turn(get, blocks, out, exact=False):
        for m in range(blocks):
            block = get(m).T
            if exact:
                out[0:128, m * 128 : (m + 1) * 128] = block.astype(bf16)
            else:
                high, low = halves(block)
                out[0:128, m * 128 : (m + 1) * 128] = high
                out[128:256, m * 128 : (m + 1) * 128] = low

    def pick_ends():
        turn(lambda m: F2[m * 128 : (m + 1) * 128, :], 8, TF)
        got = jnp.dot(TF[...], XU[...], preferred_element_type=f32)
        got = got[0:128] + got[128:256]
        return [
            jnp.sum(jnp.where(sub128 == (end_cells(e, h) & 127),
                              got[:, n * 128 : (n + 1) * 128], 0.0), axis=0, keepdims=True)
            for n, (e, h) in enumerate(ends)
        ]

    def spread_ends(end_vals):
        for n, (e, h) in enumerate(ends):
            hot = sub128 == (end_cells(e, h) & 127)
            high = end_vals[n].astype(bf16).astype(f32)
            low = end_vals[n] - high
            LVX[0:128, n * 128 : (n + 1) * 128] = jnp.where(hot, high, 0.0).astype(bf16)
            LVX[128:256, n * 128 : (n + 1) * 128] = jnp.where(hot, low, 0.0).astype(bf16)
        part = nt_dot(XU[...], LVX[...])
        S2[...] = part[:, :128] + part[:, 128:]

    def spread_slots(slot_vals):
        def body(f):
            cell = frac_cell[pl.ds(f, 1), :]
            high, low = halves(jnp.where(sub32 == cell >> 7, slot_vals[pl.ds(f, 1), :], 0.0))
            part = nt_dot(jnp.concatenate([high, low], axis=0), BF[f])
            rows = pl.ds(pl.multiple_of(f * SLABS, SLABS), SLABS)
            S2[rows, :] = S2[rows, :] + part[:32] + part[32:]
        loop(FR, body, FR)

    def build_hot(src):
        def body(f):
            cell = jnp.broadcast_to(IDX[src, pl.ds(f, 1), :], (16, 128))
            high = jnp.concatenate([(cell >> 7).astype(jnp.int16)] * 32, axis=0)
            U[src, :, slab(f)] = jnp.where(short_rows == high, bf16(1), bf16(0))
        loop(FR, body, UB)

    def spread_rock(src, vals, first):
        def body(f):
            value = vals[pl.ds(f, 1), :]
            high = value.astype(bf16).astype(f32)
            cell = jnp.broadcast_to(IDX[src, pl.ds(f, 1), :] & 127, (16, 128))
            hot = short_rows[:128] == jnp.concatenate([cell.astype(jnp.int16)] * 8, axis=0)
            for m, part in enumerate((high, value - high)):
                part = jnp.broadcast_to(part, (16, 128)).astype(bf16)
                part = jnp.concatenate([part] * 8, axis=0)
                LV[src, m * 128 : m * 128 + 128, slab(f)] = jnp.where(hot, part, bf16(0))
        loop(FR, body, FR)
        part = nt_dot(U[src], LV[src])
        total = part[:, :128] + part[:, 128:]
        DEL[...] = total if first else DEL[...] + total

    def turn_rock(get, with_agg):
        turn(get, 4, TT)
        if with_agg:
            for m in range(4):
                block = agg[m * 8 : m * 8 + 8].astype(f32).reshape(128, 128).T
                TT[256:384, m * 128 : (m + 1) * 128] = block.astype(bf16)

    def pick_rock(outs, agg_outs):
        table = TT[...] if agg_outs else TT[0:256]
        for src in outs:
            got = jnp.dot(table, U[src], preferred_element_type=f32)
            for f in range(FR):
                row, here = slice(f, f + 1), slice(f * 128, f * 128 + 128)
                hot = sub128 == IDX[src, row, :] & 127
                value = got[0:128, here] + got[128:256, here]
                outs[src][row, :] = jnp.sum(jnp.where(hot, value, 0.0), axis=0, keepdims=True)
                if agg_outs:
                    agg_outs[src][row, :] = jnp.sum(
                        jnp.where(hot, got[256:384, here], 0.0), axis=0, keepdims=True)

    def agg_cells(b, h):
        cells = agg[2 * b + h]
        return cells, pl.ds(pl.multiple_of(b * 256 + h * 128, 128), 128)

    def build_aggregates():
        def body(b):
            for h in (0, 1):
                cells, here = agg_cells(b, h)
                cells = (cells & 15).astype(jnp.int16)
                for a in range(16):
                    AY[a * 16 : a * 16 + 16, here] = jnp.where(
                        cells == jnp.int16(a), bf16(1), bf16(0))
        loop(16, body, 2)
        place = iota((256, 128), 0) >> 4 == iota((256, 128), 1) & 15
        AG[...] = place.astype(f32).astype(bf16)

    def aggregate_sums(src):
        def body(b):
            for h in (0, 1):
                cells, here = agg_cells(b, h)
                cells = cells >> 4
                value = src[2 * b + h]
                high = value.astype(bf16).astype(f32)
                low = value - high
                for a in range(4):
                    AX[a * 32 : a * 32 + 16, here] = jnp.where(cells == a, high, 0.0).astype(bf16)
                    AX[a * 32 + 16 : a * 32 + 32, here] = jnp.where(cells == a, low, 0.0).astype(bf16)
        loop(16, body, 16)
        part = nt_dot(AX[...], AY[...])
        part = jnp.where(iota((128, 256), 0) & 15 == iota((128, 256), 1) & 15, part, 0.0)
        rest = jnp.concatenate([fold(part[a * 32 : a * 32 + 32]) for a in range(4)], axis=0)
        pieces = []
        for _ in range(3):
            pieces.append(rest.astype(bf16))
            rest = rest - pieces[-1].astype(f32)
        total = jnp.dot(jnp.concatenate(pieces, axis=0), AG[...], preferred_element_type=f32)
        total = total[0:32] + total[32:64] + total[64:96]
        total = jnp.where(sub32 >> 3 == lane32 >> 4, total, 0.0)
        return jnp.broadcast_to(jnp.sum(total, axis=0, keepdims=True), (16, 128))

    def fold(x):
        return sum(x[j : j + 8] for j in range(0, x.shape[0], 8))

    loads[0].wait()
    to_table(lambda r: frac_pressure[:, slab(r)])
    pick_slots(PICK)

    def split_slots(f):
        where = offset[f]
        row = pl.ds(f, 1)
        OFF[row, :] = jnp.full((1, 128), where, jnp.int32)
        cell = rock_cell[row, :]
        live = row_lane < count[f]
        IDX[0, row, :] = jnp.where(live & (where == 0), cell, -1)
        sic[0, 0, row, :] = jnp.where(live & (where == 1), cell, -1).astype(f32)
        sic[1, 0, row, :] = jnp.where(live & (where == -1), cell, -1).astype(f32)
        value = jnp.where(live, geom[row, :] * jnp.exp(-0.5 * PICK[row, :]), 0.0)
        CPL[row, :] = value
    loop(FR, split_slots, 4)
    sic[0, 1] = CPL[...]
    sic[1, 1] = CPL[...]

    for copy in loads[1:4]:
        copy.wait()
    for d, plane in enumerate((CX - 1, 0)):
        sx[d, 0] = perm[plane]
        sx[d, 1] = pressure[plane]
        sx[d, 2] = agg[plane].astype(f32)
    for d, row in enumerate((CY - 1, 0)):
        sy[d, 0] = perm[:, row, :]
        sy[d, 1] = pressure[:, row, :]
        sy[d, 2] = agg[:, row, :].astype(f32)

    pl.semaphore_wait(barrier, len(everyone))
    slots_sent = [send(sic.at[d], ric.at[d], y_dev[d]) for d in (0, 1)]
    faces_sent = [send(sx.at[d], rx.at[d], x_dev[d]) for d in (0, 1)]
    faces_sent += [send(sy.at[d], ry.at[d], y_dev[d]) for d in (0, 1)]

    for copy in loads[4:]:
        copy.wait()

    def scale_frac(r):
        press = frac_pressure[:, slab(r)]
        TCM[:, slab(r)] = frac_perm[:, slab(r)] * jnp.exp(-0.25 * press)
    loop(SLABS, scale_frac, UF)

    def face_along(r):
        conduct, scaled = frac_perm[:, slab(r)], TCM[:, slab(r)]
        near, near_scaled = pltpu.roll(conduct, 127, 1), pltpu.roll(scaled, 127, 1)
        weight = 2.0 * scaled * near_scaled * inverse(conduct + near)
        weight = jnp.where(lane32 & (FSIDE - 1) < FSIDE - 1, weight, 0.0)
        TAP[:, slab(r)] = weight
        TAM[:, slab(r)] = pltpu.roll(weight, 1, 1)
        after = slab(jnp.minimum(r + 1, SLABS - 1))
        first = lane32 < FSIDE
        near = pltpu.roll(jnp.where(first, frac_perm[:, after], conduct), FSIDE, 1)
        near_scaled = pltpu.roll(jnp.where(first, TCM[:, after], scaled), FSIDE, 1)
        weight = 2.0 * scaled * near_scaled * inverse(conduct + near)
        TCP[:, slab(r)] = jnp.where(first | (r < SLABS - 1), weight, 0.0)
    loop(SLABS, face_along, UF)

    for n, (e, h) in enumerate(ends):
        for m in range(8):
            hot = (sub128 + m * 128 == end_cells(e, h) >> 7).astype(f32).astype(bf16)
            XU[m * 128 : (m + 1) * 128, n * 128 : (n + 1) * 128] = hot
    pressures = pick_ends()
    for h in (0, 1):
        XV[h : h + 1, :] = cross_geom[0:1, h * 128 : (h + 1) * 128] * jnp.exp(
            -0.25 * (pressures[h] + pressures[h + 2]))

    def build_lanes(f):
        BF[f] = (sub128 == (frac_cell[pl.ds(f, 1), :] & 127)).astype(f32).astype(bf16)
    loop(FR, build_lanes, 2)
    coefs = [XV[h : h + 1, :] for h in (0, 1)]
    spread_ends(coefs + coefs)
    spread_slots(CPL)

    def face_back(r):
        before = slab(jnp.maximum(r - 1, 0))
        first = lane32 < FSIDE
        own = TCP[:, slab(r)]
        back = pltpu.roll(jnp.where(first, own, TCP[:, before]), FSIDE, 1)
        back = jnp.where(jnp.logical_not(first) | (r > 0), back, 0.0)
        TCM[:, slab(r)] = back
        diag = frac_storage[:, slab(r)] + TAP[:, slab(r)] + TAM[:, slab(r)] + own + back
        diag = diag + S2[pl.ds(r, FR, stride=SLABS), :]
        FD[:, slab(r)] = diag
        INVF[:, slab(r)] = relaxation * inverse(diag)
    loop(SLABS, face_back, UF)

    def smooth_frac(k, source):
        def body(r):
            z = source[:, slab(r)] * INVF[:, slab(r)]
            ZF[k, :, slab(r)] = z
            F2[pl.ds(r, FR, stride=SLABS), :] = z
        loop(SLABS, body, UF)
        pick_slots(PICK)
        sfl[k] = CPL[...] * PICK[...]
        return [send(sfl.at[k], rfl.at[k, d], y_dev[d]) for d in (0, 1)]

    flux_sent = smooth_frac(0, frac_rhs)

    build_hot(0)
    spread_rock(0, CPL, True)
    for copy in slots_sent:
        copy.wait_recv()
    for d in (0, 1):
        IDX[1 + d] = ric[d, 0].astype(jnp.int32)
        build_hot(1 + d)
        spread_rock(1 + d, ric.at[d, 1], False)
    build_aggregates()
    for copy in faces_sent:
        copy.wait_recv()
    open_x = [gx > 0, gx < n_gx - 1]
    open_y = [gy > 0, gy < n_gy - 1]

    def scale_rock(i):
        conduct = perm[i]
        PA[i + 1] = conduct
        PE[i + 1] = conduct * jnp.exp(-0.25 * pressure[i])
    loop(CX, scale_rock, UR)
    for d, plane in enumerate((0, CX + 1)):
        conduct = jnp.where(open_x[d], rx[d, 0], 0.0)
        PA[plane] = conduct
        PE[plane] = conduct * jnp.exp(-0.25 * rx[d, 1])
    for d in (0, 1):
        conduct = jnp.where(open_y[d], ry[d, 0], 0.0)
        ry[d, 0] = conduct
        ry[d, 1] = conduct * jnp.exp(-0.25 * ry[d, 1])

    def below(x, edge):
        return jnp.where(sub16 == 0, edge, pltpu.roll(x, 1, 0))

    def above(x, edge):
        return jnp.where(sub16 == CY - 1, edge, pltpu.roll(x, CY - 1, 0))

    def face(conduct, scaled, near, near_scaled):
        return 2.0 * scaled * near_scaled * inverse(conduct + near)

    VALS[0] = face(perm[:, 0, :], PE[1 : CX + 1, 0, :], ry[0, 0], ry[0, 1])

    def rock_faces(i):
        conduct, scaled = PA[i + 1], PE[i + 1]
        row = pl.ds(i, 1)
        WX[i] = face(conduct, scaled, PA[i], PE[i])
        side = face(conduct, scaled, above(conduct, ry[1, 0, row, :]),
                    above(scaled, ry[1, 1, row, :]))
        WYP[i] = side
        WYM[i] = below(side, VALS[0, row, :])
        up = face(conduct, scaled, pltpu.roll(conduct, 127, 1), pltpu.roll(scaled, 127, 1))
        up = jnp.where(lane16 < NZ - 1, up, 0.0)
        WZP[i] = up
        WZM[i] = pltpu.roll(up, 1, 1)
    loop(CX, rock_faces, UR)
    WX[CX] = face(PA[CX], PE[CX], PA[CX + 1], PE[CX + 1])

    def rock_diagonal(i):
        faces = [WX[i], WX[i + 1], WYM[i], WYP[i], WZM[i], WZP[i]]
        rows = pl.ds(pl.multiple_of(i * CY, CY), CY)
        diag = storage[i] + sum(faces) + DEL[rows, :]
        RD[i] = diag
        INVR[i] = relaxation * inverse(diag)
        mine = agg[i]
        inside = lambda n: jnp.clip(n, 0, CX - 1)
        nears = [
            jnp.where(i > 0, agg[inside(i - 1)], -1),
            jnp.where(i < CX - 1, agg[inside(i + 1)], -1),
            below(mine, -1), above(mine, -1),
            pltpu.roll(mine, 1, 1), pltpu.roll(mine, 127, 1),
        ]
        for face, near in zip(faces, nears):
            diag = diag - jnp.where(near == mine, face, 0.0)
        S[i] = diag
    loop(CX, rock_diagonal, UR)
    coarse_diag = aggregate_sums(S)
    inverse_coarse = 1.0 / jnp.where(lane16 < NAGG, coarse_diag, 1.0)

    def stencil(i, center, low_x, high_x, low_y, high_y):
        out = RD[i] * center
        out = out - WX[i] * low_x - WX[i + 1] * high_x
        out = out - WYM[i] * below(center, low_y) - WYP[i] * above(center, high_y)
        return out - WZM[i] * pltpu.roll(center, 1, 1) - WZP[i] * pltpu.roll(center, 127, 1)

    def send_faces(k):
        for d, row in enumerate((CY - 1, 0)):
            szy[k, d] = Z0[k, 1 : CX + 1, row, :]
        return [
            send(Z0.at[k, CX], Z0.at[k, 0], x_dev[0]),
            send(Z0.at[k, 1], Z0.at[k, CX + 1], x_dev[1]),
        ] + [send(szy.at[k, d], rzy.at[k, d], y_dev[d]) for d in (0, 1)]

    def iterate(k, rock_vec, frac_vec, halo_sent, flux_sent):
        turn_rock(lambda m: Z0[k, m * 8 + 1 : m * 8 + 9].reshape(128, 128), k == 0)
        pick_rock({1: sans.at[k, 0, 0], 2: sans.at[k, 1, 0]},
                  None if k else {1: sans.at[k, 0, 1], 2: sans.at[k, 1, 1]})
        parts = 1 if k else 2
        answers_sent = [
            send(sans.at[k, 1 - d, 0:parts], rans.at[k, d, 0:parts], y_dev[d]) for d in (0, 1)]
        spread_rock(0, sfl.at[k], True)
        for copy in flux_sent:
            copy.wait_recv()
        for d in (0, 1):
            spread_rock(1 + d, rfl.at[k, d], False)
        for copy in halo_sent:
            copy.wait_recv()

        def residual(i):
            row = pl.ds(i, 1)
            rows = pl.ds(pl.multiple_of(i * CY, CY), CY)
            image = stencil(i, Z0[k, i + 1], Z0[k, i], Z0[k, i + 2],
                            rzy[k, 0, row, :], rzy[k, 1, row, :]) - DEL[rows, :]
            Q[i] = image
            S[i] = rock_vec[i] - image
        loop(CX, residual, UR)
        coarse = aggregate_sums(S) * inverse_coarse
        scs[k] = coarse[0:8]
        coarse_sent = [send(scs.at[k], rcs.at[k, d], x_dev[d]) for d in (0, 1)]
        coarse_sent += [send(scs.at[k], rcs.at[k, 2 + d], y_dev[d]) for d in (0, 1)]

        pick_rock({0: HV}, None if k else {0: AGS})
        values = pick_ends()
        coefs = [XV[h : h + 1, :] for h in (0, 1)]
        spread_ends([coefs[h] * values[2 * (1 - e) + h] for e, h in ends])

        def correct(i):
            E[k, i + 1] = lanes_of(coarse, agg[i])
        loop(CX, correct, UR)

        def frac_faces(r):
            here = slab(r)
            z = ZF[k, :, here]
            before = ZF[k, :, slab(jnp.maximum(r - 1, 0))]
            after = ZF[k, :, slab(jnp.minimum(r + 1, SLABS - 1))]
            first = lane32 < FSIDE
            down = pltpu.roll(jnp.where(first, after, z), FSIDE, 1)
            up = pltpu.roll(jnp.where(first, z, before), FSIDE, 1)
            image = FD[:, here] * z
            image = image - TAP[:, here] * pltpu.roll(z, 127, 1) - TAM[:, here] * pltpu.roll(z, 1, 1)
            image = image - TCP[:, here] * down - TCM[:, here] * up
            FI[:, here] = image - relaxation * frac_vec[:, here]
        loop(SLABS, frac_faces, UF)
        for copy in answers_sent + coarse_sent:
            copy.wait_recv()
        if k == 0:
            AGS[...] = AGS[...] + rans[0, 0, 1] + rans[0, 1, 1]
        tables = [jnp.concatenate([rcs[k, d], rcs[k, d]], axis=0) for d in range(4)]
        for d, plane in enumerate((0, CX + 1)):
            E[k, plane] = lanes_of(tables[d], rx[d, 2].astype(jnp.int32))
        for d in (0, 1):
            table = jnp.concatenate([tables[2 + d]] * 2, axis=0)
            VALS[d] = lanes_of(table, ry[d, 2].astype(jnp.int32))
        slot_agg = AGS[...].astype(jnp.int32)
        four = [jnp.concatenate([t] * 2, axis=0) for t in (coarse, tables[2], tables[3])]
        own, low, high = [lanes_of(t, slot_agg) for t in four]
        where = OFF[...]
        host = HV[...] + rans[k, 0, 0] + rans[k, 1, 0]
        host = host + jnp.where(where == 0, own, jnp.where(where < 0, low, high))
        VALS[2] = CPL[...] * host

        zero = jnp.zeros((8, 128), f32)

        def products(x, v, b):
            if k == 0:
                return fold(v * v), fold(x * v), fold(x * x)
            return fold(x * b), fold(x * v), fold(x * x)

        def rock_image(i, accs):
            row = pl.ds(i, 1)
            vec = rock_vec[i]
            image = Q[i] + stencil(i, E[k, i + 1], E[k, i], E[k, i + 2],
                                   VALS[0, row, :], VALS[1, row, :])
            image = image - relaxation * vec
            if k == 0:
                W1R[i] = image
                Z0[1, i + 1] = image * INVR[i]
            return tuple(a + p for a, p in zip(accs, products(image, vec, rock_rhs[i])))
        accs = lax.fori_loop(0, CX, rock_image, (zero,) * 3, unroll=UR)
        halo_sent = send_faces(1) if k == 0 else None
        spread_slots(VALS.at[2])

        def frac_image(r, accs):
            here = slab(r)
            vec = frac_vec[:, here]
            image = FI[:, here] - S2[pl.ds(r, FR, stride=SLABS), :]
            if k == 0:
                W1F[:, here] = image
            return tuple(a + p for a, p in zip(accs, products(image, vec, frac_rhs[:, here])))
        accs = lax.fori_loop(0, SLABS, frac_image, accs, unroll=UF)
        return list(accs), halo_sent

    def smooth_rock(i):
        Z0[0, i + 1] = rock_rhs[i] * INVR[i]
    loop(CX, smooth_rock, UR)
    dots, halo_sent = iterate(0, rock_rhs, frac_rhs, send_faces(0), flux_sent)
    flux_sent = smooth_frac(1, W1F)
    dots += iterate(1, W1R, W1F, halo_sent, flux_sent)[0]

    tile = jnp.zeros((8, 128), f32)
    for n, part in enumerate(dots):
        tile = jnp.where(sub8 == n, jnp.sum(part, axis=0, keepdims=True), tile)
    groups = [(AR0, gx, gx_peers, n_gx), (AR1, my_y, y_peers, n_y), (AR2, my_z, z_peers, n_z)]
    for slots, me, peers, size in groups:
        slots[pl.ds(me, 1)] = tile[None]
        copies = [send(slots.at[me], slots.at[me], device) for device in peers]
        for copy in copies:
            copy.wait_recv()
        tile = sum(slots[n] for n in range(size))
    tile = jnp.sum(tile, axis=1, keepdims=True)
    bb, pb, pp, qb, qp, qq = [tile[n : n + 1, :] for n in range(6)]
    gram = [[bb, pb, qb], [pb, pp, qp], [qb, qp, qq]]
    shift = relaxation

    def inner(a, c):
        return sum(a[m] * c[n] * gram[m][n] for m in range(3) for n in range(3))

    one, none = jnp.ones((1, 1), f32), jnp.zeros((1, 1), f32)
    start_norm = jnp.sqrt(bb + epsilon)
    v0 = [one / start_norm, none, none]
    image = [shift * v0[0], v0[0], none]
    rest0 = inner(image, image)
    h00 = inner(image, v0)
    image = [a - h00 * c for a, c in zip(image, v0)]
    h10 = jnp.sqrt(jnp.maximum(inner(image, image), 0.0) + epsilon)
    v1 = [a / h10 for a in image]
    image = [shift * v1[0], v1[0] + shift * v1[1], v1[1]]
    h01, h11 = inner(image, v0), inner(image, v1)
    image = [a - h01 * c - h11 * d for a, c, d in zip(image, v0, v1)]
    h21 = jnp.sqrt(jnp.maximum(inner(image, image), 0.0) + epsilon)

    radius = jnp.sqrt(h00 * h00 + h10 * h10)
    cosine, sine = h00 / radius, h10 / radius
    upper01 = cosine * h01 + sine * h11
    lower = cosine * h11 - sine * h01
    right0, right1 = cosine * start_norm, -sine * start_norm
    radius1 = jnp.sqrt(lower * lower + h21 * h21)
    cosine1, sine1 = lower / radius1, h21 / radius1
    res_out[...] = jnp.abs(-sine1 * right1)
    y1 = cosine1 * right1 / radius1
    y0 = (right0 - upper01 * y1) / radius
    on_b = y0 * v0[0] + y1 * v1[0]
    on_p = y1 * v1[1]

    def rock_update(i):
        rock_out[i] = on_b * (Z0[0, i + 1] + E[0, i + 1]) + on_p * (Z0[1, i + 1] + E[1, i + 1])
    loop(CX, rock_update, UR)

    def frac_update(r):
        frac_out[:, slab(r)] = on_b * ZF[0, :, slab(r)] + on_p * ZF[1, :, slab(r)]
    loop(SLABS, frac_update, UF)
    for copy in started:
        copy.wait_send()


def local(sizes, rock_rhs, frac_rhs, perm, storage, pressure, frac_perm, frac_storage,
          frac_pressure, couple_geom, couple_count, couple_frac_cell, couple_rock_cell,
          host_offset, cross_pairs, cross_geom, aggregates):
    n_gx, n_y, n_z = sizes
    vmem = pl.BlockSpec(memory_space=pltpu.VMEM)
    smem = pl.BlockSpec(memory_space=pltpu.SMEM)
    in_specs = [pl.BlockSpec(memory_space=pl.ANY)] * 8 + [vmem] * 7
    in_specs.append(pl.BlockSpec(memory_space=pl.ANY))
    in_specs[9] = in_specs[12] = smem
    block = (CX, CY, NZ)
    tall = (CX + 2, CY, NZ)
    frac = (FR, FCELLS)
    slot = (FR, KC)

    def mem(*shape, kind=f32):
        return pltpu.VMEM(shape, kind)

    scratch = [
        mem(2, *tall), mem(2, *tall), mem(*tall), mem(*tall), mem(CX + 1, CY, NZ),
        *[mem(*block) for _ in range(9)], mem(ROWS, 128),
        *[mem(*frac) for _ in range(7)], mem(2, *frac), mem(FR * SLABS, 128), mem(FR * SLABS, 128),
        mem(3, ROWS, FR * KC, kind=bf16),
        mem(3, 256, FR * KC, kind=bf16), mem(384, ROWS, kind=bf16), mem(256, FR * SLABS, kind=bf16),
        mem(FR, 128, 128, kind=bf16), mem(FR * SLABS, 2 * CROSS, kind=bf16),
        mem(256, 2 * CROSS, kind=bf16), mem(128, 4096, kind=bf16), mem(256, 4096, kind=bf16),
        mem(256, 128, kind=bf16), mem(*frac), mem(8, 128),
        mem(3, *slot, kind=jnp.int32), mem(*slot, kind=jnp.int32),
        mem(*slot), mem(*slot), mem(*slot), mem(*slot), mem(3, *slot),
        mem(2, 3, CY, NZ), mem(2, 3, CY, NZ), mem(2, 3, CX, NZ), mem(2, 3, CX, NZ),
        mem(2, 2, *slot), mem(2, 2, *slot),
        mem(2, 2, CX, NZ), mem(2, 2, CX, NZ), mem(2, *slot), mem(2, 2, *slot),
        mem(2, 2, 2, *slot), mem(2, 2, 2, *slot), mem(2, 8, 128), mem(2, 4, 8, 128),
        mem(n_gx, 8, 128), mem(n_y, 8, 128), mem(n_z, 8, 128),
        mem(*block), mem(*frac), mem(*block), mem(*block), mem(*block), mem(*frac), mem(*frac),
        mem(*frac), mem(*block, kind=jnp.int32),
        pltpu.SemaphoreType.DMA((64,)), pltpu.SemaphoreType.DMA((64,)),
        pltpu.SemaphoreType.DMA((9,)),
    ]
    rock, fracs, norm = pl.pallas_call(
        functools.partial(kernel, sizes),
        out_shape=(
            jax.ShapeDtypeStruct(block, f32),
            jax.ShapeDtypeStruct(frac, f32),
            jax.ShapeDtypeStruct((1, 1), f32),
        ),
        in_specs=in_specs,
        out_specs=(vmem, vmem, vmem),
        scratch_shapes=scratch,
        compiler_params=pltpu.CompilerParams(
            collective_id=0, has_side_effects=True, vmem_limit_bytes=60 * 1024 * 1024),
    )(rock_rhs, frac_rhs, perm, storage, pressure, frac_perm, frac_storage, frac_pressure,
      couple_geom, couple_count, couple_frac_cell, couple_rock_cell, host_offset, cross_pairs,
      cross_geom.reshape(1, CROSS), aggregates)
    return rock, fracs, norm[0, 0]


def solution(mesh):
    n_gx, n_gy = mesh.shape["gx"], mesh.shape["gy"]
    n_z = 8 if n_gy % 8 == 0 else 2
    grid = P("gx", "gy", None)
    owned = P(("gx", "gy"), None)
    flat = P(("gx", "gy"))
    in_specs = (grid, owned, grid, grid, grid, owned, owned, owned, owned, flat, owned, owned,
                flat, P(None, ("gx", "gy")), flat, grid)
    return jax.shard_map(
        functools.partial(local, (n_gx, n_gy // n_z, n_z)), mesh=mesh, in_specs=in_specs,
        out_specs=(grid, owned, P()), check_vma=False)
```

```python
import functools

import jax
import jax.numpy as jnp
from jax import lax
from jax.experimental import pallas as pl
from jax.experimental.pallas import tpu as pltpu
from jax.sharding import PartitionSpec as P

CX, CY, NZ = 32, 16, 128
FR, FCELLS, FSIDE, KC = 32, 4096, 64, 128
SLABS = FCELLS // 128
NAGG = 64
ROWS = CX * CY
CROSS = 256
relaxation = 0.8
epsilon = 1e-06
MESH = pl.DeviceIdType.MESH
UB, UF, UR = 32, 32, 32
f32 = jnp.float32
bf16 = jnp.bfloat16


def iota(shape, dim):
    return lax.broadcasted_iota(jnp.int32, shape, dim)


def loop(count, body, unroll=1):
    lax.fori_loop(0, count, lambda i, c: (body(i), c)[1], 0, unroll=unroll)


def halves(x):
    high = x.astype(bf16)
    return high, (x - high.astype(f32)).astype(bf16)


def nt_dot(a, b):
    return lax.dot_general(a, b, (((1,), (1,)), ((), ())), preferred_element_type=f32)


def inverse(x):
    guess = pl.reciprocal(x, approx=True)
    guess = guess * (2.0 - x * guess)
    return guess * (2.0 - x * guess)


def lanes_of(table, index):
    return jnp.take_along_axis(table, index, axis=1)


def kernel(
    sizes,
    rock_rhs_in, frac_rhs_in, perm_in, storage_in, pressure_in, frac_perm_in, frac_storage_in,
    frac_pressure_in, geom, count, frac_cell, rock_cell, offset, pairs, cross_geom, agg_in,
    rock_out, frac_out, res_out,
    Z0, E, PA, PE, WX, WYM, WYP, WZM, WZP, RD, INVR, W1R, Q, S, DEL,
    FD, INVF, TAP, TAM, TCP, TCM, W1F, ZF, F2, S2,
    U, LV, TT, TF, BF, XU, LVX, AX, AY, AG, FI, XV, IDX, OFF, CPL, PICK, HV, AGS, VALS,
    sx, rx, sy, ry, sic, ric, szy, rzy, sfl, rfl, sans, rans, scs, rcs,
    AR0, AR1, AR2, rock_rhs, frac_rhs, perm, storage, pressure, frac_perm, frac_storage,
    frac_pressure, agg, send_sem, recv_sem, load_sem,
):
    n_gx, n_y, n_z = sizes
    n_gy = n_y * n_z
    gx = lax.axis_index("gx")
    gy = lax.axis_index("gy")
    my_y, my_z = gy // n_z, gy % n_z
    x_dev = [((gx + 1) % n_gx, gy), ((gx + n_gx - 1) % n_gx, gy)]
    y_dev = [(gx, (gy + 1) % n_gy), (gx, (gy + n_gy - 1) % n_gy)]
    gx_peers = [((gx + p) % n_gx, gy) for p in range(1, n_gx)]
    y_peers = [(gx, (my_y + p) % n_y * n_z + my_z) for p in range(1, n_y)]
    z_peers = [(gx, my_y * n_z + (my_z + p) % n_z) for p in range(1, n_z)]

    loads = [
        pltpu.make_async_copy(src, dst, load_sem.at[n])
        for n, (src, dst) in enumerate((
            (frac_pressure_in, frac_pressure), (perm_in, perm), (pressure_in, pressure),
            (agg_in, agg), (frac_perm_in, frac_perm), (frac_storage_in, frac_storage),
            (frac_rhs_in, frac_rhs), (storage_in, storage), (rock_rhs_in, rock_rhs)))
    ]
    for copy in loads:
        copy.start()

    barrier = pltpu.get_barrier_semaphore()
    everyone = gx_peers + y_peers + z_peers + y_dev
    for device in everyone:
        pl.semaphore_signal(barrier, inc=1, device_id=device, device_id_type=MESH)

    started = []

    def send(src, dst, device):
        number = len(started)
        copy = pltpu.make_async_remote_copy(
            src_ref=src, dst_ref=dst, send_sem=send_sem.at[number],
            recv_sem=recv_sem.at[number], device_id=device, device_id_type=MESH,
        )
        copy.start()
        started.append(copy)
        return copy

    sub8 = iota((8, 128), 0)
    sub16 = iota((16, 128), 0)
    sub32 = iota((32, 128), 0)
    sub128 = iota((128, 128), 0)
    lane16 = iota((16, 128), 1)
    lane32 = iota((32, 128), 1)
    row_lane = iota((1, 128), 1)
    short_rows = iota((ROWS, 128), 0).astype(jnp.int16)

    def to_table(get):
        def body(r):
            F2[pl.ds(r, FR, stride=SLABS), :] = get(r)
        loop(SLABS, body, 2)

    def slab(r):
        return pl.ds(pl.multiple_of(r * 128, 128), 128)

    def pick_slots(out):
        def body(f):
            cell = frac_cell[pl.ds(f, 1), :]
            table = F2[pl.ds(pl.multiple_of(f * SLABS, SLABS), SLABS), :]
            got = lanes_of(table, jnp.broadcast_to(cell & 127, (SLABS, 128)))
            out[pl.ds(f, 1), :] = jnp.sum(
                jnp.where(sub32 == cell >> 7, got, 0.0), axis=0, keepdims=True)
        loop(FR, body, 32)

    ends = [(e, h) for e in (0, 1) for h in (0, 1)]

    def end_cells(e, h):
        return pairs[e : e + 1, h * 128 : (h + 1) * 128]

    def turn(get, blocks, out, exact=False):
        for m in range(blocks):
            block = get(m).T
            if exact:
                out[0:128, m * 128 : (m + 1) * 128] = block.astype(bf16)
            else:
                high, low = halves(block)
                out[0:128, m * 128 : (m + 1) * 128] = high
                out[128:256, m * 128 : (m + 1) * 128] = low

    def pick_ends():
        turn(lambda m: F2[m * 128 : (m + 1) * 128, :], 8, TF)
        got = jnp.dot(TF[...], XU[...], preferred_element_type=f32)
        got = got[0:128] + got[128:256]
        return [
            jnp.sum(jnp.where(sub128 == (end_cells(e, h) & 127),
                              got[:, n * 128 : (n + 1) * 128], 0.0), axis=0, keepdims=True)
            for n, (e, h) in enumerate(ends)
        ]

    def spread_ends(end_vals):
        for n, (e, h) in enumerate(ends):
            hot = sub128 == (end_cells(e, h) & 127)
            high = end_vals[n].astype(bf16).astype(f32)
            low = end_vals[n] - high
            LVX[0:128, n * 128 : (n + 1) * 128] = jnp.where(hot, high, 0.0).astype(bf16)
            LVX[128:256, n * 128 : (n + 1) * 128] = jnp.where(hot, low, 0.0).astype(bf16)
        part = nt_dot(XU[...], LVX[...])
        S2[...] = part[:, :128] + part[:, 128:]

    def spread_slots(slot_vals):
        def body(f):
            cell = frac_cell[pl.ds(f, 1), :]
            high, low = halves(jnp.where(sub32 == cell >> 7, slot_vals[pl.ds(f, 1), :], 0.0))
            part = nt_dot(jnp.concatenate([high, low], axis=0), BF[f])
            rows = pl.ds(pl.multiple_of(f * SLABS, SLABS), SLABS)
            S2[rows, :] = S2[rows, :] + part[:32] + part[32:]
        loop(FR, body, FR)

    def build_hot(src):
        def body(f):
            cell = jnp.broadcast_to(IDX[src, pl.ds(f, 1), :], (16, 128))
            high = jnp.concatenate([(cell >> 7).astype(jnp.int16)] * 32, axis=0)
            U[src, :, slab(f)] = jnp.where(short_rows == high, bf16(1), bf16(0))
        loop(FR, body, UB)

    def spread_rock(src, vals, first):
        def body(f):
            value = vals[pl.ds(f, 1), :]
            high = value.astype(bf16).astype(f32)
            cell = jnp.broadcast_to(IDX[src, pl.ds(f, 1), :] & 127, (16, 128))
            hot = short_rows[:128] == jnp.concatenate([cell.astype(jnp.int16)] * 8, axis=0)
            for m, part in enumerate((high, value - high)):
                part = jnp.broadcast_to(part, (16, 128)).astype(bf16)
                part = jnp.concatenate([part] * 8, axis=0)
                LV[src, m * 128 : m * 128 + 128, slab(f)] = jnp.where(hot, part, bf16(0))
        loop(FR, body, FR)
        part = nt_dot(U[src], LV[src])
        total = part[:, :128] + part[:, 128:]
        DEL[...] = total if first else DEL[...] + total

    def turn_rock(get, with_agg):
        turn(get, 4, TT)
        if with_agg:
            for m in range(4):
                block = agg[m * 8 : m * 8 + 8].astype(f32).reshape(128, 128).T
                TT[256:384, m * 128 : (m + 1) * 128] = block.astype(bf16)

    def pick_rock(outs, agg_outs):
        table = TT[...] if agg_outs else TT[0:256]
        for src in outs:
            got = jnp.dot(table, U[src], preferred_element_type=f32)
            for f in range(FR):
                row, here = slice(f, f + 1), slice(f * 128, f * 128 + 128)
                hot = sub128 == IDX[src, row, :] & 127
                value = got[0:128, here] + got[128:256, here]
                outs[src][row, :] = jnp.sum(jnp.where(hot, value, 0.0), axis=0, keepdims=True)
                if agg_outs:
                    agg_outs[src][row, :] = jnp.sum(
                        jnp.where(hot, got[256:384, here], 0.0), axis=0, keepdims=True)

    def agg_cells(b, h):
        cells = agg[2 * b + h]
        return cells, pl.ds(pl.multiple_of(b * 256 + h * 128, 128), 128)

    def build_aggregates():
        def body(b):
            for h in (0, 1):
                cells, here = agg_cells(b, h)
                cells = (cells & 15).astype(jnp.int16)
                for a in range(16):
                    AY[a * 16 : a * 16 + 16, here] = jnp.where(
                        cells == jnp.int16(a), bf16(1), bf16(0))
        loop(16, body, 2)
        place = iota((256, 128), 0) >> 4 == iota((256, 128), 1) & 15
        AG[...] = place.astype(f32).astype(bf16)

    def aggregate_sums(src):
        def body(b):
            for h in (0, 1):
                cells, here = agg_cells(b, h)
                cells = cells >> 4
                value = src[2 * b + h]
                high = value.astype(bf16).astype(f32)
                low = value - high
                for a in range(4):
                    AX[a * 32 : a * 32 + 16, here] = jnp.where(cells == a, high, 0.0).astype(bf16)
                    AX[a * 32 + 16 : a * 32 + 32, here] = jnp.where(cells == a, low, 0.0).astype(bf16)
        loop(16, body, 16)
        part = nt_dot(AX[...], AY[...])
        part = jnp.where(iota((128, 256), 0) & 15 == iota((128, 256), 1) & 15, part, 0.0)
        rest = jnp.concatenate([fold(part[a * 32 : a * 32 + 32]) for a in range(4)], axis=0)
        pieces = []
        for _ in range(3):
            pieces.append(rest.astype(bf16))
            rest = rest - pieces[-1].astype(f32)
        total = jnp.dot(jnp.concatenate(pieces, axis=0), AG[...], preferred_element_type=f32)
        total = total[0:32] + total[32:64] + total[64:96]
        total = jnp.where(sub32 >> 3 == lane32 >> 4, total, 0.0)
        return jnp.broadcast_to(jnp.sum(total, axis=0, keepdims=True), (16, 128))

    def fold(x):
        return sum(x[j : j + 8] for j in range(0, x.shape[0], 8))

    loads[0].wait()
    to_table(lambda r: frac_pressure[:, slab(r)])
    pick_slots(PICK)

    def split_slots(f):
        where = offset[f]
        row = pl.ds(f, 1)
        OFF[row, :] = jnp.full((1, 128), where, jnp.int32)
        cell = rock_cell[row, :]
        live = row_lane < count[f]
        IDX[0, row, :] = jnp.where(live & (where == 0), cell, -1)
        sic[0, 0, row, :] = jnp.where(live & (where == 1), cell, -1).astype(f32)
        sic[1, 0, row, :] = jnp.where(live & (where == -1), cell, -1).astype(f32)
        value = jnp.where(live, geom[row, :] * jnp.exp(-0.5 * PICK[row, :]), 0.0)
        CPL[row, :] = value
    loop(FR, split_slots, 4)
    sic[0, 1] = CPL[...]
    sic[1, 1] = CPL[...]

    for copy in loads[1:4]:
        copy.wait()
    for d, plane in enumerate((CX - 1, 0)):
        sx[d, 0] = perm[plane]
        sx[d, 1] = pressure[plane]
        sx[d, 2] = agg[plane].astype(f32)
    for d, row in enumerate((CY - 1, 0)):
        sy[d, 0] = perm[:, row, :]
        sy[d, 1] = pressure[:, row, :]
        sy[d, 2] = agg[:, row, :].astype(f32)

    pl.semaphore_wait(barrier, len(everyone))
    slots_sent = [send(sic.at[d], ric.at[d], y_dev[d]) for d in (0, 1)]
    faces_sent = [send(sx.at[d], rx.at[d], x_dev[d]) for d in (0, 1)]
    faces_sent += [send(sy.at[d], ry.at[d], y_dev[d]) for d in (0, 1)]

    for copy in loads[4:]:
        copy.wait()

    def scale_frac(r):
        press = frac_pressure[:, slab(r)]
        TCM[:, slab(r)] = frac_perm[:, slab(r)] * jnp.exp(-0.25 * press)
    loop(SLABS, scale_frac, UF)

    def face_along(r):
        conduct, scaled = frac_perm[:, slab(r)], TCM[:, slab(r)]
        near, near_scaled = pltpu.roll(conduct, 127, 1), pltpu.roll(scaled, 127, 1)
        weight = 2.0 * scaled * near_scaled * inverse(conduct + near)
        weight = jnp.where(lane32 & (FSIDE - 1) < FSIDE - 1, weight, 0.0)
        TAP[:, slab(r)] = weight
        TAM[:, slab(r)] = pltpu.roll(weight, 1, 1)
        after = slab(jnp.minimum(r + 1, SLABS - 1))
        first = lane32 < FSIDE
        near = pltpu.roll(jnp.where(first, frac_perm[:, after], conduct), FSIDE, 1)
        near_scaled = pltpu.roll(jnp.where(first, TCM[:, after], scaled), FSIDE, 1)
        weight = 2.0 * scaled * near_scaled * inverse(conduct + near)
        TCP[:, slab(r)] = jnp.where(first | (r < SLABS - 1), weight, 0.0)
    loop(SLABS, face_along, UF)

    for n, (e, h) in enumerate(ends):
        for m in range(8):
            hot = (sub128 + m * 128 == end_cells(e, h) >> 7).astype(f32).astype(bf16)
            XU[m * 128 : (m + 1) * 128, n * 128 : (n + 1) * 128] = hot
    pressures = pick_ends()
    for h in (0, 1):
        XV[h : h + 1, :] = cross_geom[0:1, h * 128 : (h + 1) * 128] * jnp.exp(
            -0.25 * (pressures[h] + pressures[h + 2]))

    def build_lanes(f):
        BF[f] = (sub128 == (frac_cell[pl.ds(f, 1), :] & 127)).astype(f32).astype(bf16)
    loop(FR, build_lanes, 2)
    coefs = [XV[h : h + 1, :] for h in (0, 1)]
    spread_ends(coefs + coefs)
    spread_slots(CPL)

    def face_back(r):
        before = slab(jnp.maximum(r - 1, 0))
        first = lane32 < FSIDE
        own = TCP[:, slab(r)]
        back = pltpu.roll(jnp.where(first, own, TCP[:, before]), FSIDE, 1)
        back = jnp.where(jnp.logical_not(first) | (r > 0), back, 0.0)
        TCM[:, slab(r)] = back
        diag = frac_storage[:, slab(r)] + TAP[:, slab(r)] + TAM[:, slab(r)] + own + back
        diag = diag + S2[pl.ds(r, FR, stride=SLABS), :]
        FD[:, slab(r)] = diag
        INVF[:, slab(r)] = relaxation * inverse(diag)
    loop(SLABS, face_back, UF)

    def smooth_frac(k, source):
        def body(r):
            z = source[:, slab(r)] * INVF[:, slab(r)]
            ZF[k, :, slab(r)] = z
            F2[pl.ds(r, FR, stride=SLABS), :] = z
        loop(SLABS, body, UF)
        pick_slots(PICK)
        sfl[k] = CPL[...] * PICK[...]
        return [send(sfl.at[k], rfl.at[k, d], y_dev[d]) for d in (0, 1)]

    flux_sent = smooth_frac(0, frac_rhs)

    build_hot(0)
    spread_rock(0, CPL, True)
    for copy in slots_sent:
        copy.wait_recv()
    for d in (0, 1):
        IDX[1 + d] = ric[d, 0].astype(jnp.int32)
        build_hot(1 + d)
        spread_rock(1 + d, ric.at[d, 1], False)
    build_aggregates()
    for copy in faces_sent:
        copy.wait_recv()
    open_x = [gx > 0, gx < n_gx - 1]
    open_y = [gy > 0, gy < n_gy - 1]

    def scale_rock(i):
        conduct = perm[i]
        PA[i + 1] = conduct
        PE[i + 1] = conduct * jnp.exp(-0.25 * pressure[i])
    loop(CX, scale_rock, UR)
    for d, plane in enumerate((0, CX + 1)):
        conduct = jnp.where(open_x[d], rx[d, 0], 0.0)
        PA[plane] = conduct
        PE[plane] = conduct * jnp.exp(-0.25 * rx[d, 1])
    for d in (0, 1):
        conduct = jnp.where(open_y[d], ry[d, 0], 0.0)
        ry[d, 0] = conduct
        ry[d, 1] = conduct * jnp.exp(-0.25 * ry[d, 1])

    def below(x, edge):
        return jnp.where(sub16 == 0, edge, pltpu.roll(x, 1, 0))

    def above(x, edge):
        return jnp.where(sub16 == CY - 1, edge, pltpu.roll(x, CY - 1, 0))

    def face(conduct, scaled, near, near_scaled):
        return 2.0 * scaled * near_scaled * inverse(conduct + near)

    VALS[0] = face(perm[:, 0, :], PE[1 : CX + 1, 0, :], ry[0, 0], ry[0, 1])

    def rock_faces(i):
        conduct, scaled = PA[i + 1], PE[i + 1]
        row = pl.ds(i, 1)
        WX[i] = face(conduct, scaled, PA[i], PE[i])
        side = face(conduct, scaled, above(conduct, ry[1, 0, row, :]),
                    above(scaled, ry[1, 1, row, :]))
        WYP[i] = side
        WYM[i] = below(side, VALS[0, row, :])
        up = face(conduct, scaled, pltpu.roll(conduct, 127, 1), pltpu.roll(scaled, 127, 1))
        up = jnp.where(lane16 < NZ - 1, up, 0.0)
        WZP[i] = up
        WZM[i] = pltpu.roll(up, 1, 1)
    loop(CX, rock_faces, UR)
    WX[CX] = face(PA[CX], PE[CX], PA[CX + 1], PE[CX + 1])

    def rock_diagonal(i):
        faces = [WX[i], WX[i + 1], WYM[i], WYP[i], WZM[i], WZP[i]]
        rows = pl.ds(pl.multiple_of(i * CY, CY), CY)
        diag = storage[i] + sum(faces) + DEL[rows, :]
        RD[i] = diag
        INVR[i] = relaxation * inverse(diag)
        mine = agg[i]
        inside = lambda n: jnp.clip(n, 0, CX - 1)
        nears = [
            jnp.where(i > 0, agg[inside(i - 1)], -1),
            jnp.where(i < CX - 1, agg[inside(i + 1)], -1),
            below(mine, -1), above(mine, -1),
            pltpu.roll(mine, 1, 1), pltpu.roll(mine, 127, 1),
        ]
        for face, near in zip(faces, nears):
            diag = diag - jnp.where(near == mine, face, 0.0)
        S[i] = diag
    loop(CX, rock_diagonal, UR)
    coarse_diag = aggregate_sums(S)
    inverse_coarse = 1.0 / jnp.where(lane16 < NAGG, coarse_diag, 1.0)

    def stencil(i, center, low_x, high_x, low_y, high_y):
        out = RD[i] * center
        out = out - WX[i] * low_x - WX[i + 1] * high_x
        out = out - WYM[i] * below(center, low_y) - WYP[i] * above(center, high_y)
        return out - WZM[i] * pltpu.roll(center, 1, 1) - WZP[i] * pltpu.roll(center, 127, 1)

    def send_faces(k):
        for d, row in enumerate((CY - 1, 0)):
            szy[k, d] = Z0[k, 1 : CX + 1, row, :]
        return [
            send(Z0.at[k, CX], Z0.at[k, 0], x_dev[0]),
            send(Z0.at[k, 1], Z0.at[k, CX + 1], x_dev[1]),
        ] + [send(szy.at[k, d], rzy.at[k, d], y_dev[d]) for d in (0, 1)]

    def iterate(k, rock_vec, frac_vec, halo_sent, flux_sent):
        turn_rock(lambda m: Z0[k, m * 8 + 1 : m * 8 + 9].reshape(128, 128), k == 0)
        pick_rock({1: sans.at[k, 0, 0], 2: sans.at[k, 1, 0]},
                  None if k else {1: sans.at[k, 0, 1], 2: sans.at[k, 1, 1]})
        parts = 1 if k else 2
        answers_sent = [
            send(sans.at[k, 1 - d, 0:parts], rans.at[k, d, 0:parts], y_dev[d]) for d in (0, 1)]
        spread_rock(0, sfl.at[k], True)
        for copy in flux_sent:
            copy.wait_recv()
        for d in (0, 1):
            spread_rock(1 + d, rfl.at[k, d], False)
        for copy in halo_sent:
            copy.wait_recv()

        def residual(i):
            row = pl.ds(i, 1)
            rows = pl.ds(pl.multiple_of(i * CY, CY), CY)
            image = stencil(i, Z0[k, i + 1], Z0[k, i], Z0[k, i + 2],
                            rzy[k, 0, row, :], rzy[k, 1, row, :]) - DEL[rows, :]
            Q[i] = image
            S[i] = rock_vec[i] - image
        loop(CX, residual, UR)
        coarse = aggregate_sums(S) * inverse_coarse
        scs[k] = coarse[0:8]
        coarse_sent = [send(scs.at[k], rcs.at[k, d], x_dev[d]) for d in (0, 1)]
        coarse_sent += [send(scs.at[k], rcs.at[k, 2 + d], y_dev[d]) for d in (0, 1)]

        pick_rock({0: HV}, None if k else {0: AGS})
        values = pick_ends()
        coefs = [XV[h : h + 1, :] for h in (0, 1)]
        spread_ends([coefs[h] * values[2 * (1 - e) + h] for e, h in ends])

        def correct(i):
            E[k, i + 1] = lanes_of(coarse, agg[i])
        loop(CX, correct, UR)
        for plane in (0, CX + 1):
            E[k, plane] = jnp.zeros((CY, NZ), f32)

        def correct_image(i):
            edge = jnp.zeros((1, NZ), f32)
            image = stencil(i, E[k, i + 1], E[k, i], E[k, i + 2], edge, edge)
            Q[i] = Q[i] + image - relaxation * rock_vec[i]
        loop(CX, correct_image, UR)

        def frac_faces(r):
            here = slab(r)
            z = ZF[k, :, here]
            before = ZF[k, :, slab(jnp.maximum(r - 1, 0))]
            after = ZF[k, :, slab(jnp.minimum(r + 1, SLABS - 1))]
            first = lane32 < FSIDE
            down = pltpu.roll(jnp.where(first, after, z), FSIDE, 1)
            up = pltpu.roll(jnp.where(first, z, before), FSIDE, 1)
            image = FD[:, here] * z
            image = image - TAP[:, here] * pltpu.roll(z, 127, 1) - TAM[:, here] * pltpu.roll(z, 1, 1)
            image = image - TCP[:, here] * down - TCM[:, here] * up
            FI[:, here] = image - relaxation * frac_vec[:, here]
        loop(SLABS, frac_faces, UF)
        for copy in answers_sent + coarse_sent:
            copy.wait_recv()
        if k == 0:
            AGS[...] = AGS[...] + rans[0, 0, 1] + rans[0, 1, 1]
        tables = [jnp.concatenate([rcs[k, d], rcs[k, d]], axis=0) for d in range(4)]
        for d, plane in enumerate((0, CX - 1)):
            near = lanes_of(tables[d], rx[d, 2].astype(jnp.int32))
            Q[plane] = Q[plane] - WX[plane + d] * near
        for d in (0, 1):
            table = jnp.concatenate([tables[2 + d]] * 2, axis=0)
            VALS[d] = lanes_of(table, ry[d, 2].astype(jnp.int32))
        slot_agg = AGS[...].astype(jnp.int32)
        four = [jnp.concatenate([t] * 2, axis=0) for t in (coarse, tables[2], tables[3])]
        own, low, high = [lanes_of(t, slot_agg) for t in four]
        where = OFF[...]
        host = HV[...] + rans[k, 0, 0] + rans[k, 1, 0]
        host = host + jnp.where(where == 0, own, jnp.where(where < 0, low, high))
        VALS[2] = CPL[...] * host

        zero = jnp.zeros((8, 128), f32)

        def products(x, v, b):
            if k == 0:
                return fold(v * v), fold(x * v), fold(x * x)
            return fold(x * b), fold(x * v), fold(x * x)

        spread_slots(VALS.at[2])

        def frac_image(r, accs):
            here = slab(r)
            vec = frac_vec[:, here]
            image = FI[:, here] - S2[pl.ds(r, FR, stride=SLABS), :]
            if k == 0:
                W1F[:, here] = image
            return tuple(a + p for a, p in zip(accs, products(image, vec, frac_rhs[:, here])))
        accs = lax.fori_loop(0, SLABS, frac_image, (zero,) * 3, unroll=UF)
        flux_next = smooth_frac(1, W1F) if k == 0 else None

        def rock_image(i, accs):
            row = pl.ds(i, 1)
            vec = rock_vec[i]
            image = Q[i] - jnp.where(sub16 == 0, WYM[i] * VALS[0, row, :], 0.0)
            image = image - jnp.where(sub16 == CY - 1, WYP[i] * VALS[1, row, :], 0.0)
            if k == 0:
                W1R[i] = image
                Z0[1, i + 1] = image * INVR[i]
            return tuple(a + p for a, p in zip(accs, products(image, vec, rock_rhs[i])))
        accs = lax.fori_loop(0, CX, rock_image, accs, unroll=UR)
        halo_next = send_faces(1) if k == 0 else None
        return list(accs), halo_next, flux_next

    def smooth_rock(i):
        Z0[0, i + 1] = rock_rhs[i] * INVR[i]
    loop(CX, smooth_rock, UR)
    dots, halo_sent, flux_sent = iterate(0, rock_rhs, frac_rhs, send_faces(0), flux_sent)
    dots += iterate(1, W1R, W1F, halo_sent, flux_sent)[0]

    tile = jnp.zeros((8, 128), f32)
    for n, part in enumerate(dots):
        tile = jnp.where(sub8 == n, jnp.sum(part, axis=0, keepdims=True), tile)
    groups = [(AR0, gx, gx_peers, n_gx), (AR1, my_y, y_peers, n_y), (AR2, my_z, z_peers, n_z)]
    for slots, me, peers, size in groups:
        slots[pl.ds(me, 1)] = tile[None]
        earlier = len(started)
        copies = [send(slots.at[me], slots.at[me], device) for device in peers]
        if slots is AR0:
            def join(i):
                for k in (0, 1):
                    E[k, i + 1] = E[k, i + 1] + Z0[k, i + 1]
            loop(CX, join, UR)
        if slots is AR2:
            for copy in started[:earlier]:
                copy.wait_send()
        for copy in copies:
            copy.wait_recv()
        tile = sum(slots[n] for n in range(size))
    tile = jnp.sum(tile, axis=1, keepdims=True)
    bb, pb, pp, qb, qp, qq = [tile[n : n + 1, :] for n in range(6)]
    gram = [[bb, pb, qb], [pb, pp, qp], [qb, qp, qq]]
    shift = relaxation

    def inner(a, c):
        return sum(a[m] * c[n] * gram[m][n] for m in range(3) for n in range(3))

    one, none = jnp.ones((1, 1), f32), jnp.zeros((1, 1), f32)
    start_norm = jnp.sqrt(bb + epsilon)
    v0 = [one / start_norm, none, none]
    image = [shift * v0[0], v0[0], none]
    rest0 = inner(image, image)
    h00 = inner(image, v0)
    image = [a - h00 * c for a, c in zip(image, v0)]
    h10 = jnp.sqrt(jnp.maximum(inner(image, image), 0.0) + epsilon)
    v1 = [a / h10 for a in image]
    image = [shift * v1[0], v1[0] + shift * v1[1], v1[1]]
    h01, h11 = inner(image, v0), inner(image, v1)
    image = [a - h01 * c - h11 * d for a, c, d in zip(image, v0, v1)]
    h21 = jnp.sqrt(jnp.maximum(inner(image, image), 0.0) + epsilon)

    radius = jnp.sqrt(h00 * h00 + h10 * h10)
    cosine, sine = h00 / radius, h10 / radius
    upper01 = cosine * h01 + sine * h11
    lower = cosine * h11 - sine * h01
    right0, right1 = cosine * start_norm, -sine * start_norm
    radius1 = jnp.sqrt(lower * lower + h21 * h21)
    cosine1, sine1 = lower / radius1, h21 / radius1
    res_out[...] = jnp.abs(-sine1 * right1)
    y1 = cosine1 * right1 / radius1
    y0 = (right0 - upper01 * y1) / radius
    on_b = y0 * v0[0] + y1 * v1[0]
    on_p = y1 * v1[1]

    def rock_update(i):
        rock_out[i] = on_b * E[0, i + 1] + on_p * E[1, i + 1]
    loop(CX, rock_update, UR)

    def frac_update(r):
        frac_out[:, slab(r)] = on_b * ZF[0, :, slab(r)] + on_p * ZF[1, :, slab(r)]
    loop(SLABS, frac_update, UF)
    for copy in started[earlier:]:
        copy.wait_send()


def local(sizes, rock_rhs, frac_rhs, perm, storage, pressure, frac_perm, frac_storage,
          frac_pressure, couple_geom, couple_count, couple_frac_cell, couple_rock_cell,
          host_offset, cross_pairs, cross_geom, aggregates):
    n_gx, n_y, n_z = sizes
    vmem = pl.BlockSpec(memory_space=pltpu.VMEM)
    smem = pl.BlockSpec(memory_space=pltpu.SMEM)
    in_specs = [pl.BlockSpec(memory_space=pl.ANY)] * 8 + [vmem] * 7
    in_specs.append(pl.BlockSpec(memory_space=pl.ANY))
    in_specs[9] = in_specs[12] = smem
    block = (CX, CY, NZ)
    tall = (CX + 2, CY, NZ)
    frac = (FR, FCELLS)
    slot = (FR, KC)

    def mem(*shape, kind=f32):
        return pltpu.VMEM(shape, kind)

    scratch = [
        mem(2, *tall), mem(2, *tall), mem(*tall), mem(*tall), mem(CX + 1, CY, NZ),
        *[mem(*block) for _ in range(9)], mem(ROWS, 128),
        *[mem(*frac) for _ in range(7)], mem(2, *frac), mem(FR * SLABS, 128), mem(FR * SLABS, 128),
        mem(3, ROWS, FR * KC, kind=bf16),
        mem(3, 256, FR * KC, kind=bf16), mem(384, ROWS, kind=bf16), mem(256, FR * SLABS, kind=bf16),
        mem(FR, 128, 128, kind=bf16), mem(FR * SLABS, 2 * CROSS, kind=bf16),
        mem(256, 2 * CROSS, kind=bf16), mem(128, 4096, kind=bf16), mem(256, 4096, kind=bf16),
        mem(256, 128, kind=bf16), mem(*frac), mem(8, 128),
        mem(3, *slot, kind=jnp.int32), mem(*slot, kind=jnp.int32),
        mem(*slot), mem(*slot), mem(*slot), mem(*slot), mem(3, *slot),
        mem(2, 3, CY, NZ), mem(2, 3, CY, NZ), mem(2, 3, CX, NZ), mem(2, 3, CX, NZ),
        mem(2, 2, *slot), mem(2, 2, *slot),
        mem(2, 2, CX, NZ), mem(2, 2, CX, NZ), mem(2, *slot), mem(2, 2, *slot),
        mem(2, 2, 2, *slot), mem(2, 2, 2, *slot), mem(2, 8, 128), mem(2, 4, 8, 128),
        mem(n_gx, 8, 128), mem(n_y, 8, 128), mem(n_z, 8, 128),
        mem(*block), mem(*frac), mem(*block), mem(*block), mem(*block), mem(*frac), mem(*frac),
        mem(*frac), mem(*block, kind=jnp.int32),
        pltpu.SemaphoreType.DMA((64,)), pltpu.SemaphoreType.DMA((64,)),
        pltpu.SemaphoreType.DMA((9,)),
    ]
    rock, fracs, norm = pl.pallas_call(
        functools.partial(kernel, sizes),
        out_shape=(
            jax.ShapeDtypeStruct(block, f32),
            jax.ShapeDtypeStruct(frac, f32),
            jax.ShapeDtypeStruct((1, 1), f32),
        ),
        in_specs=in_specs,
        out_specs=(vmem, vmem, vmem),
        scratch_shapes=scratch,
        compiler_params=pltpu.CompilerParams(
            collective_id=0, has_side_effects=True, vmem_limit_bytes=60 * 1024 * 1024),
    )(rock_rhs, frac_rhs, perm, storage, pressure, frac_perm, frac_storage, frac_pressure,
      couple_geom, couple_count, couple_frac_cell, couple_rock_cell, host_offset, cross_pairs,
      cross_geom.reshape(1, CROSS), aggregates)
    return rock, fracs, norm[0, 0]


def solution(mesh):
    n_gx, n_gy = mesh.shape["gx"], mesh.shape["gy"]
    n_z = 8 if n_gy % 8 == 0 else 2
    grid = P("gx", "gy", None)
    owned = P(("gx", "gy"), None)
    flat = P(("gx", "gy"))
    in_specs = (grid, owned, grid, grid, grid, owned, owned, owned, owned, flat, owned, owned,
                flat, P(None, ("gx", "gy")), flat, grid)
    return jax.shard_map(
        functools.partial(local, (n_gx, n_gy // n_z, n_z)), mesh=mesh, in_specs=in_specs,
        out_specs=(grid, owned, P()), check_vma=False)
```

```python
import functools

import jax
import jax.numpy as jnp
from jax import lax
from jax.experimental import pallas as pl
from jax.experimental.pallas import tpu as pltpu
from jax.sharding import PartitionSpec as P

CX, CY, NZ = 32, 16, 128
FR, FCELLS, FSIDE, KC = 32, 4096, 64, 128
SLABS = FCELLS // 128
NAGG = 64
ROWS = CX * CY
CROSS = 256
relaxation = 0.8
epsilon = 1e-06
MESH = pl.DeviceIdType.MESH
UB, UF, UR = 32, 32, 32
f32 = jnp.float32
bf16 = jnp.bfloat16


def iota(shape, dim):
    return lax.broadcasted_iota(jnp.int32, shape, dim)


def loop(count, body, unroll=1):
    lax.fori_loop(0, count, lambda i, c: (body(i), c)[1], 0, unroll=unroll)


def halves(x):
    high = x.astype(bf16)
    return high, (x - high.astype(f32)).astype(bf16)


def nt_dot(a, b):
    return lax.dot_general(a, b, (((1,), (1,)), ((), ())), preferred_element_type=f32)


def inverse(x):
    guess = pl.reciprocal(x, approx=True)
    guess = guess * (2.0 - x * guess)
    return guess * (2.0 - x * guess)


def lanes_of(table, index):
    return jnp.take_along_axis(table, index, axis=1)


def kernel(
    sizes,
    rock_rhs_in, frac_rhs_in, perm_in, storage_in, pressure_in, frac_perm_in, frac_storage_in,
    frac_pressure_in, geom, count, frac_cell, rock_cell, offset, pairs, cross_geom, agg_in,
    rock_out, frac_out, res_out,
    Z0, E, PA, PE, WX, WYM, WYP, WZM, WZP, RD, INVR, W1R, Q, S, DEL,
    FD, INVF, TAP, TAM, TCP, TCM, W1F, ZF, F2, S2,
    U, LV, TT, TF, BF, XU, LVX, AX, AY, AG, FI, XV, IDX, OFF, CPL, PICK, HV, AGS, VALS,
    sx, rx, sy, ry, sic, ric, szy, rzy, sfl, rfl, sans, rans, scs, rcs,
    AR0, AR2, rock_rhs, frac_rhs, perm, storage, pressure, frac_perm, frac_storage,
    frac_pressure, agg, send_sem, recv_sem, load_sem,
):
    n_gx, n_y, n_z = sizes
    n_gy = n_y * n_z
    gx = lax.axis_index("gx")
    gy = lax.axis_index("gy")
    my_y, my_z = gy // n_z, gy % n_z
    x_dev = [((gx + 1) % n_gx, gy), ((gx + n_gx - 1) % n_gx, gy)]
    y_dev = [(gx, (gy + 1) % n_gy), (gx, (gy + n_gy - 1) % n_gy)]
    my_xy, n_xy = gx * n_y + my_y, n_gx * n_y
    xy_peers = [
        (n // n_y, n % n_y * n_z + my_z) for n in ((my_xy + p) % n_xy for p in range(1, n_xy))]
    z_peers = [(gx, my_y * n_z + (my_z + p) % n_z) for p in range(1, n_z)]

    loads = [
        pltpu.make_async_copy(src, dst, load_sem.at[n])
        for n, (src, dst) in enumerate((
            (frac_pressure_in, frac_pressure), (perm_in, perm), (pressure_in, pressure),
            (agg_in, agg), (frac_perm_in, frac_perm), (frac_storage_in, frac_storage),
            (frac_rhs_in, frac_rhs), (storage_in, storage), (rock_rhs_in, rock_rhs)))
    ]
    for copy in loads:
        copy.start()

    barrier = pltpu.get_barrier_semaphore()
    everyone = xy_peers + z_peers + y_dev
    for device in everyone:
        pl.semaphore_signal(barrier, inc=1, device_id=device, device_id_type=MESH)

    started = []

    def send(src, dst, device):
        number = len(started)
        copy = pltpu.make_async_remote_copy(
            src_ref=src, dst_ref=dst, send_sem=send_sem.at[number],
            recv_sem=recv_sem.at[number], device_id=device, device_id_type=MESH,
        )
        copy.start()
        started.append(copy)
        return copy

    sub8 = iota((8, 128), 0)
    sub16 = iota((16, 128), 0)
    sub32 = iota((32, 128), 0)
    sub128 = iota((128, 128), 0)
    lane16 = iota((16, 128), 1)
    lane32 = iota((32, 128), 1)
    row_lane = iota((1, 128), 1)
    short_rows = iota((ROWS, 128), 0).astype(jnp.int16)

    def to_table(get):
        def body(r):
            F2[pl.ds(r, FR, stride=SLABS), :] = get(r)
        loop(SLABS, body, 2)

    def slab(r):
        return pl.ds(pl.multiple_of(r * 128, 128), 128)

    def pick_slots(out):
        def body(f):
            cell = frac_cell[pl.ds(f, 1), :]
            table = F2[pl.ds(pl.multiple_of(f * SLABS, SLABS), SLABS), :]
            got = lanes_of(table, jnp.broadcast_to(cell & 127, (SLABS, 128)))
            out[pl.ds(f, 1), :] = jnp.sum(
                jnp.where(sub32 == cell >> 7, got, 0.0), axis=0, keepdims=True)
        loop(FR, body, 32)

    ends = [(e, h) for e in (0, 1) for h in (0, 1)]

    def end_cells(e, h):
        return pairs[e : e + 1, h * 128 : (h + 1) * 128]

    def turn(get, blocks, out, exact=False):
        for m in range(blocks):
            block = get(m).T
            if exact:
                out[0:128, m * 128 : (m + 1) * 128] = block.astype(bf16)
            else:
                high, low = halves(block)
                out[0:128, m * 128 : (m + 1) * 128] = high
                out[128:256, m * 128 : (m + 1) * 128] = low

    def pick_ends():
        turn(lambda m: F2[m * 128 : (m + 1) * 128, :], 8, TF)
        got = jnp.dot(TF[...], XU[...], preferred_element_type=f32)
        got = got[0:128] + got[128:256]
        return [
            jnp.sum(jnp.where(sub128 == (end_cells(e, h) & 127),
                              got[:, n * 128 : (n + 1) * 128], 0.0), axis=0, keepdims=True)
            for n, (e, h) in enumerate(ends)
        ]

    def spread_ends(end_vals):
        for n, (e, h) in enumerate(ends):
            hot = sub128 == (end_cells(e, h) & 127)
            high = end_vals[n].astype(bf16).astype(f32)
            low = end_vals[n] - high
            LVX[0:128, n * 128 : (n + 1) * 128] = jnp.where(hot, high, 0.0).astype(bf16)
            LVX[128:256, n * 128 : (n + 1) * 128] = jnp.where(hot, low, 0.0).astype(bf16)
        part = nt_dot(XU[...], LVX[...])
        S2[...] = part[:, :128] + part[:, 128:]

    def spread_slots(slot_vals):
        def body(f):
            cell = frac_cell[pl.ds(f, 1), :]
            high, low = halves(jnp.where(sub32 == cell >> 7, slot_vals[pl.ds(f, 1), :], 0.0))
            part = nt_dot(jnp.concatenate([high, low], axis=0), BF[f])
            rows = pl.ds(pl.multiple_of(f * SLABS, SLABS), SLABS)
            S2[rows, :] = S2[rows, :] + part[:32] + part[32:]
        loop(FR, body, FR)

    def build_hot(src):
        def body(f):
            cell = jnp.broadcast_to(IDX[src, pl.ds(f, 1), :], (16, 128))
            high = jnp.concatenate([(cell >> 7).astype(jnp.int16)] * 32, axis=0)
            U[src, :, slab(f)] = jnp.where(short_rows == high, bf16(1), bf16(0))
        loop(FR, body, UB)

    def spread_rock(src, vals, first):
        def body(f):
            value = vals[pl.ds(f, 1), :]
            high = value.astype(bf16).astype(f32)
            cell = jnp.broadcast_to(IDX[src, pl.ds(f, 1), :] & 127, (16, 128))
            hot = short_rows[:128] == jnp.concatenate([cell.astype(jnp.int16)] * 8, axis=0)
            for m, part in enumerate((high, value - high)):
                part = jnp.broadcast_to(part, (16, 128)).astype(bf16)
                part = jnp.concatenate([part] * 8, axis=0)
                LV[src, m * 128 : m * 128 + 128, slab(f)] = jnp.where(hot, part, bf16(0))
        loop(FR, body, FR)
        part = nt_dot(U[src], LV[src])
        total = part[:, :128] + part[:, 128:]
        DEL[...] = total if first else DEL[...] + total

    def turn_rock(get, with_agg):
        turn(get, 4, TT)
        if with_agg:
            for m in range(4):
                block = agg[m * 8 : m * 8 + 8].astype(f32).reshape(128, 128).T
                TT[256:384, m * 128 : (m + 1) * 128] = block.astype(bf16)

    def pick_rock(outs, agg_outs):
        table = TT[...] if agg_outs else TT[0:256]
        for src in outs:
            got = jnp.dot(table, U[src], preferred_element_type=f32)
            for f in range(FR):
                row, here = slice(f, f + 1), slice(f * 128, f * 128 + 128)
                hot = sub128 == IDX[src, row, :] & 127
                value = got[0:128, here] + got[128:256, here]
                outs[src][row, :] = jnp.sum(jnp.where(hot, value, 0.0), axis=0, keepdims=True)
                if agg_outs:
                    agg_outs[src][row, :] = jnp.sum(
                        jnp.where(hot, got[256:384, here], 0.0), axis=0, keepdims=True)

    def agg_cells(b, h):
        cells = agg[2 * b + h]
        return cells, pl.ds(pl.multiple_of(b * 256 + h * 128, 128), 128)

    def build_aggregates():
        def body(b):
            for h in (0, 1):
                cells, here = agg_cells(b, h)
                cells = (cells & 15).astype(jnp.int16)
                for a in range(16):
                    AY[a * 16 : a * 16 + 16, here] = jnp.where(
                        cells == jnp.int16(a), bf16(1), bf16(0))
        loop(16, body, 2)
        place = iota((256, 128), 0) >> 4 == iota((256, 128), 1) & 15
        AG[...] = place.astype(f32).astype(bf16)

    def aggregate_sums(src):
        def body(b):
            for h in (0, 1):
                cells, here = agg_cells(b, h)
                cells = cells >> 4
                value = src[2 * b + h]
                high = value.astype(bf16).astype(f32)
                low = value - high
                for a in range(4):
                    AX[a * 32 : a * 32 + 16, here] = jnp.where(cells == a, high, 0.0).astype(bf16)
                    AX[a * 32 + 16 : a * 32 + 32, here] = jnp.where(cells == a, low, 0.0).astype(bf16)
        loop(16, body, 16)
        part = nt_dot(AX[...], AY[...])
        part = jnp.where(iota((128, 256), 0) & 15 == iota((128, 256), 1) & 15, part, 0.0)
        rest = jnp.concatenate([fold(part[a * 32 : a * 32 + 32]) for a in range(4)], axis=0)
        pieces = []
        for _ in range(3):
            pieces.append(rest.astype(bf16))
            rest = rest - pieces[-1].astype(f32)
        total = jnp.dot(jnp.concatenate(pieces, axis=0), AG[...], preferred_element_type=f32)
        total = total[0:32] + total[32:64] + total[64:96]
        total = jnp.where(sub32 >> 3 == lane32 >> 4, total, 0.0)
        return jnp.broadcast_to(jnp.sum(total, axis=0, keepdims=True), (16, 128))

    def fold(x):
        return sum(x[j : j + 8] for j in range(0, x.shape[0], 8))

    loads[0].wait()
    to_table(lambda r: frac_pressure[:, slab(r)])
    pick_slots(PICK)

    def split_slots(f):
        where = offset[f]
        row = pl.ds(f, 1)
        OFF[row, :] = jnp.full((1, 128), where, jnp.int32)
        cell = rock_cell[row, :]
        live = row_lane < count[f]
        IDX[0, row, :] = jnp.where(live & (where == 0), cell, -1)
        sic[0, 0, row, :] = jnp.where(live & (where == 1), cell, -1).astype(f32)
        sic[1, 0, row, :] = jnp.where(live & (where == -1), cell, -1).astype(f32)
        value = jnp.where(live, geom[row, :] * jnp.exp(-0.5 * PICK[row, :]), 0.0)
        CPL[row, :] = value
    loop(FR, split_slots, 4)
    sic[0, 1] = CPL[...]
    sic[1, 1] = CPL[...]

    for copy in loads[1:4]:
        copy.wait()
    for d, plane in enumerate((CX - 1, 0)):
        sx[d, 0] = perm[plane]
        sx[d, 1] = pressure[plane]
        sx[d, 2] = agg[plane].astype(f32)
    for d, row in enumerate((CY - 1, 0)):
        sy[d, 0] = perm[:, row, :]
        sy[d, 1] = pressure[:, row, :]
        sy[d, 2] = agg[:, row, :].astype(f32)

    pl.semaphore_wait(barrier, len(everyone))
    slots_sent = [send(sic.at[d], ric.at[d], y_dev[d]) for d in (0, 1)]
    faces_sent = [send(sx.at[d], rx.at[d], x_dev[d]) for d in (0, 1)]
    faces_sent += [send(sy.at[d], ry.at[d], y_dev[d]) for d in (0, 1)]

    for copy in loads[4:]:
        copy.wait()

    def scale_frac(r):
        press = frac_pressure[:, slab(r)]
        TCM[:, slab(r)] = frac_perm[:, slab(r)] * jnp.exp(-0.25 * press)
    loop(SLABS, scale_frac, UF)

    def face_along(r):
        conduct, scaled = frac_perm[:, slab(r)], TCM[:, slab(r)]
        near, near_scaled = pltpu.roll(conduct, 127, 1), pltpu.roll(scaled, 127, 1)
        weight = 2.0 * scaled * near_scaled * inverse(conduct + near)
        weight = jnp.where(lane32 & (FSIDE - 1) < FSIDE - 1, weight, 0.0)
        TAP[:, slab(r)] = weight
        TAM[:, slab(r)] = pltpu.roll(weight, 1, 1)
        after = slab(jnp.minimum(r + 1, SLABS - 1))
        first = lane32 < FSIDE
        near = pltpu.roll(jnp.where(first, frac_perm[:, after], conduct), FSIDE, 1)
        near_scaled = pltpu.roll(jnp.where(first, TCM[:, after], scaled), FSIDE, 1)
        weight = 2.0 * scaled * near_scaled * inverse(conduct + near)
        TCP[:, slab(r)] = jnp.where(first | (r < SLABS - 1), weight, 0.0)
    loop(SLABS, face_along, UF)

    for n, (e, h) in enumerate(ends):
        for m in range(8):
            hot = (sub128 + m * 128 == end_cells(e, h) >> 7).astype(f32).astype(bf16)
            XU[m * 128 : (m + 1) * 128, n * 128 : (n + 1) * 128] = hot
    pressures = pick_ends()
    for h in (0, 1):
        XV[h : h + 1, :] = cross_geom[0:1, h * 128 : (h + 1) * 128] * jnp.exp(
            -0.25 * (pressures[h] + pressures[h + 2]))

    def build_lanes(f):
        BF[f] = (sub128 == (frac_cell[pl.ds(f, 1), :] & 127)).astype(f32).astype(bf16)
    loop(FR, build_lanes, 2)
    coefs = [XV[h : h + 1, :] for h in (0, 1)]
    spread_ends(coefs + coefs)
    spread_slots(CPL)

    def face_back(r):
        before = slab(jnp.maximum(r - 1, 0))
        first = lane32 < FSIDE
        own = TCP[:, slab(r)]
        back = pltpu.roll(jnp.where(first, own, TCP[:, before]), FSIDE, 1)
        back = jnp.where(jnp.logical_not(first) | (r > 0), back, 0.0)
        TCM[:, slab(r)] = back
        diag = frac_storage[:, slab(r)] + TAP[:, slab(r)] + TAM[:, slab(r)] + own + back
        diag = diag + S2[pl.ds(r, FR, stride=SLABS), :]
        FD[:, slab(r)] = diag
        INVF[:, slab(r)] = relaxation * inverse(diag)
    loop(SLABS, face_back, UF)

    def smooth_frac(k, source):
        def body(r):
            z = source[:, slab(r)] * INVF[:, slab(r)]
            ZF[k, :, slab(r)] = z
            F2[pl.ds(r, FR, stride=SLABS), :] = z
        loop(SLABS, body, UF)
        pick_slots(PICK)
        sfl[k] = CPL[...] * PICK[...]
        return [send(sfl.at[k], rfl.at[k, d], y_dev[d]) for d in (0, 1)]

    flux_sent = smooth_frac(0, frac_rhs)

    build_hot(0)
    spread_rock(0, CPL, True)
    for copy in slots_sent:
        copy.wait_recv()
    for d in (0, 1):
        IDX[1 + d] = ric[d, 0].astype(jnp.int32)
        build_hot(1 + d)
        spread_rock(1 + d, ric.at[d, 1], False)
    build_aggregates()
    for copy in faces_sent:
        copy.wait_recv()
    open_x = [gx > 0, gx < n_gx - 1]
    open_y = [gy > 0, gy < n_gy - 1]

    def scale_rock(i):
        conduct = perm[i]
        PA[i + 1] = conduct
        PE[i + 1] = conduct * jnp.exp(-0.25 * pressure[i])
    loop(CX, scale_rock, UR)
    for d, plane in enumerate((0, CX + 1)):
        conduct = jnp.where(open_x[d], rx[d, 0], 0.0)
        PA[plane] = conduct
        PE[plane] = conduct * jnp.exp(-0.25 * rx[d, 1])
    for d in (0, 1):
        conduct = jnp.where(open_y[d], ry[d, 0], 0.0)
        ry[d, 0] = conduct
        ry[d, 1] = conduct * jnp.exp(-0.25 * ry[d, 1])

    def below(x, edge):
        return jnp.where(sub16 == 0, edge, pltpu.roll(x, 1, 0))

    def above(x, edge):
        return jnp.where(sub16 == CY - 1, edge, pltpu.roll(x, CY - 1, 0))

    def face(conduct, scaled, near, near_scaled):
        return 2.0 * scaled * near_scaled * inverse(conduct + near)

    VALS[0] = face(perm[:, 0, :], PE[1 : CX + 1, 0, :], ry[0, 0], ry[0, 1])

    def rock_faces(i):
        conduct, scaled = PA[i + 1], PE[i + 1]
        row = pl.ds(i, 1)
        WX[i] = face(conduct, scaled, PA[i], PE[i])
        side = face(conduct, scaled, above(conduct, ry[1, 0, row, :]),
                    above(scaled, ry[1, 1, row, :]))
        WYP[i] = side
        WYM[i] = below(side, VALS[0, row, :])
        up = face(conduct, scaled, pltpu.roll(conduct, 127, 1), pltpu.roll(scaled, 127, 1))
        up = jnp.where(lane16 < NZ - 1, up, 0.0)
        WZP[i] = up
        WZM[i] = pltpu.roll(up, 1, 1)
    loop(CX, rock_faces, UR)
    WX[CX] = face(PA[CX], PE[CX], PA[CX + 1], PE[CX + 1])

    def rock_diagonal(i):
        faces = [WX[i], WX[i + 1], WYM[i], WYP[i], WZM[i], WZP[i]]
        rows = pl.ds(pl.multiple_of(i * CY, CY), CY)
        diag = storage[i] + sum(faces) + DEL[rows, :]
        RD[i] = diag
        INVR[i] = relaxation * inverse(diag)
        mine = agg[i]
        inside = lambda n: jnp.clip(n, 0, CX - 1)
        nears = [
            jnp.where(i > 0, agg[inside(i - 1)], -1),
            jnp.where(i < CX - 1, agg[inside(i + 1)], -1),
            below(mine, -1), above(mine, -1),
            pltpu.roll(mine, 1, 1), pltpu.roll(mine, 127, 1),
        ]
        for face, near in zip(faces, nears):
            diag = diag - jnp.where(near == mine, face, 0.0)
        S[i] = diag
    loop(CX, rock_diagonal, UR)
    coarse_diag = aggregate_sums(S)
    inverse_coarse = 1.0 / jnp.where(lane16 < NAGG, coarse_diag, 1.0)

    def stencil(i, center, low_x, high_x, low_y, high_y):
        out = RD[i] * center
        out = out - WX[i] * low_x - WX[i + 1] * high_x
        out = out - WYM[i] * below(center, low_y) - WYP[i] * above(center, high_y)
        return out - WZM[i] * pltpu.roll(center, 1, 1) - WZP[i] * pltpu.roll(center, 127, 1)

    def send_faces(k):
        for d, row in enumerate((CY - 1, 0)):
            szy[k, d] = Z0[k, 1 : CX + 1, row, :]
        return [
            send(Z0.at[k, CX], Z0.at[k, 0], x_dev[0]),
            send(Z0.at[k, 1], Z0.at[k, CX + 1], x_dev[1]),
        ] + [send(szy.at[k, d], rzy.at[k, d], y_dev[d]) for d in (0, 1)]

    def iterate(k, rock_vec, frac_vec, halo_sent, flux_sent):
        turn_rock(lambda m: Z0[k, m * 8 + 1 : m * 8 + 9].reshape(128, 128), k == 0)
        pick_rock({1: sans.at[k, 0, 0], 2: sans.at[k, 1, 0]},
                  None if k else {1: sans.at[k, 0, 1], 2: sans.at[k, 1, 1]})
        parts = 1 if k else 2
        answers_sent = [
            send(sans.at[k, 1 - d, 0:parts], rans.at[k, d, 0:parts], y_dev[d]) for d in (0, 1)]
        spread_rock(0, sfl.at[k], True)
        for copy in flux_sent:
            copy.wait_recv()
        for d in (0, 1):
            spread_rock(1 + d, rfl.at[k, d], False)
        for copy in halo_sent:
            copy.wait_recv()

        def residual(i):
            row = pl.ds(i, 1)
            rows = pl.ds(pl.multiple_of(i * CY, CY), CY)
            image = stencil(i, Z0[k, i + 1], Z0[k, i], Z0[k, i + 2],
                            rzy[k, 0, row, :], rzy[k, 1, row, :]) - DEL[rows, :]
            Q[i] = image
            S[i] = rock_vec[i] - image
        loop(CX, residual, UR)
        coarse = aggregate_sums(S) * inverse_coarse
        scs[k] = coarse[0:8]
        coarse_sent = [send(scs.at[k], rcs.at[k, d], x_dev[d]) for d in (0, 1)]
        coarse_sent += [send(scs.at[k], rcs.at[k, 2 + d], y_dev[d]) for d in (0, 1)]

        pick_rock({0: HV}, None if k else {0: AGS})
        values = pick_ends()
        coefs = [XV[h : h + 1, :] for h in (0, 1)]
        spread_ends([coefs[h] * values[2 * (1 - e) + h] for e, h in ends])

        def correct(i):
            E[k, i + 1] = lanes_of(coarse, agg[i])
        loop(CX, correct, UR)
        for plane in (0, CX + 1):
            E[k, plane] = jnp.zeros((CY, NZ), f32)

        def correct_image(i):
            edge = jnp.zeros((1, NZ), f32)
            image = stencil(i, E[k, i + 1], E[k, i], E[k, i + 2], edge, edge)
            Q[i] = Q[i] + image - relaxation * rock_vec[i]
        loop(CX, correct_image, UR)

        def frac_faces(r):
            here = slab(r)
            z = ZF[k, :, here]
            before = ZF[k, :, slab(jnp.maximum(r - 1, 0))]
            after = ZF[k, :, slab(jnp.minimum(r + 1, SLABS - 1))]
            first = lane32 < FSIDE
            down = pltpu.roll(jnp.where(first, after, z), FSIDE, 1)
            up = pltpu.roll(jnp.where(first, z, before), FSIDE, 1)
            image = FD[:, here] * z
            image = image - TAP[:, here] * pltpu.roll(z, 127, 1) - TAM[:, here] * pltpu.roll(z, 1, 1)
            image = image - TCP[:, here] * down - TCM[:, here] * up
            FI[:, here] = image - relaxation * frac_vec[:, here]
        loop(SLABS, frac_faces, UF)
        for copy in answers_sent + coarse_sent:
            copy.wait_recv()
        if k == 0:
            AGS[...] = AGS[...] + rans[0, 0, 1] + rans[0, 1, 1]
        tables = [jnp.concatenate([rcs[k, d], rcs[k, d]], axis=0) for d in range(4)]
        for d, plane in enumerate((0, CX - 1)):
            near = lanes_of(tables[d], rx[d, 2].astype(jnp.int32))
            Q[plane] = Q[plane] - WX[plane + d] * near
        for d in (0, 1):
            table = jnp.concatenate([tables[2 + d]] * 2, axis=0)
            VALS[d] = lanes_of(table, ry[d, 2].astype(jnp.int32))
        slot_agg = AGS[...].astype(jnp.int32)
        four = [jnp.concatenate([t] * 2, axis=0) for t in (coarse, tables[2], tables[3])]
        own, low, high = [lanes_of(t, slot_agg) for t in four]
        where = OFF[...]
        host = HV[...] + rans[k, 0, 0] + rans[k, 1, 0]
        host = host + jnp.where(where == 0, own, jnp.where(where < 0, low, high))
        VALS[2] = CPL[...] * host

        zero = jnp.zeros((8, 128), f32)

        def products(x, v, b):
            if k == 0:
                return fold(v * v), fold(x * v), fold(x * x)
            return fold(x * b), fold(x * v), fold(x * x)

        spread_slots(VALS.at[2])

        def frac_image(r, accs):
            here = slab(r)
            vec = frac_vec[:, here]
            image = FI[:, here] - S2[pl.ds(r, FR, stride=SLABS), :]
            if k == 0:
                W1F[:, here] = image
            return tuple(a + p for a, p in zip(accs, products(image, vec, frac_rhs[:, here])))
        accs = lax.fori_loop(0, SLABS, frac_image, (zero,) * 3, unroll=UF)
        flux_next = smooth_frac(1, W1F) if k == 0 else None

        def rock_image(i, accs):
            row = pl.ds(i, 1)
            vec = rock_vec[i]
            image = Q[i] - jnp.where(sub16 == 0, WYM[i] * VALS[0, row, :], 0.0)
            image = image - jnp.where(sub16 == CY - 1, WYP[i] * VALS[1, row, :], 0.0)
            if k == 0:
                W1R[i] = image
                Z0[1, i + 1] = image * INVR[i]
            return tuple(a + p for a, p in zip(accs, products(image, vec, rock_rhs[i])))
        accs = lax.fori_loop(0, CX, rock_image, accs, unroll=UR)
        halo_next = send_faces(1) if k == 0 else None
        return list(accs), halo_next, flux_next

    def smooth_rock(i):
        Z0[0, i + 1] = rock_rhs[i] * INVR[i]
    loop(CX, smooth_rock, UR)
    dots, halo_sent, flux_sent = iterate(0, rock_rhs, frac_rhs, send_faces(0), flux_sent)
    dots += iterate(1, W1R, W1F, halo_sent, flux_sent)[0]

    tile = jnp.zeros((8, 128), f32)
    for n, part in enumerate(dots):
        tile = jnp.where(sub8 == n, jnp.sum(part, axis=0, keepdims=True), tile)
    groups = [(AR0, my_xy, xy_peers, n_xy), (AR2, my_z, z_peers, n_z)]
    for slots, me, peers, size in groups:
        slots[pl.ds(me, 1)] = tile[None]
        earlier = len(started)
        copies = [send(slots.at[me], slots.at[me], device) for device in peers]
        if slots is AR0:
            def join(i):
                for k in (0, 1):
                    E[k, i + 1] = E[k, i + 1] + Z0[k, i + 1]
            loop(CX, join, UR)
        if slots is AR2:
            for copy in started[:earlier]:
                copy.wait_send()
        for copy in copies:
            copy.wait_recv()
        tile = sum(slots[n] for n in range(size))
    tile = jnp.sum(tile, axis=1, keepdims=True)
    bb, pb, pp, qb, qp, qq = [tile[n : n + 1, :] for n in range(6)]
    gram = [[bb, pb, qb], [pb, pp, qp], [qb, qp, qq]]
    shift = relaxation

    def inner(a, c):
        return sum(a[m] * c[n] * gram[m][n] for m in range(3) for n in range(3))

    one, none = jnp.ones((1, 1), f32), jnp.zeros((1, 1), f32)
    start_norm = jnp.sqrt(bb + epsilon)
    v0 = [one / start_norm, none, none]
    image = [shift * v0[0], v0[0], none]
    rest0 = inner(image, image)
    h00 = inner(image, v0)
    image = [a - h00 * c for a, c in zip(image, v0)]
    h10 = jnp.sqrt(jnp.maximum(inner(image, image), 0.0) + epsilon)
    v1 = [a / h10 for a in image]
    image = [shift * v1[0], v1[0] + shift * v1[1], v1[1]]
    h01, h11 = inner(image, v0), inner(image, v1)
    image = [a - h01 * c - h11 * d for a, c, d in zip(image, v0, v1)]
    h21 = jnp.sqrt(jnp.maximum(inner(image, image), 0.0) + epsilon)

    radius = jnp.sqrt(h00 * h00 + h10 * h10)
    cosine, sine = h00 / radius, h10 / radius
    upper01 = cosine * h01 + sine * h11
    lower = cosine * h11 - sine * h01
    right0, right1 = cosine * start_norm, -sine * start_norm
    radius1 = jnp.sqrt(lower * lower + h21 * h21)
    cosine1, sine1 = lower / radius1, h21 / radius1
    res_out[...] = jnp.abs(-sine1 * right1)
    y1 = cosine1 * right1 / radius1
    y0 = (right0 - upper01 * y1) / radius
    on_b = y0 * v0[0] + y1 * v1[0]
    on_p = y1 * v1[1]

    def rock_update(i):
        rock_out[i] = on_b * E[0, i + 1] + on_p * E[1, i + 1]
    loop(CX, rock_update, UR)

    def frac_update(r):
        frac_out[:, slab(r)] = on_b * ZF[0, :, slab(r)] + on_p * ZF[1, :, slab(r)]
    loop(SLABS, frac_update, UF)
    for copy in started[earlier:]:
        copy.wait_send()


def local(sizes, rock_rhs, frac_rhs, perm, storage, pressure, frac_perm, frac_storage,
          frac_pressure, couple_geom, couple_count, couple_frac_cell, couple_rock_cell,
          host_offset, cross_pairs, cross_geom, aggregates):
    n_gx, n_y, n_z = sizes
    vmem = pl.BlockSpec(memory_space=pltpu.VMEM)
    smem = pl.BlockSpec(memory_space=pltpu.SMEM)
    in_specs = [pl.BlockSpec(memory_space=pl.ANY)] * 8 + [vmem] * 7
    in_specs.append(pl.BlockSpec(memory_space=pl.ANY))
    in_specs[9] = in_specs[12] = smem
    block = (CX, CY, NZ)
    tall = (CX + 2, CY, NZ)
    frac = (FR, FCELLS)
    slot = (FR, KC)

    def mem(*shape, kind=f32):
        return pltpu.VMEM(shape, kind)

    scratch = [
        mem(2, *tall), mem(2, *tall), mem(*tall), mem(*tall), mem(CX + 1, CY, NZ),
        *[mem(*block) for _ in range(9)], mem(ROWS, 128),
        *[mem(*frac) for _ in range(7)], mem(2, *frac), mem(FR * SLABS, 128), mem(FR * SLABS, 128),
        mem(3, ROWS, FR * KC, kind=bf16),
        mem(3, 256, FR * KC, kind=bf16), mem(384, ROWS, kind=bf16), mem(256, FR * SLABS, kind=bf16),
        mem(FR, 128, 128, kind=bf16), mem(FR * SLABS, 2 * CROSS, kind=bf16),
        mem(256, 2 * CROSS, kind=bf16), mem(128, 4096, kind=bf16), mem(256, 4096, kind=bf16),
        mem(256, 128, kind=bf16), mem(*frac), mem(8, 128),
        mem(3, *slot, kind=jnp.int32), mem(*slot, kind=jnp.int32),
        mem(*slot), mem(*slot), mem(*slot), mem(*slot), mem(3, *slot),
        mem(2, 3, CY, NZ), mem(2, 3, CY, NZ), mem(2, 3, CX, NZ), mem(2, 3, CX, NZ),
        mem(2, 2, *slot), mem(2, 2, *slot),
        mem(2, 2, CX, NZ), mem(2, 2, CX, NZ), mem(2, *slot), mem(2, 2, *slot),
        mem(2, 2, 2, *slot), mem(2, 2, 2, *slot), mem(2, 8, 128), mem(2, 4, 8, 128),
        mem(n_gx * n_y, 8, 128), mem(n_z, 8, 128),
        mem(*block), mem(*frac), mem(*block), mem(*block), mem(*block), mem(*frac), mem(*frac),
        mem(*frac), mem(*block, kind=jnp.int32),
        pltpu.SemaphoreType.DMA((80,)), pltpu.SemaphoreType.DMA((80,)),
        pltpu.SemaphoreType.DMA((9,)),
    ]
    rock, fracs, norm = pl.pallas_call(
        functools.partial(kernel, sizes),
        out_shape=(
            jax.ShapeDtypeStruct(block, f32),
            jax.ShapeDtypeStruct(frac, f32),
            jax.ShapeDtypeStruct((1, 1), f32),
        ),
        in_specs=in_specs,
        out_specs=(vmem, vmem, vmem),
        scratch_shapes=scratch,
        compiler_params=pltpu.CompilerParams(
            collective_id=0, has_side_effects=True, vmem_limit_bytes=60 * 1024 * 1024),
    )(rock_rhs, frac_rhs, perm, storage, pressure, frac_perm, frac_storage, frac_pressure,
      couple_geom, couple_count, couple_frac_cell, couple_rock_cell, host_offset, cross_pairs,
      cross_geom.reshape(1, CROSS), aggregates)
    return rock, fracs, norm[0, 0]


def solution(mesh):
    n_gx, n_gy = mesh.shape["gx"], mesh.shape["gy"]
    n_z = 8 if n_gy % 8 == 0 else 2
    grid = P("gx", "gy", None)
    owned = P(("gx", "gy"), None)
    flat = P(("gx", "gy"))
    in_specs = (grid, owned, grid, grid, grid, owned, owned, owned, owned, flat, owned, owned,
                flat, P(None, ("gx", "gy")), flat, grid)
    return jax.shard_map(
        functools.partial(local, (n_gx, n_gy // n_z, n_z)), mesh=mesh, in_specs=in_specs,
        out_specs=(grid, owned, P()), check_vma=False)
```
